128 devices in a mesh: box: 8 (over y, x_hi), dir: 16 (over z, x_lo, core).
Axes of the slice: x: 4 (x_hi: 2, x_lo: 2; x = x_hi * 2 + x_lo), y: 4, z: 4, core: 2. Of those that a mesh axis runs over, the one named last changes fastest.
Arguments:
- currents: bfloat16 [8192, 512], P(('box', 'dir')), may hold values from -6 to 6
- near_list: int32 [8192, 27], P(('box', 'dir')), may hold values from 0 to 8191, as said below
- far_list: int32 [1024, 20], replicated, may hold values from 0 to 1023, as said below
- far_kind: int32 [1024, 20], replicated, may hold values from 0 to 315
- aggregate: bfloat16 [512, 1024], replicated, may hold values from -0.25 to 0.25
- interp: bfloat16 [1024, 4096], replicated, may hold values from -0.1875 to 0.1875
- receive: bfloat16 [1024, 512], replicated, may hold values from -0.1875 to 0.1875
- shift_angle: float32 [8, 2048], replicated, may hold values from -3.140625 to 3.140625
- translation: float32 [316, 2, 2048], P(None, None, 'dir'), may hold values from -0.6 to 0.6
- near_matrix: bfloat16 [27, 512, 512], replicated, may hold values from -0.0546875 to 0.0546875
Outputs:
- fields: float32 [8192, 512], P(('box', 'dir'))
The draws below stay inside these ranges and needn't reach their ends.
Inputs may be any that keep to these rules, and one draw needn't show every extreme that they name: `near_list`: entry [l, n] lies within 32 of l. `far_list`: entry [p, j] differs from p by 2 to 64.
All inputs are finite; a program needn't handle non-finite values.
Results may differ from the reference program's by a relative error of at most 0.013.
Values may be sent and summed in bfloat16 or wider, within the bound.
No kernel may reach another device: no remote copies, remote signals or barrier semaphores. Data moves between devices by JAX's collectives and lax.ppermute only.
A program may use at most 128 MiB of HBM per device.

```python
import jax
import jax.numpy as jnp
from jax import lax

CUR = 256
Q0 = 512
Q1 = 2048
KINDS = 316
FAR = 20
NEAR = 27
LEAVES = 8192
PARENTS = 1024
REACH = 32
FAR_REACH = 64


def draw_near_list(key, part):
    leaf_index = jnp.arange(LEAVES, dtype=jnp.int32)[:, None]
    offset = jax.random.randint(jax.random.fold_in(key, 7), (LEAVES, NEAR), -REACH, REACH + 1, dtype=jnp.int32)
    return jnp.clip(leaf_index + offset, 0, LEAVES - 1).astype(jnp.int32)


def far_pairs(key):
    base = jax.random.fold_in(key, 31)
    magnitude = jax.random.randint(jax.random.fold_in(base, 1), (PARENTS, FAR), 2, FAR_REACH + 1, dtype=jnp.int32)
    sign_draw = jax.random.randint(jax.random.fold_in(base, 2), (PARENTS, FAR), 0, 2, dtype=jnp.int32)
    offset = magnitude * (2 * sign_draw - 1)
    parent_index = jnp.arange(PARENTS, dtype=jnp.int32)[:, None]
    target = parent_index + offset
    offset = jnp.where((target < 0) | (target >= PARENTS), -offset, offset)
    return (parent_index + offset).astype(jnp.int32)


def draw_far_list(key, part):
    targets = far_pairs(key)
    return targets


def draw_far_kind(key, part):
    kinds = jax.random.randint(jax.random.fold_in(key, 53), (PARENTS, FAR), 0, KINDS, dtype=jnp.int32)
    kinds = kinds.at[0, 0].set(KINDS - 1)
    kinds = kinds.at[0, 1].set(0)
    return kinds.astype(jnp.int32)


def levels(rng, dims, cuts, low, top_value):
    def one(dim, blocks):
        draws = jax.random.uniform(jax.random.fold_in(jax.random.fold_in(rng, 6), dim), (blocks,), jnp.float32, low / len(cuts), top_value / len(cuts))
        return jnp.repeat(jnp.exp(draws), dims[dim] // blocks).reshape((-1,) + (1,) * (len(dims) - dim - 1))

    loudness = one(*cuts[0])
    for cut in cuts[1:]:
        loudness = loudness * one(*cut)
    return loudness


def noise(rng, extent, width, limit, cuts=(), kind=jnp.bfloat16):
    values = jax.random.normal(rng, extent, jnp.float32) * width
    if len(cuts) > 0:
        values = levels(rng, extent, cuts, -0.22, 0.18) * values
    return jnp.clip(values, min=-limit, max=limit).astype(kind)


def setup_inputs(seed: int = 0) -> dict:
    arg_keys = jax.random.split(jax.random.key(seed), 11)
    currents = noise(arg_keys[0], (LEAVES, 2 * CUR), 1.0, 6.0, ((0, 128),))
    near_list = draw_near_list(jax.random.fold_in(arg_keys[10], 71), 0)
    far_list = draw_far_list(jax.random.fold_in(arg_keys[10], 71), 0)
    far_kind = draw_far_kind(jax.random.fold_in(arg_keys[10], 71), 0)
    aggregate = noise(arg_keys[4], (2 * CUR, 2 * Q0), (2 * CUR) ** -0.5, 0.25)
    interp = noise(arg_keys[5], (2 * Q0, 2 * Q1), (2 * Q0) ** -0.5, 0.1875)
    receive = noise(arg_keys[6], (2 * Q0, 2 * CUR), (2 * Q0) ** -0.5, 0.1875)
    shift_angle = jnp.clip(jax.random.uniform(arg_keys[7], (8, Q1), jnp.float32, -3.140625, 3.140625), -3.140625, 3.140625)
    translation = noise(arg_keys[8], (KINDS, 2, Q1), 0.1, 0.6, ((2, 16),), jnp.float32)
    near_matrix = noise(arg_keys[9], (NEAR, 2 * CUR, 2 * CUR), (2 * CUR * NEAR) ** -0.5, 0.0546875)
    return {"currents": currents, "near_list": near_list, "far_list": far_list, "far_kind": far_kind, "aggregate": aggregate, "interp": interp, "receive": receive, "shift_angle": shift_angle, "translation": translation, "near_matrix": near_matrix}


def reference(currents, near_list, far_list, far_kind, aggregate, interp, receive, shift_angle, translation, near_matrix):
    leaves = currents.shape[0]
    parents = leaves // 8
    pattern = jnp.dot(currents, aggregate, preferred_element_type=jnp.float32).astype(jnp.bfloat16)
    children = jnp.dot(pattern, interp, preferred_element_type=jnp.float32).reshape(parents, 8, 2, Q1)
    cosine = jnp.cos(shift_angle)
    sine_part = jnp.sin(shift_angle)
    real_part = jnp.sum(children[:, :, 0] * cosine - children[:, :, 1] * sine_part, axis=1)
    imag_part = jnp.sum(children[:, :, 0] * sine_part + children[:, :, 1] * cosine, axis=1)
    local_real = jnp.zeros((parents, Q1), jnp.float32)
    local_imag = jnp.zeros((parents, Q1), jnp.float32)
    for slot in range(FAR):
        source_real = real_part[far_list[:, slot]]
        source_imag = imag_part[far_list[:, slot]]
        operator = translation[far_kind[:, slot]]
        local_real = local_real + operator[:, 0] * source_real - operator[:, 1] * source_imag
        local_imag = local_imag + operator[:, 0] * source_imag + operator[:, 1] * source_real
    rot_real = local_real[:, None] * cosine + local_imag[:, None] * sine_part
    rot_imag = local_imag[:, None] * cosine - local_real[:, None] * sine_part
    received = jnp.stack([rot_real, rot_imag], axis=2).reshape(leaves, 2 * Q1).astype(jnp.bfloat16)
    back_pattern = lax.dot_general(received, interp, (((1,), (1,)), ((), ())), preferred_element_type=jnp.float32).astype(jnp.bfloat16)
    fields = jnp.dot(back_pattern, receive, preferred_element_type=jnp.float32)
    for slot in range(NEAR):
        fields = fields + jnp.dot(currents[near_list[:, slot]], near_matrix[slot], preferred_element_type=jnp.float32)
    return fields
```

```python
import functools

import jax
import jax.numpy as jnp
from jax import lax
from jax.experimental import pallas as pl
from jax.experimental.pallas import tpu as pltpu
from jax.sharding import PartitionSpec as P

BF16, F32, I32 = jnp.bfloat16, jnp.float32, jnp.int32
BOTH = ("box", "dir")
VMEM = pltpu.VMEM


def whole(space=VMEM):
    return pl.BlockSpec(memory_space=space)


def call(body, out, args, specs, scratch, mib, flops, moved):
    return pl.pallas_call(
        body,
        out_shape=out,
        in_specs=specs,
        out_specs=jax.tree.map(lambda _: whole(), out),
        scratch_shapes=scratch,
        compiler_params=pltpu.CompilerParams(vmem_limit_bytes=mib << 20),
        cost_estimate=pl.CostEstimate(flops=flops, bytes_accessed=moved, transcendentals=0),
    )(*args)


def dot(a, b, ca=1, cb=0):
    return lax.dot_general(a, b, (((ca,), (cb,)), ((), ())), preferred_element_type=F32)


def up_kernel(cur_ref, agg_ref, cos_ref, sin_ref, interp, out_ref, buf, sems):
    chunks, width = buf.shape[0] // 2, buf.shape[2]
    copies = []
    for j in range(2 * chunks):
        copies.append(
            pltpu.make_async_copy(interp.at[:, pl.ds(j * width, width)], buf.at[j], sems.at[j])
        )
    for j in range(chunks):
        copies[j].start()
        copies[chunks + j].start()
    rows = cur_ref.shape[0]
    parents = rows // 8
    r = lax.broadcasted_iota(I32, (rows, rows), 0)
    c = lax.broadcasted_iota(I32, (rows, rows), 1)
    pick = jnp.where(c == 8 * (r % parents) + r // parents, 1.0, 0.0).astype(BF16)
    cur = dot(pick, cur_ref[...]).astype(BF16)
    pattern = dot(cur, agg_ref[...]).astype(BF16)
    for j in range(chunks):
        copies[j].wait()
        copies[chunks + j].wait()
        re = dot(pattern, buf[j])
        im = dot(pattern, buf[chunks + j])
        acc_re = jnp.zeros((parents, width), F32)
        acc_im = jnp.zeros((parents, width), F32)
        for k in range(8):
            cosine = cos_ref[pl.ds(k, 1), pl.ds(j * width, width)]
            sine = sin_ref[pl.ds(k, 1), pl.ds(j * width, width)]
            a, b = re[k * parents : (k + 1) * parents], im[k * parents : (k + 1) * parents]
            acc_re += a * cosine - b * sine
            acc_im += a * sine + b * cosine
        for h in range(width // 128):
            s = slice(h * 128, (h + 1) * 128)
            out_ref[j * (width // 128) + h, 0:parents, :] = acc_re[:, s].astype(BF16)
            out_ref[j * (width // 128) + h, parents : 2 * parents, :] = acc_im[:, s].astype(BF16)


def operators_kernel(kind_ref, table_ref, out_ref):
    rows, slots = kind_ref.shape
    lane = lax.broadcasted_iota(I32, (rows, table_ref.shape[0]), 1)
    for j in range(slots):
        hot = jnp.where(lane == kind_ref[:, j : j + 1], 1.0, 0.0).astype(BF16)
        out_ref[j] = dot(hot, table_ref[...]).astype(BF16)


def translate_kernel(upper_ref, index_ref, operator_ref, out_ref):
    sources = upper_ref.shape[0] * 16
    rows, slots = index_ref.shape
    field = jnp.concatenate(
        [
            upper_ref[:, 0:16, :].reshape(sources, 128),
            upper_ref[:, 16:32, :].reshape(sources, 128),
        ],
        axis=1,
    )
    lane = lax.broadcasted_iota(I32, (rows, sources), 1)
    acc_re = jnp.zeros((rows, 128), F32)
    acc_im = jnp.zeros((rows, 128), F32)
    for j in range(slots):
        hot = jnp.where(lane == index_ref[:, j : j + 1], 1.0, 0.0).astype(BF16)
        x = dot(hot, field)
        op = operator_ref[j].astype(F32)
        xr, xi = x[:, :128], x[:, 128:]
        tr, ti = op[:, :128], op[:, 128:]
        acc_re += tr * xr - ti * xi
        acc_im += tr * xi + ti * xr
    blocks = out_ref.shape[0]
    out_ref[:, 0:8, :] = acc_re.reshape(blocks, 8, 128).astype(BF16)
    out_ref[:, 8:16, :] = acc_im.reshape(blocks, 8, 128).astype(BF16)


def down_kernel(inc_ref, cos_ref, sin_ref, receive_ref, near_ref, interp, out_ref, buf, received, sems):
    chunks, width = buf.shape[0], buf.shape[1]
    copies = []
    for j in range(chunks):
        copies.append(
            pltpu.make_async_copy(interp.at[pl.ds(j * width, width)], buf.at[j], sems.at[j])
        )
        copies[j].start()
    leaves = received.shape[0]
    half = received.shape[1] // 2
    for s in range(inc_ref.shape[0]):
        lanes = slice(s * 128, (s + 1) * 128)
        block = inc_ref[s].astype(F32)
        re, im = block[0:8][:, None, :], block[8:16][:, None, :]
        cosine, sine = cos_ref[:, lanes][None], sin_ref[:, lanes][None]
        received[:, s * 128 : (s + 1) * 128] = (
            (re * cosine + im * sine).reshape(leaves, 128).astype(BF16)
        )
        received[:, half + s * 128 : half + (s + 1) * 128] = (
            (im * cosine - re * sine).reshape(leaves, 128).astype(BF16)
        )
    total = near_ref[...]
    for j in range(chunks):
        copies[j].wait()
        back = dot(received[...], buf[j], 1, 1).astype(BF16)
        total += dot(back, receive_ref[pl.ds(j * width, width), :])
    out_ref[...] = total


def near_kernel(cur_ref, col_ref, near_hbm, out_ref, buf, sems):
    slots = col_ref.shape[1]
    copies = []
    for n in range(slots):
        copies.append(pltpu.make_async_copy(near_hbm.at[n], buf.at[n], sems.at[n]))
        copies[n].start()
    rows = col_ref.shape[0]
    lane = lax.broadcasted_iota(I32, (rows, cur_ref.shape[0]), 1)
    total = jnp.zeros(out_ref.shape, F32)
    for n in range(slots):
        hot = jnp.where(lane == col_ref[:, n : n + 1], 1.0, 0.0).astype(BF16)
        picked = dot(hot, cur_ref[...]).astype(BF16)
        copies[n].wait()
        total += dot(picked, buf[n])
    out_ref[...] = total


def halo_partner(i, boxes, dirs):
    b, d = divmod(i, dirs)
    quarter = dirs // 4
    z, r = divmod(d, quarter)
    other = b + 1 if z >= 2 else b - 1
    if other < 0 or other >= boxes:
        return i ^ 1
    return other * dirs + (3 - z) * quarter + r


def on_device(
    boxes,
    dirs,
    currents,
    near_list,
    far_list,
    far_kind,
    aggregate,
    interp,
    receive,
    shift_angle,
    translation,
    near_matrix,
):
    leaves, width = currents.shape
    n = boxes * dirs
    me = lax.axis_index(BOTH)
    box = lax.axis_index("box")
    odd = me % 2
    parents = leaves // 8 * dirs
    directions = shift_angle.shape[1]

    far_half = lax.ppermute(currents, BOTH, [(i, halo_partner(i, boxes, dirs)) for i in range(n)])
    outward = lax.dynamic_slice_in_dim(currents, odd * (leaves // 2), leaves // 2, 0)
    inward = lax.dynamic_slice_in_dim(currents, (1 - odd) * (leaves // 2), leaves // 2, 0)
    cross = [(i, min(max(i + (1 if i % 2 else -1), 0), n - 1)) for i in range(n)]
    from_cross = lax.ppermute(outward, BOTH, cross)
    from_sibling = lax.ppermute(inward, BOTH, [(i, i ^ 1) for i in range(n)])

    cosine, sine = jnp.cos(shift_angle), jnp.sin(shift_angle)

    slots = far_list.shape[1]
    my_far = lax.dynamic_slice_in_dim(far_list, box * parents, parents, 0)
    my_kind = lax.dynamic_slice_in_dim(far_kind, box * parents, parents, 0)
    kinds = translation.shape[0]
    table = jnp.concatenate([translation[:, 0], translation[:, 1]], axis=1).astype(BF16)
    table = jnp.pad(table, ((0, -kinds % 128), (0, 0)))
    operators = call(
        operators_kernel,
        jax.ShapeDtypeStruct((slots, parents, 256), BF16),
        (my_kind, table),
        [whole()] * 2,
        [],
        16,
        2 * slots * parents * 384 * 256,
        4 << 20,
    )
    e = my_far - box * parents + parents // 2
    q = e - parents // 2
    own = (q // 8) * 16 + q % 8
    g = jnp.where(q < 0, e, q - parents)
    low = ((1 - g // 32) * 4 + (g // 8) % 4) * 16 + 8 + g % 8
    high = ((3 - g // 32) * 4 + (g // 8) % 4) * 16 + 8 + g % 8
    index = jnp.where(q < 0, low, jnp.where(q < parents, own, high))

    rows = jnp.concatenate([currents, far_half], axis=0)
    up = call(
        up_kernel,
        jax.ShapeDtypeStruct((dirs, 4 * leaves // 8, 128), BF16),
        (rows, aggregate, cosine, sine, interp),
        [whole()] * 4 + [whole(pl.ANY)],
        [pltpu.VMEM((16, interp.shape[0], 256), BF16), pltpu.SemaphoreType.DMA((16,))],
        20,
        2 * 128 * 1024 * 4608,
        10 << 20,
    )
    upper = lax.all_to_all(up, "dir", split_axis=0, concat_axis=0, tiled=True)

    near_rows = jnp.concatenate([currents, from_sibling, from_cross], axis=0)
    rel = near_list - me * leaves
    reach = leaves // 2
    outside = jnp.where((rel < 0) == (odd == 0), leaves + reach, leaves) + rel % reach
    column = jnp.where((rel >= 0) & (rel < leaves), rel, outside)
    near = call(
        near_kernel,
        jax.ShapeDtypeStruct((leaves, width), F32),
        (near_rows, column, near_matrix),
        [whole()] * 2 + [whole(pl.ANY)],
        [pltpu.VMEM(near_matrix.shape, BF16), pltpu.SemaphoreType.DMA((near_matrix.shape[0],))],
        24,
        2 * leaves * 27 * 512 * 640,
        15 << 20,
    )

    local = call(
        translate_kernel,
        jax.ShapeDtypeStruct((dirs, 2 * leaves // 8, 128), BF16),
        (upper, index, operators),
        [whole()] * 3,
        [],
        16,
        2 * slots * parents * 256 * 256,
        2 << 20,
    )
    incoming = lax.all_to_all(local, "dir", split_axis=0, concat_axis=0, tiled=True)

    return call(
        down_kernel,
        jax.ShapeDtypeStruct((leaves, width), F32),
        (incoming, cosine, sine, receive, near, interp),
        [whole()] * 5 + [whole(pl.ANY)],
        [
            pltpu.VMEM((4, interp.shape[0] // 4, interp.shape[1]), BF16),
            pltpu.VMEM((leaves, 2 * directions), BF16),
            pltpu.SemaphoreType.DMA((4,)),
        ],
        20,
        2 * 64 * 4096 * 1536,
        10 << 20,
    )


def solution(mesh):
    placed = (
        P(BOTH, None),
        P(BOTH, None),
        P(),
        P(),
        P(),
        P(),
        P(),
        P(),
        P(None, None, "dir"),
        P(),
    )
    body = functools.partial(on_device, mesh.shape["box"], mesh.shape["dir"])
    return jax.shard_map(
        body, mesh=mesh, in_specs=placed, out_specs=P(BOTH, None), check_vma=False
    )
```

```python
import functools

import jax
import jax.numpy as jnp
from jax import lax
from jax.experimental import pallas as pl
from jax.experimental.pallas import tpu as pltpu
from jax.sharding import PartitionSpec as P

BF16, F32, I32 = jnp.bfloat16, jnp.float32, jnp.int32
BOTH = ("box", "dir")
VMEM = pltpu.VMEM


def whole(space=VMEM):
    return pl.BlockSpec(memory_space=space)


def call(body, out, args, specs, scratch, mib, flops, moved):
    return pl.pallas_call(
        body,
        out_shape=out,
        in_specs=specs,
        out_specs=jax.tree.map(lambda _: whole(), out),
        scratch_shapes=scratch,
        compiler_params=pltpu.CompilerParams(vmem_limit_bytes=mib << 20),
        cost_estimate=pl.CostEstimate(flops=flops, bytes_accessed=moved, transcendentals=0),
    )(*args)


def dot(a, b, ca=1, cb=0):
    return lax.dot_general(a, b, (((ca,), (cb,)), ((), ())), preferred_element_type=F32)


def prepare_kernel(
    box_ref,
    far_hbm,
    kind_hbm,
    angle_ref,
    table_ref,
    near_list_ref,
    aggregate,
    interp,
    receive,
    operators,
    index_ref,
    column_ref,
    cosine_ref,
    sine_ref,
    aggregate_out,
    interp_out,
    receive_out,
    far_ref,
    kind_ref,
    table,
    sems,
):
    slots, parents = far_ref.shape
    box, me = box_ref[0], box_ref[1]
    mine = pl.ds(pl.multiple_of(box * parents, parents), parents)
    lists = [
        pltpu.make_async_copy(far_hbm.at[:, mine], far_ref, sems.at[0]),
        pltpu.make_async_copy(kind_hbm.at[:, mine], kind_ref, sems.at[1]),
    ]
    weights = [
        pltpu.make_async_copy(aggregate, aggregate_out, sems.at[2]),
        pltpu.make_async_copy(interp, interp_out, sems.at[3]),
        pltpu.make_async_copy(receive, receive_out, sems.at[4]),
    ]
    for copy in lists + weights:
        copy.start()
    cosine_ref[...] = jnp.cos(angle_ref[...])
    sine_ref[...] = jnp.sin(angle_ref[...])
    kinds = table_ref.shape[0] // 2
    table[...] = jnp.zeros_like(table)
    table[0:kinds, 0:128] = table_ref[pl.ds(0, kinds, stride=2), :].astype(BF16)
    table[0:kinds, 128:256] = table_ref[pl.ds(1, kinds, stride=2), :].astype(BF16)

    leaves = near_list_ref.shape[1]
    rel = near_list_ref[...] - me * leaves
    odd = me & 1
    below = jnp.where(odd == 0, 3 * leaves, leaves * 2)
    above = jnp.where(odd == 0, 0, leaves)
    column = jnp.where(rel < 0, rel + below, jnp.where(rel < leaves, rel, rel + above))
    column_ref[...] = jnp.pad(column, ((0, 32 - column.shape[0]), (0, 0))).T

    lists[0].wait()
    lists[1].wait()
    q = far_ref[...] - box * parents
    half = parents // 2
    g = jnp.where(q < 0, q + half, q - parents)
    own = ((q >> 3) << 4) + (q & 7)
    row = (((g >> 3) & 3) << 4) + 8 + (g & 7)
    low, high = row + ((1 - (g >> 5)) << 6), row + ((3 - (g >> 5)) << 6)
    index = jnp.where(q < 0, low, jnp.where(q < parents, own, high))
    index_ref[...] = jnp.pad(index, ((0, 32 - slots), (0, 0))).T
    kind = jnp.pad(kind_ref[...], ((0, 32 - slots), (0, 0))).T
    lane = lax.broadcasted_iota(I32, (parents, table.shape[0]), 1)
    for j in range(slots):
        hot = jnp.where(lane == kind[:, j : j + 1], 1.0, 0.0).astype(BF16)
        operators[j] = dot(hot, table[...]).astype(BF16)
    for copy in weights:
        copy.wait()


def up_kernel(own_ref, far_ref, agg_ref, cos_ref, sin_ref, interp, out_ref):
    width = 256
    directions = cos_ref.shape[1]
    leaves = own_ref.shape[0]
    rows = 2 * leaves
    parents = rows // 8
    r = lax.broadcasted_iota(I32, (rows, leaves), 0)
    c = lax.broadcasted_iota(I32, (rows, leaves), 1)
    leaf = 8 * (r % parents) + r // parents
    from_own = jnp.where(c == leaf, 1.0, 0.0).astype(BF16)
    from_far = jnp.where(c + leaves == leaf, 1.0, 0.0).astype(BF16)
    cur = (dot(from_own, own_ref[...]) + dot(from_far, far_ref[...])).astype(BF16)
    pattern = dot(cur, agg_ref[...]).astype(BF16)
    for j in range(directions // width):
        re = dot(pattern, interp[:, j * width : (j + 1) * width])
        im = dot(pattern, interp[:, directions + j * width : directions + (j + 1) * width])
        acc_re = jnp.zeros((parents, width), F32)
        acc_im = jnp.zeros((parents, width), F32)
        for k in range(8):
            cosine = cos_ref[pl.ds(k, 1), pl.ds(j * width, width)]
            sine = sin_ref[pl.ds(k, 1), pl.ds(j * width, width)]
            a, b = re[k * parents : (k + 1) * parents], im[k * parents : (k + 1) * parents]
            acc_re += a * cosine - b * sine
            acc_im += a * sine + b * cosine
        for h in range(width // 128):
            s = slice(h * 128, (h + 1) * 128)
            out_ref[j * (width // 128) + h, 0:parents, :] = acc_re[:, s].astype(BF16)
            out_ref[j * (width // 128) + h, parents : 2 * parents, :] = acc_im[:, s].astype(BF16)


def translate_kernel(upper_ref, index_ref, operator_ref, _, out_ref):
    sources = upper_ref.shape[0] * 16
    slots, rows = operator_ref.shape[:2]
    field = jnp.concatenate(
        [
            upper_ref[:, 0:16, :].reshape(sources, 128),
            upper_ref[:, 16:32, :].reshape(sources, 128),
        ],
        axis=1,
    )
    lane = lax.broadcasted_iota(I32, (rows, sources), 1)
    acc_re = jnp.zeros((rows, 128), F32)
    acc_im = jnp.zeros((rows, 128), F32)
    for j in range(slots):
        hot = jnp.where(lane == index_ref[:, j : j + 1], 1.0, 0.0).astype(BF16)
        x = dot(hot, field)
        op = operator_ref[j].astype(F32)
        xr, xi = x[:, :128], x[:, 128:]
        tr, ti = op[:, :128], op[:, 128:]
        acc_re += tr * xr - ti * xi
        acc_im += tr * xi + ti * xr
    blocks = out_ref.shape[0]
    out_ref[:, 0:8, :] = acc_re.reshape(blocks, 8, 128).astype(BF16)
    out_ref[:, 8:16, :] = acc_im.reshape(blocks, 8, 128).astype(BF16)


def down_kernel(inc_ref, cos_ref, sin_ref, receive_ref, near_ref, interp, out_ref, received):
    leaves = received.shape[0]
    half = received.shape[1] // 2
    for s in range(inc_ref.shape[0]):
        lanes = slice(s * 128, (s + 1) * 128)
        block = inc_ref[s].astype(F32)
        re, im = block[0:8][:, None, :], block[8:16][:, None, :]
        cosine, sine = cos_ref[:, lanes][None], sin_ref[:, lanes][None]
        received[:, s * 128 : (s + 1) * 128] = (
            (re * cosine + im * sine).reshape(leaves, 128).astype(BF16)
        )
        received[:, half + s * 128 : half + (s + 1) * 128] = (
            (im * cosine - re * sine).reshape(leaves, 128).astype(BF16)
        )
    back = dot(received[...], interp[...], 1, 1).astype(BF16)
    out_ref[...] = near_ref[...] + dot(back, receive_ref[...])


def near_kernel(own_ref, sibling_ref, cross_ref, col_ref, near_hbm, _, out_ref, buf, hot, sems):
    slots = near_hbm.shape[0]
    copies = []
    for n in range(slots):
        copies.append(pltpu.make_async_copy(near_hbm.at[n], buf.at[n], sems.at[n]))
        copies[n].start()
    rows = out_ref.shape[0]
    lane = lax.broadcasted_iota(I32, (rows, 3 * rows), 1)
    for n in range(slots):
        hot[n * rows : (n + 1) * rows] = jnp.where(
            lane == col_ref[:, n : n + 1], 1.0, 0.0
        ).astype(BF16)
    sources = jnp.concatenate([own_ref[...], sibling_ref[...], cross_ref[...]], axis=0)
    picked = dot(hot[...], sources).astype(BF16)
    total = jnp.zeros(out_ref.shape, F32)
    for n in range(slots):
        copies[n].wait()
        total += dot(picked[n * rows : (n + 1) * rows], buf[n])
    out_ref[...] = total


def halo_partner(i, boxes, dirs):
    b, d = divmod(i, dirs)
    quarter = dirs // 4
    z, r = divmod(d, quarter)
    other = b + 1 if z >= 2 else b - 1
    if other < 0 or other >= boxes:
        return i ^ 1
    return other * dirs + (3 - z) * quarter + r


def on_device(
    boxes,
    dirs,
    currents,
    near_list,
    far_list,
    far_kind,
    aggregate,
    interp,
    receive,
    shift_angle,
    translation,
    near_matrix,
):
    leaves, width = currents.shape
    n = boxes * dirs
    me = lax.axis_index(BOTH)
    box = lax.axis_index("box")
    parents = leaves // 8 * dirs
    slots, near_slots = far_list.shape[1], near_list.shape[1]

    far_half = lax.ppermute(currents, BOTH, [(i, halo_partner(i, boxes, dirs)) for i in range(n)])
    cross = [(i, min(max(i + (1 if i % 2 else -1), 0), n - 1)) for i in range(n)]
    from_cross = lax.ppermute(currents, BOTH, cross)
    from_sibling = lax.ppermute(currents, BOTH, [(i, i ^ 1) for i in range(n)])

    place = jnp.stack([box, me]).astype(I32)
    operators, index, column, cosine, sine, aggregate, interp, receive = call(
        prepare_kernel,
        (
            pltpu.VMEM((slots, parents, 256), BF16),
            pltpu.VMEM((parents, 32), I32),
            pltpu.VMEM((leaves, 32), I32),
            pltpu.VMEM(shift_angle.shape, F32),
            pltpu.VMEM(shift_angle.shape, F32),
            pltpu.VMEM(aggregate.shape, BF16),
            pltpu.VMEM(interp.shape, BF16),
            pltpu.VMEM(receive.shape, BF16),
        ),
        (
            place,
            far_list.T,
            far_kind.T,
            shift_angle,
            translation.reshape(-1, translation.shape[2]),
            near_list.T,
            aggregate,
            interp,
            receive,
        ),
        [whole(pltpu.SMEM)] + [whole(pltpu.HBM)] * 2 + [whole()] * 3 + [whole(pltpu.HBM)] * 3,
        [
            pltpu.VMEM((slots, parents), I32),
            pltpu.VMEM((slots, parents), I32),
            pltpu.VMEM((384, 256), BF16),
            pltpu.SemaphoreType.DMA((5,)),
        ],
        8,
        2 * slots * parents * 384 * 256,
        11 << 20,
    )

    up = call(
        up_kernel,
        jax.ShapeDtypeStruct((dirs, 4 * leaves // 8, 128), BF16),
        (currents, far_half, aggregate, cosine, sine, interp),
        [whole()] * 6,
        [],
        8,
        2 * 128 * 1024 * 4608,
        10 << 20,
    )
    upper = lax.all_to_all(up, "dir", split_axis=0, concat_axis=0, tiled=True)

    near = call(
        near_kernel,
        jax.ShapeDtypeStruct((leaves, width), F32),
        (currents, from_sibling, from_cross, column, near_matrix, up),
        [whole()] * 4 + [whole(pltpu.HBM), whole(pl.ANY)],
        [
            pltpu.VMEM(near_matrix.shape, BF16),
            pltpu.VMEM((near_slots * leaves, 3 * leaves), BF16),
            pltpu.SemaphoreType.DMA((near_slots,)),
        ],
        24,
        2 * leaves * 27 * 512 * 640,
        15 << 20,
    )

    local = call(
        translate_kernel,
        jax.ShapeDtypeStruct((dirs, 2 * leaves // 8, 128), BF16),
        (upper, index, operators, near),
        [whole()] * 3 + [whole(pl.ANY)],
        [],
        8,
        2 * slots * parents * 256 * 256,
        2 << 20,
    )
    incoming = lax.all_to_all(local, "dir", split_axis=0, concat_axis=0, tiled=True)

    return call(
        down_kernel,
        jax.ShapeDtypeStruct((leaves, width), F32),
        (incoming, cosine, sine, receive, near, interp),
        [whole()] * 6,
        [pltpu.VMEM((leaves, interp.shape[1]), BF16)],
        8,
        2 * 64 * 4096 * 1536,
        10 << 20,
    )


def solution(mesh):
    placed = (
        P(BOTH, None),
        P(BOTH, None),
        P(),
        P(),
        P(),
        P(),
        P(),
        P(),
        P(None, None, "dir"),
        P(),
    )
    body = functools.partial(on_device, mesh.shape["box"], mesh.shape["dir"])
    return jax.shard_map(
        body, mesh=mesh, in_specs=placed, out_specs=P(BOTH, None), check_vma=False
    )
```

```python
import functools

import jax
import jax.numpy as jnp
from jax import lax
from jax.experimental import pallas as pl
from jax.experimental.pallas import tpu as pltpu
from jax.sharding import PartitionSpec as P

BF16, F32, I32 = jnp.bfloat16, jnp.float32, jnp.int32
BOTH = ("box", "dir")
VMEM = pltpu.VMEM


def whole(space=VMEM):
    return pl.BlockSpec(memory_space=space)


def call(body, out, args, specs, scratch, mib, flops, moved):
    return pl.pallas_call(
        body,
        out_shape=out,
        in_specs=specs,
        out_specs=jax.tree.map(lambda _: whole(), out),
        scratch_shapes=scratch,
        compiler_params=pltpu.CompilerParams(vmem_limit_bytes=mib << 20),
        cost_estimate=pl.CostEstimate(flops=flops, bytes_accessed=moved, transcendentals=0),
    )(*args)


def in_hbm(*arrays):
    return tuple(pltpu.with_memory_space_constraint(a, pltpu.HBM) for a in arrays)


def in_vmem(array):
    return pltpu.with_memory_space_constraint(array, VMEM)


def dot(a, b, ca=1, cb=0):
    return lax.dot_general(a, b, (((ca,), (cb,)), ((), ())), preferred_element_type=F32)


def prepare_kernel(
    box_ref,
    far_hbm,
    kind_hbm,
    angle_hbm,
    table_hbm,
    near_list_hbm,
    aggregate,
    interp,
    receive,
    operators,
    index_ref,
    column_ref,
    cosine_ref,
    sine_ref,
    aggregate_out,
    interp_out,
    receive_out,
    far_ref,
    kind_ref,
    angle_ref,
    table_ref,
    near_list_ref,
    table,
    sems,
):
    slots, parents = far_ref.shape
    box, me = box_ref[0], box_ref[1]
    mine = pl.ds(pl.multiple_of(box * parents, parents), parents)
    lists = [
        pltpu.make_async_copy(far_hbm.at[:, mine], far_ref, sems.at[0]),
        pltpu.make_async_copy(kind_hbm.at[:, mine], kind_ref, sems.at[1]),
    ]
    lists += [
        pltpu.make_async_copy(near_list_hbm, near_list_ref, sems.at[2]),
        pltpu.make_async_copy(angle_hbm, angle_ref, sems.at[3]),
        pltpu.make_async_copy(table_hbm, table_ref, sems.at[4]),
    ]
    weights = [
        pltpu.make_async_copy(aggregate, aggregate_out, sems.at[5]),
        pltpu.make_async_copy(interp, interp_out, sems.at[6]),
        pltpu.make_async_copy(receive, receive_out, sems.at[7]),
    ]
    for copy in lists + weights:
        copy.start()
    table[...] = jnp.zeros_like(table)
    for copy in lists:
        copy.wait()
    cosine_ref[...] = jnp.cos(angle_ref[...])
    sine_ref[...] = jnp.sin(angle_ref[...])
    kinds = table_ref.shape[0] // 2
    table[0:kinds, 0:128] = table_ref[pl.ds(0, kinds, stride=2), :].astype(BF16)
    table[0:kinds, 128:256] = table_ref[pl.ds(1, kinds, stride=2), :].astype(BF16)

    leaves = near_list_ref.shape[1]
    rel = near_list_ref[...] - me * leaves
    odd = me & 1
    below = jnp.where(odd == 0, 3 * leaves, leaves * 2)
    above = jnp.where(odd == 0, 0, leaves)
    column = jnp.where(rel < 0, rel + below, jnp.where(rel < leaves, rel, rel + above))
    column_ref[...] = jnp.pad(column, ((0, 32 - column.shape[0]), (0, 0))).T

    q = far_ref[...] - box * parents
    half = parents // 2
    g = jnp.where(q < 0, q + half, q - parents)
    own = ((q >> 3) << 4) + (q & 7)
    row = (((g >> 3) & 3) << 4) + 8 + (g & 7)
    low, high = row + ((1 - (g >> 5)) << 6), row + ((3 - (g >> 5)) << 6)
    index = jnp.where(q < 0, low, jnp.where(q < parents, own, high))
    index_ref[...] = jnp.pad(index, ((0, 32 - slots), (0, 0))).T
    kind = jnp.pad(kind_ref[...], ((0, 32 - slots), (0, 0))).T
    lane = lax.broadcasted_iota(I32, (parents, table.shape[0]), 1)
    for j in range(slots):
        hot = jnp.where(lane == kind[:, j : j + 1], 1.0, 0.0).astype(BF16)
        operators[j] = dot(hot, table[...]).astype(BF16)
    for copy in weights:
        copy.wait()


def up_kernel(own_ref, far_ref, agg_ref, cos_ref, sin_ref, interp, out_ref):
    width = 256
    directions = cos_ref.shape[1]
    leaves = own_ref.shape[0]
    rows = 2 * leaves
    parents = rows // 8
    r = lax.broadcasted_iota(I32, (rows, leaves), 0)
    c = lax.broadcasted_iota(I32, (rows, leaves), 1)
    leaf = 8 * (r % parents) + r // parents
    from_own = jnp.where(c == leaf, 1.0, 0.0).astype(BF16)
    from_far = jnp.where(c + leaves == leaf, 1.0, 0.0).astype(BF16)
    cur = (dot(from_own, own_ref[...]) + dot(from_far, far_ref[...])).astype(BF16)
    pattern = dot(cur, agg_ref[...]).astype(BF16)
    for j in range(directions // width):
        re = dot(pattern, interp[:, j * width : (j + 1) * width])
        im = dot(pattern, interp[:, directions + j * width : directions + (j + 1) * width])
        acc_re = jnp.zeros((parents, width), F32)
        acc_im = jnp.zeros((parents, width), F32)
        for k in range(8):
            cosine = cos_ref[pl.ds(k, 1), pl.ds(j * width, width)]
            sine = sin_ref[pl.ds(k, 1), pl.ds(j * width, width)]
            a, b = re[k * parents : (k + 1) * parents], im[k * parents : (k + 1) * parents]
            acc_re += a * cosine - b * sine
            acc_im += a * sine + b * cosine
        for h in range(width // 128):
            s = slice(h * 128, (h + 1) * 128)
            out_ref[j * (width // 128) + h, 0:parents, :] = acc_re[:, s].astype(BF16)
            out_ref[j * (width // 128) + h, parents : 2 * parents, :] = acc_im[:, s].astype(BF16)


def translate_kernel(upper_ref, index_ref, operator_ref, _, out_ref):
    sources = upper_ref.shape[0] * 16
    slots, rows = operator_ref.shape[:2]
    field = jnp.concatenate(
        [
            upper_ref[:, 0:16, :].reshape(sources, 128),
            upper_ref[:, 16:32, :].reshape(sources, 128),
        ],
        axis=1,
    )
    lane = lax.broadcasted_iota(I32, (rows, sources), 1)
    acc_re = jnp.zeros((rows, 128), F32)
    acc_im = jnp.zeros((rows, 128), F32)
    for j in range(slots):
        hot = jnp.where(lane == index_ref[:, j : j + 1], 1.0, 0.0).astype(BF16)
        x = dot(hot, field)
        op = operator_ref[j].astype(F32)
        xr, xi = x[:, :128], x[:, 128:]
        tr, ti = op[:, :128], op[:, 128:]
        acc_re += tr * xr - ti * xi
        acc_im += tr * xi + ti * xr
    blocks = out_ref.shape[0]
    out_ref[:, 0:8, :] = acc_re.reshape(blocks, 8, 128).astype(BF16)
    out_ref[:, 8:16, :] = acc_im.reshape(blocks, 8, 128).astype(BF16)


def down_kernel(inc_ref, cos_ref, sin_ref, receive_ref, near_ref, turned, out_ref, received):
    leaves = received.shape[0]
    half = received.shape[1] // 2
    for s in range(inc_ref.shape[0]):
        lanes = slice(s * 128, (s + 1) * 128)
        block = inc_ref[s].astype(F32)
        re, im = block[0:8][:, None, :], block[8:16][:, None, :]
        cosine, sine = cos_ref[:, lanes][None], sin_ref[:, lanes][None]
        received[:, s * 128 : (s + 1) * 128] = (
            (re * cosine + im * sine).reshape(leaves, 128).astype(BF16)
        )
        received[:, half + s * 128 : half + (s + 1) * 128] = (
            (im * cosine - re * sine).reshape(leaves, 128).astype(BF16)
        )
    back = dot(received[...], turned[...]).astype(BF16)
    out_ref[...] = near_ref[...] + dot(back, receive_ref[...])


def turn_kernel(interp, _, out_ref, buf, sems):
    chunks, rows = buf.shape[:2]
    copies = []
    for j in range(chunks):
        copies.append(pltpu.make_async_copy(interp.at[pl.ds(j * rows, rows)], buf.at[j], sems.at[j]))
        copies[j].start()
    for j in range(chunks):
        copies[j].wait()
        out_ref[:, j * rows : (j + 1) * rows] = buf[j].T


def near_kernel(own_ref, sibling_ref, cross_ref, col_ref, near_hbm, _, out_ref, buf, hot, sems):
    slots = near_hbm.shape[0]
    copies = []
    for n in range(slots):
        copies.append(pltpu.make_async_copy(near_hbm.at[n], buf.at[n], sems.at[n]))
        copies[n].start()
    rows = out_ref.shape[0]
    lane = lax.broadcasted_iota(I32, (rows, 3 * rows), 1)
    for n in range(slots):
        hot[n * rows : (n + 1) * rows] = jnp.where(
            lane == col_ref[:, n : n + 1], 1.0, 0.0
        ).astype(BF16)
    sources = jnp.concatenate([own_ref[...], sibling_ref[...], cross_ref[...]], axis=0)
    picked = dot(hot[...], sources).astype(BF16)
    total = jnp.zeros(out_ref.shape, F32)
    for n in range(slots):
        copies[n].wait()
        total += dot(picked[n * rows : (n + 1) * rows], buf[n])
    out_ref[...] = total


def halo_partner(i, boxes, dirs):
    b, d = divmod(i, dirs)
    quarter = dirs // 4
    z, r = divmod(d, quarter)
    other = b + 1 if z >= 2 else b - 1
    if other < 0 or other >= boxes:
        return i ^ 1
    return other * dirs + (3 - z) * quarter + r


def on_device(
    boxes,
    dirs,
    currents,
    near_list,
    far_list,
    far_kind,
    aggregate,
    interp,
    receive,
    shift_angle,
    translation,
    near_matrix,
):
    leaves, width = currents.shape
    n = boxes * dirs
    me = lax.axis_index(BOTH)
    box = lax.axis_index("box")
    parents = leaves // 8 * dirs
    slots, near_slots = far_list.shape[1], near_list.shape[1]

    far_half = lax.ppermute(currents, BOTH, [(i, halo_partner(i, boxes, dirs)) for i in range(n)])
    cross = [(i, min(max(i + (1 if i % 2 else -1), 0), n - 1)) for i in range(n)]
    from_cross = lax.ppermute(currents, BOTH, cross)
    from_sibling = lax.ppermute(currents, BOTH, [(i, i ^ 1) for i in range(n)])

    place = jnp.stack([box, me]).astype(I32)
    operators, index, column, cosine, sine, aggregate, held, receive = call(
        prepare_kernel,
        (
            pltpu.VMEM((slots, parents, 256), BF16),
            pltpu.VMEM((parents, 32), I32),
            pltpu.VMEM((leaves, 32), I32),
            pltpu.VMEM(shift_angle.shape, F32),
            pltpu.VMEM(shift_angle.shape, F32),
            pltpu.VMEM(aggregate.shape, BF16),
            pltpu.VMEM(interp.shape, BF16),
            pltpu.VMEM(receive.shape, BF16),
        ),
        (
            place,
            *in_hbm(
                far_list.T,
                far_kind.T,
                shift_angle,
                translation.reshape(-1, translation.shape[2]),
                near_list.T,
                aggregate,
                interp,
                receive,
            ),
        ),
        [whole(pltpu.SMEM)] + [whole(pltpu.HBM)] * 8,
        [
            pltpu.VMEM((slots, parents), I32),
            pltpu.VMEM((slots, parents), I32),
            pltpu.VMEM(shift_angle.shape, F32),
            pltpu.VMEM((2 * translation.shape[0], translation.shape[2]), F32),
            pltpu.VMEM((near_slots, leaves), I32),
            pltpu.VMEM((384, 256), BF16),
            pltpu.SemaphoreType.DMA((8,)),
        ],
        8,
        2 * slots * parents * 384 * 256,
        11 << 20,
    )

    up = call(
        up_kernel,
        jax.ShapeDtypeStruct((dirs, 4 * leaves // 8, 128), BF16),
        (currents, far_half, aggregate, cosine, sine, in_vmem(held)),
        [whole()] * 6,
        [],
        8,
        2 * 128 * 1024 * 4608,
        10 << 20,
    )
    upper = lax.all_to_all(up, "dir", split_axis=0, concat_axis=0, tiled=True)

    near = call(
        near_kernel,
        jax.ShapeDtypeStruct((leaves, width), F32),
        (currents, from_sibling, from_cross, column, *in_hbm(near_matrix), up),
        [whole()] * 4 + [whole(pltpu.HBM), whole(pl.ANY)],
        [
            pltpu.VMEM(near_matrix.shape, BF16),
            pltpu.VMEM((near_slots * leaves, 3 * leaves), BF16),
            pltpu.SemaphoreType.DMA((near_slots,)),
        ],
        24,
        2 * leaves * 27 * 512 * 640,
        15 << 20,
    )

    local = call(
        translate_kernel,
        jax.ShapeDtypeStruct((dirs, 2 * leaves // 8, 128), BF16),
        (upper, index, operators, near),
        [whole()] * 3 + [whole(pl.ANY)],
        [],
        8,
        2 * slots * parents * 256 * 256,
        2 << 20,
    )
    incoming = lax.all_to_all(local, "dir", split_axis=0, concat_axis=0, tiled=True)

    turned = call(
        turn_kernel,
        pltpu.VMEM(interp.shape[::-1], BF16),
        (*in_hbm(interp), local),
        [whole(pltpu.HBM), whole(pl.ANY)],
        [
            pltpu.VMEM((8, interp.shape[0] // 8, interp.shape[1]), BF16),
            pltpu.SemaphoreType.DMA((8,)),
        ],
        20,
        2 * 64 * 4096 * 1024,
        12 << 20,
    )

    return call(
        down_kernel,
        jax.ShapeDtypeStruct((leaves, width), F32),
        (incoming, cosine, sine, receive, near, in_vmem(turned)),
        [whole()] * 6,
        [pltpu.VMEM((leaves, interp.shape[1]), BF16)],
        8,
        2 * 64 * 4096 * 1536,
        10 << 20,
    )


def solution(mesh):
    placed = (
        P(BOTH, None),
        P(BOTH, None),
        P(),
        P(),
        P(),
        P(),
        P(),
        P(),
        P(None, None, "dir"),
        P(),
    )
    body = functools.partial(on_device, mesh.shape["box"], mesh.shape["dir"])
    return jax.shard_map(
        body, mesh=mesh, in_specs=placed, out_specs=P(BOTH, None), check_vma=False
    )
```

```python
import functools

import jax
import jax.numpy as jnp
from jax import lax
from jax.experimental import pallas as pl
from jax.experimental.pallas import tpu as pltpu
from jax.sharding import PartitionSpec as P

BF16, F32, I32 = jnp.bfloat16, jnp.float32, jnp.int32
BOTH = ("box", "dir")
VMEM = pltpu.VMEM


def whole(space=VMEM):
    return pl.BlockSpec(memory_space=space)


def call(body, out, args, specs, scratch, mib, flops, moved):
    return pl.pallas_call(
        body,
        out_shape=out,
        in_specs=specs,
        out_specs=jax.tree.map(lambda _: whole(), out),
        scratch_shapes=scratch,
        compiler_params=pltpu.CompilerParams(vmem_limit_bytes=mib << 20),
        cost_estimate=pl.CostEstimate(flops=flops, bytes_accessed=moved, transcendentals=0),
    )(*args)


def in_hbm(*arrays):
    return tuple(pltpu.with_memory_space_constraint(a, pltpu.HBM) for a in arrays)


def in_vmem(array):
    return pltpu.with_memory_space_constraint(array, VMEM)


def dot(a, b, ca=1, cb=0):
    return lax.dot_general(a, b, (((ca,), (cb,)), ((), ())), preferred_element_type=F32)


def prepare_kernel(
    angle, aggregate, interp, cosine_ref, sine_ref, aggregate_out, interp_out, angle_ref, sems
):
    copies = [
        pltpu.make_async_copy(angle, angle_ref, sems.at[2]),
        pltpu.make_async_copy(aggregate, aggregate_out, sems.at[0]),
        pltpu.make_async_copy(interp, interp_out, sems.at[1]),
    ]
    for copy in copies:
        copy.start()
    copies[0].wait()
    cosine_ref[...] = jnp.cos(angle_ref[...])
    sine_ref[...] = jnp.sin(angle_ref[...])
    for copy in copies[1:]:
        copy.wait()


def tables_kernel(
    place_ref,
    far_hbm,
    kind_hbm,
    table_hbm,
    near_list_hbm,
    _,
    operators,
    index_ref,
    column_ref,
    far_ref,
    kind_ref,
    table_ref,
    near_list_ref,
    table,
    sems,
):
    slots, parents = far_ref.shape
    box, me = place_ref[0], place_ref[1]
    mine = pl.ds(pl.multiple_of(box * parents, parents), parents)
    copies = [
        pltpu.make_async_copy(table_hbm, table_ref, sems.at[0]),
        pltpu.make_async_copy(far_hbm.at[:, mine], far_ref, sems.at[1]),
        pltpu.make_async_copy(kind_hbm.at[:, mine], kind_ref, sems.at[2]),
        pltpu.make_async_copy(near_list_hbm, near_list_ref, sems.at[3]),
    ]
    for copy in copies:
        copy.start()
    table[...] = jnp.zeros_like(table)
    for copy in copies:
        copy.wait()
    kinds = table_ref.shape[0] // 2
    table[0:kinds, 0:128] = table_ref[pl.ds(0, kinds, stride=2), :].astype(BF16)
    table[0:kinds, 128:256] = table_ref[pl.ds(1, kinds, stride=2), :].astype(BF16)

    leaves = near_list_ref.shape[1]
    rel = near_list_ref[...] - me * leaves
    odd = me & 1
    below = jnp.where(odd == 0, 3 * leaves, leaves * 2)
    above = jnp.where(odd == 0, 0, leaves)
    column = jnp.where(rel < 0, rel + below, jnp.where(rel < leaves, rel, rel + above))
    column_ref[...] = jnp.pad(column, ((0, 32 - column.shape[0]), (0, 0))).T

    q = far_ref[...] - box * parents
    half = parents // 2
    g = jnp.where(q < 0, q + half, q - parents)
    own = ((q >> 3) << 4) + (q & 7)
    row = (((g >> 3) & 3) << 4) + 8 + (g & 7)
    low, high = row + ((1 - (g >> 5)) << 6), row + ((3 - (g >> 5)) << 6)
    index = jnp.where(q < 0, low, jnp.where(q < parents, own, high))
    index_ref[...] = jnp.pad(index, ((0, 32 - slots), (0, 0))).T
    kind = jnp.pad(kind_ref[...], ((0, 32 - slots), (0, 0))).T
    lane = lax.broadcasted_iota(I32, (parents, table.shape[0]), 1)
    for j in range(slots):
        hot = jnp.where(lane == kind[:, j : j + 1], 1.0, 0.0).astype(BF16)
        operators[j] = dot(hot, table[...]).astype(BF16)


def up_kernel(own_ref, far_ref, agg_ref, cos_ref, sin_ref, interp, out_ref, relay_ref):
    relay_ref[...] = own_ref[...]
    width = 256
    directions = cos_ref.shape[1]
    leaves = own_ref.shape[0]
    rows = 2 * leaves
    parents = rows // 8
    r = lax.broadcasted_iota(I32, (rows, leaves), 0)
    c = lax.broadcasted_iota(I32, (rows, leaves), 1)
    leaf = 8 * (r % parents) + r // parents
    from_own = jnp.where(c == leaf, 1.0, 0.0).astype(BF16)
    from_far = jnp.where(c + leaves == leaf, 1.0, 0.0).astype(BF16)
    cur = (dot(from_own, own_ref[...]) + dot(from_far, far_ref[...])).astype(BF16)
    pattern = dot(cur, agg_ref[...]).astype(BF16)
    for j in range(directions // width):
        re = dot(pattern, interp[:, j * width : (j + 1) * width])
        im = dot(pattern, interp[:, directions + j * width : directions + (j + 1) * width])
        acc_re = jnp.zeros((parents, width), F32)
        acc_im = jnp.zeros((parents, width), F32)
        for k in range(8):
            cosine = cos_ref[pl.ds(k, 1), pl.ds(j * width, width)]
            sine = sin_ref[pl.ds(k, 1), pl.ds(j * width, width)]
            a, b = re[k * parents : (k + 1) * parents], im[k * parents : (k + 1) * parents]
            acc_re += a * cosine - b * sine
            acc_im += a * sine + b * cosine
        for h in range(width // 128):
            s = slice(h * 128, (h + 1) * 128)
            out_ref[j * (width // 128) + h, 0:parents, :] = acc_re[:, s].astype(BF16)
            out_ref[j * (width // 128) + h, parents : 2 * parents, :] = acc_im[:, s].astype(BF16)


def translate_kernel(upper_ref, index_ref, operator_ref, out_ref):
    sources = upper_ref.shape[0] * 16
    slots, rows = operator_ref.shape[:2]
    field = jnp.concatenate(
        [
            upper_ref[:, 0:16, :].reshape(sources, 128),
            upper_ref[:, 16:32, :].reshape(sources, 128),
        ],
        axis=1,
    )
    lane = lax.broadcasted_iota(I32, (rows, sources), 1)
    acc_re = jnp.zeros((rows, 128), F32)
    acc_im = jnp.zeros((rows, 128), F32)
    for j in range(slots):
        hot = jnp.where(lane == index_ref[:, j : j + 1], 1.0, 0.0).astype(BF16)
        x = dot(hot, field)
        op = operator_ref[j].astype(F32)
        xr, xi = x[:, :128], x[:, 128:]
        tr, ti = op[:, :128], op[:, 128:]
        acc_re += tr * xr - ti * xi
        acc_im += tr * xi + ti * xr
    blocks = out_ref.shape[0]
    out_ref[:, 0:8, :] = acc_re.reshape(blocks, 8, 128).astype(BF16)
    out_ref[:, 8:16, :] = acc_im.reshape(blocks, 8, 128).astype(BF16)


def down_kernel(inc_ref, cos_ref, sin_ref, near_ref, receive, interp, out_ref, buf, received, receive_ref, sems):
    width = 256
    chunks = buf.shape[1] // width
    copies = []
    for j in range(chunks):
        lanes = pl.ds(j * width, width)
        copies.append(pltpu.make_async_copy(interp.at[:, lanes], buf.at[:, lanes], sems.at[j]))
    copies.append(pltpu.make_async_copy(receive, receive_ref, sems.at[chunks]))
    for copy in copies:
        copy.start()
    leaves = received.shape[0]
    half = received.shape[1] // 2
    for s in range(inc_ref.shape[0]):
        lanes = slice(s * 128, (s + 1) * 128)
        block = inc_ref[s].astype(F32)
        re, im = block[0:8][:, None, :], block[8:16][:, None, :]
        cosine, sine = cos_ref[:, lanes][None], sin_ref[:, lanes][None]
        received[:, s * 128 : (s + 1) * 128] = (
            (re * cosine + im * sine).reshape(leaves, 128).astype(BF16)
        )
        received[:, half + s * 128 : half + (s + 1) * 128] = (
            (im * cosine - re * sine).reshape(leaves, 128).astype(BF16)
        )
    back = jnp.zeros((leaves, buf.shape[0]), F32)
    for j in range(chunks):
        lanes = slice(j * width, (j + 1) * width)
        copies[j].wait()
        back += dot(received[:, lanes], buf[:, lanes], 1, 1)
    copies[chunks].wait()
    out_ref[...] = near_ref[...] + dot(back.astype(BF16), receive_ref[...])


def near_kernel(own_ref, sibling_ref, cross_ref, col_ref, near_hbm, _, out_ref, buf, hot, sems):
    slots = near_hbm.shape[0]
    copies = []
    for n in range(slots):
        copies.append(pltpu.make_async_copy(near_hbm.at[n], buf.at[n], sems.at[n]))
        copies[n].start()
    rows = out_ref.shape[0]
    lane = lax.broadcasted_iota(I32, (rows, 3 * rows), 1)
    for n in range(slots):
        hot[n * rows : (n + 1) * rows] = jnp.where(
            lane == col_ref[:, n : n + 1], 1.0, 0.0
        ).astype(BF16)
    sources = jnp.concatenate([own_ref[...], sibling_ref[...], cross_ref[...]], axis=0)
    picked = dot(hot[...], sources).astype(BF16)
    total = jnp.zeros(out_ref.shape, F32)
    for n in range(slots):
        copies[n].wait()
        total += dot(picked[n * rows : (n + 1) * rows], buf[n])
    out_ref[...] = total


def halo_partner(i, boxes, dirs):
    b, d = divmod(i, dirs)
    quarter = dirs // 4
    z, r = divmod(d, quarter)
    other = b + 1 if z >= 2 else b - 1
    if other < 0 or other >= boxes:
        return i ^ 1
    return other * dirs + (3 - z) * quarter + r


def on_device(
    boxes,
    dirs,
    currents,
    near_list,
    far_list,
    far_kind,
    aggregate,
    interp,
    receive,
    shift_angle,
    translation,
    near_matrix,
):
    leaves, width = currents.shape
    n = boxes * dirs
    me = lax.axis_index(BOTH)
    box = lax.axis_index("box")
    parents = leaves // 8 * dirs
    slots, near_slots = far_list.shape[1], near_list.shape[1]

    far_half = lax.ppermute(currents, BOTH, [(i, halo_partner(i, boxes, dirs)) for i in range(n)])
    from_sibling = lax.ppermute(currents, BOTH, [(i, i ^ 1) for i in range(n)])

    cosine, sine, held_aggregate, held = call(
        prepare_kernel,
        (
            pltpu.VMEM(shift_angle.shape, F32),
            pltpu.VMEM(shift_angle.shape, F32),
            pltpu.VMEM(aggregate.shape, BF16),
            pltpu.VMEM(interp.shape, BF16),
        ),
        in_hbm(shift_angle, aggregate, interp),
        [whole(pltpu.HBM)] * 3,
        [pltpu.VMEM(shift_angle.shape, F32), pltpu.SemaphoreType.DMA((3,))],
        8,
        1 << 28,
        9 << 20,
    )

    up, relay = call(
        up_kernel,
        (
            jax.ShapeDtypeStruct((dirs, 4 * leaves // 8, 128), BF16),
            jax.ShapeDtypeStruct(currents.shape, BF16),
        ),
        (currents, far_half, held_aggregate, cosine, sine, in_vmem(held)),
        [whole()] * 6,
        [],
        8,
        2 * 128 * 1024 * 4608,
        10 << 20,
    )
    upper = lax.all_to_all(up, "dir", split_axis=0, concat_axis=0, tiled=True)

    cross = [(i, min(max(i + (1 if i % 2 else -1), 0), n - 1)) for i in range(n)]
    from_cross = lax.ppermute(relay, BOTH, cross)
    place = jnp.stack([box, me]).astype(I32)
    operators, index, column = call(
        tables_kernel,
        (
            pltpu.VMEM((slots, parents, 256), BF16),
            pltpu.VMEM((parents, 32), I32),
            pltpu.VMEM((leaves, 32), I32),
        ),
        (
            place,
            *in_hbm(
                far_list.T,
                far_kind.T,
                translation.reshape(-1, translation.shape[2]),
                near_list.T,
            ),
            relay,
        ),
        [whole(pltpu.SMEM)] + [whole(pltpu.HBM)] * 4 + [whole(pl.ANY)],
        [
            pltpu.VMEM((slots, parents), I32),
            pltpu.VMEM((slots, parents), I32),
            pltpu.VMEM((2 * translation.shape[0], translation.shape[2]), F32),
            pltpu.VMEM((near_slots, leaves), I32),
            pltpu.VMEM((384, 256), BF16),
            pltpu.SemaphoreType.DMA((4,)),
        ],
        8,
        2 * slots * parents * 384 * 256,
        2 << 20,
    )

    local = call(
        translate_kernel,
        jax.ShapeDtypeStruct((dirs, 2 * leaves // 8, 128), BF16),
        (upper, index, operators),
        [whole()] * 3,
        [],
        8,
        2 * slots * parents * 256 * 256,
        2 << 20,
    )
    incoming = lax.all_to_all(local, "dir", split_axis=0, concat_axis=0, tiled=True)

    near = call(
        near_kernel,
        jax.ShapeDtypeStruct((leaves, width), F32),
        (currents, from_sibling, from_cross, column, *in_hbm(near_matrix), local),
        [whole()] * 4 + [whole(pltpu.HBM), whole(pl.ANY)],
        [
            pltpu.VMEM(near_matrix.shape, BF16),
            pltpu.VMEM((near_slots * leaves, 3 * leaves), BF16),
            pltpu.SemaphoreType.DMA((near_slots,)),
        ],
        24,
        2 * leaves * 27 * 512 * 640,
        15 << 20,
    )

    return call(
        down_kernel,
        jax.ShapeDtypeStruct((leaves, width), F32),
        (incoming, cosine, sine, near, *in_hbm(receive, interp)),
        [whole()] * 4 + [whole(pltpu.HBM)] * 2,
        [
            pltpu.VMEM(interp.shape, BF16),
            pltpu.VMEM((leaves, interp.shape[1]), BF16),
            pltpu.VMEM(receive.shape, BF16),
            pltpu.SemaphoreType.DMA((interp.shape[1] // 256 + 1,)),
        ],
        16,
        2 * 64 * 4096 * 1536,
        10 << 20,
    )


def solution(mesh):
    placed = (
        P(BOTH, None),
        P(BOTH, None),
        P(),
        P(),
        P(),
        P(),
        P(),
        P(),
        P(None, None, "dir"),
        P(),
    )
    body = functools.partial(on_device, mesh.shape["box"], mesh.shape["dir"])
    return jax.shard_map(
        body, mesh=mesh, in_specs=placed, out_specs=P(BOTH, None), check_vma=False
    )
```

```python
import functools

import jax
import jax.numpy as jnp
from jax import lax
from jax.experimental import pallas as pl
from jax.experimental.pallas import tpu as pltpu
from jax.sharding import PartitionSpec as P

BF16, F32, I32 = jnp.bfloat16, jnp.float32, jnp.int32
BOTH = ("box", "dir")
VMEM = pltpu.VMEM


def whole(space=VMEM):
    return pl.BlockSpec(memory_space=space)


def call(body, out, args, specs, scratch, mib, flops, moved):
    return pl.pallas_call(
        body,
        out_shape=out,
        in_specs=specs,
        out_specs=jax.tree.map(lambda _: whole(), out),
        scratch_shapes=scratch,
        compiler_params=pltpu.CompilerParams(vmem_limit_bytes=mib << 20),
        cost_estimate=pl.CostEstimate(flops=flops, bytes_accessed=moved, transcendentals=0),
    )(*args)


def in_hbm(*arrays):
    return tuple(pltpu.with_memory_space_constraint(a, pltpu.HBM) for a in arrays)


def in_vmem(array):
    return pltpu.with_memory_space_constraint(array, VMEM)


def dot(a, b, ca=1, cb=0):
    return lax.dot_general(a, b, (((ca,), (cb,)), ((), ())), preferred_element_type=F32)


def prepare_kernel(
    place_ref,
    far_hbm,
    kind_hbm,
    angle_hbm,
    table_hbm,
    near_list_hbm,
    aggregate,
    interp,
    operators,
    index_ref,
    column_ref,
    cosine_ref,
    sine_ref,
    aggregate_out,
    interp_out,
    far_ref,
    kind_ref,
    angle_ref,
    table_ref,
    near_list_ref,
    table,
    sems,
):
    slots, parents = far_ref.shape
    box, me = place_ref[0], place_ref[1]
    mine = pl.ds(pl.multiple_of(box * parents, parents), parents)
    copies = [
        pltpu.make_async_copy(table_hbm, table_ref, sems.at[0]),
        pltpu.make_async_copy(far_hbm.at[:, mine], far_ref, sems.at[1]),
        pltpu.make_async_copy(kind_hbm.at[:, mine], kind_ref, sems.at[2]),
        pltpu.make_async_copy(near_list_hbm, near_list_ref, sems.at[3]),
        pltpu.make_async_copy(angle_hbm, angle_ref, sems.at[4]),
    ]
    weights = [
        pltpu.make_async_copy(aggregate, aggregate_out, sems.at[5]),
        pltpu.make_async_copy(interp, interp_out, sems.at[6]),
    ]
    for copy in copies + weights:
        copy.start()
    table[...] = jnp.zeros_like(table)
    for copy in copies:
        copy.wait()
    cosine_ref[...] = jnp.cos(angle_ref[...])
    sine_ref[...] = jnp.sin(angle_ref[...])
    kinds = table_ref.shape[0] // 2
    table[0:kinds, 0:128] = table_ref[pl.ds(0, kinds, stride=2), :].astype(BF16)
    table[0:kinds, 128:256] = table_ref[pl.ds(1, kinds, stride=2), :].astype(BF16)

    leaves = near_list_ref.shape[1]
    rel = near_list_ref[...] - me * leaves
    odd = me & 1
    below = jnp.where(odd == 0, 3 * leaves, leaves * 2)
    above = jnp.where(odd == 0, 0, leaves)
    column = jnp.where(rel < 0, rel + below, jnp.where(rel < leaves, rel, rel + above))
    column_ref[...] = jnp.pad(column, ((0, 32 - column.shape[0]), (0, 0))).T

    q = far_ref[...] - box * parents
    half = parents // 2
    g = jnp.where(q < 0, q + half, q - parents)
    own = ((q >> 3) << 4) + (q & 7)
    row = ((((g >> 3) & 3) ^ 2) << 4) + 8 + (g & 7)
    low, high = row + ((2 + (g >> 5)) << 6), row + ((g >> 5) << 6)
    index = jnp.where(q < 0, low, jnp.where(q < parents, own, high))
    index_ref[...] = jnp.pad(index, ((0, 32 - slots), (0, 0))).T
    kind = jnp.pad(kind_ref[...], ((0, 32 - slots), (0, 0))).T
    lane = lax.broadcasted_iota(I32, (parents, table.shape[0]), 1)
    for j in range(slots):
        hot = jnp.where(lane == kind[:, j : j + 1], 1.0, 0.0).astype(BF16)
        operators[j] = dot(hot, table[...]).astype(BF16)
    for copy in weights:
        copy.wait()


def up_kernel(own_ref, far_ref, agg_ref, cos_ref, sin_ref, interp, out_ref, relay_ref):
    relay_ref[...] = own_ref[...]
    width = 256
    directions = cos_ref.shape[1]
    leaves = own_ref.shape[0]
    rows = 2 * leaves
    parents = rows // 8
    r = lax.broadcasted_iota(I32, (rows, leaves), 0)
    c = lax.broadcasted_iota(I32, (rows, leaves), 1)
    leaf = 8 * (r % parents) + r // parents
    from_own = jnp.where(c == leaf, 1.0, 0.0).astype(BF16)
    from_far = jnp.where(c + leaves == leaf, 1.0, 0.0).astype(BF16)
    cur = (dot(from_own, own_ref[...]) + dot(from_far, far_ref[...])).astype(BF16)
    pattern = dot(cur, agg_ref[...]).astype(BF16)
    for j in range(directions // width):
        re = dot(pattern, interp[:, j * width : (j + 1) * width])
        im = dot(pattern, interp[:, directions + j * width : directions + (j + 1) * width])
        acc_re = jnp.zeros((parents, width), F32)
        acc_im = jnp.zeros((parents, width), F32)
        for k in range(8):
            cosine = cos_ref[pl.ds(k, 1), pl.ds(j * width, width)]
            sine = sin_ref[pl.ds(k, 1), pl.ds(j * width, width)]
            a, b = re[k * parents : (k + 1) * parents], im[k * parents : (k + 1) * parents]
            acc_re += a * cosine - b * sine
            acc_im += a * sine + b * cosine
        for h in range(width // 128):
            s = slice(h * 128, (h + 1) * 128)
            out_ref[j * (width // 128) + h, 0:parents, :] = acc_re[:, s].astype(BF16)
            out_ref[j * (width // 128) + h, parents : 2 * parents, :] = acc_im[:, s].astype(BF16)


def translate_kernel(upper_ref, index_ref, operator_ref, out_ref):
    sources = upper_ref.shape[0] * 16
    slots, rows = operator_ref.shape[:2]
    field = jnp.concatenate(
        [
            upper_ref[:, 0:16, :].reshape(sources, 128),
            upper_ref[:, 16:32, :].reshape(sources, 128),
        ],
        axis=1,
    )
    lane = lax.broadcasted_iota(I32, (rows, sources), 1)
    acc_re = jnp.zeros((rows, 128), F32)
    acc_im = jnp.zeros((rows, 128), F32)
    for j in range(slots):
        hot = jnp.where(lane == index_ref[:, j : j + 1], 1.0, 0.0).astype(BF16)
        x = dot(hot, field)
        op = operator_ref[j].astype(F32)
        xr, xi = x[:, :128], x[:, 128:]
        tr, ti = op[:, :128], op[:, 128:]
        acc_re += tr * xr - ti * xi
        acc_im += tr * xi + ti * xr
    blocks = out_ref.shape[0]
    out_ref[:, 0:8, :] = acc_re.reshape(blocks, 8, 128).astype(BF16)
    out_ref[:, 8:16, :] = acc_im.reshape(blocks, 8, 128).astype(BF16)


def down_kernel(inc_ref, cos_ref, sin_ref, near_ref, receive, interp, out_ref, buf, received, receive_ref, sems):
    width = 256
    chunks = buf.shape[1] // width
    copies = []
    for j in range(chunks):
        lanes = pl.ds(j * width, width)
        copies.append(pltpu.make_async_copy(interp.at[:, lanes], buf.at[:, lanes], sems.at[j]))
    copies.append(pltpu.make_async_copy(receive, receive_ref, sems.at[chunks]))
    for copy in copies:
        copy.start()
    leaves = received.shape[0]
    half = received.shape[1] // 2
    for s in range(inc_ref.shape[0]):
        lanes = slice(s * 128, (s + 1) * 128)
        block = inc_ref[s].astype(F32)
        re, im = block[0:8][:, None, :], block[8:16][:, None, :]
        cosine, sine = cos_ref[:, lanes][None], sin_ref[:, lanes][None]
        received[:, s * 128 : (s + 1) * 128] = (
            (re * cosine + im * sine).reshape(leaves, 128).astype(BF16)
        )
        received[:, half + s * 128 : half + (s + 1) * 128] = (
            (im * cosine - re * sine).reshape(leaves, 128).astype(BF16)
        )
    back = jnp.zeros((leaves, buf.shape[0]), F32)
    for j in range(chunks):
        lanes = slice(j * width, (j + 1) * width)
        copies[j].wait()
        back += dot(received[:, lanes], buf[:, lanes], 1, 1)
    copies[chunks].wait()
    out_ref[...] = near_ref[...] + dot(back.astype(BF16), receive_ref[...])


def near_kernel(own_ref, sibling_ref, cross_ref, col_ref, near_hbm, _, out_ref, buf, hot, sems):
    slots = near_hbm.shape[0]
    copies = []
    for n in range(slots):
        copies.append(pltpu.make_async_copy(near_hbm.at[n], buf.at[n], sems.at[n]))
        copies[n].start()
    rows = out_ref.shape[0]
    lane = lax.broadcasted_iota(I32, (rows, 3 * rows), 1)
    for n in range(slots):
        hot[n * rows : (n + 1) * rows] = jnp.where(
            lane == col_ref[:, n : n + 1], 1.0, 0.0
        ).astype(BF16)
    sources = jnp.concatenate([own_ref[...], sibling_ref[...], cross_ref[...]], axis=0)
    picked = dot(hot[...], sources).astype(BF16)
    total = jnp.zeros(out_ref.shape, F32)
    for n in range(slots):
        copies[n].wait()
        total += dot(picked[n * rows : (n + 1) * rows], buf[n])
    out_ref[...] = total


def halo_target(i, boxes, dirs):
    b, d = divmod(i, dirs)
    z, r = divmod(d, dirs // 4)
    other = b + 1 if z >= 2 else b - 1
    if other < 0 or other >= boxes:
        return b * dirs + (3 - z) * (dirs // 4) + r
    return other * dirs + z * (dirs // 4) + (r ^ 2)


def on_device(
    boxes,
    dirs,
    currents,
    near_list,
    far_list,
    far_kind,
    aggregate,
    interp,
    receive,
    shift_angle,
    translation,
    near_matrix,
):
    leaves, width = currents.shape
    n = boxes * dirs
    me = lax.axis_index(BOTH)
    box = lax.axis_index("box")
    parents = leaves // 8 * dirs
    slots, near_slots = far_list.shape[1], near_list.shape[1]

    far_half = lax.ppermute(currents, BOTH, [(i, halo_target(i, boxes, dirs)) for i in range(n)])
    from_sibling = lax.ppermute(currents, BOTH, [(i, i ^ 1) for i in range(n)])

    place = jnp.stack([box, me]).astype(I32)
    operators, index, column, cosine, sine, held_aggregate, held = call(
        prepare_kernel,
        (
            pltpu.VMEM((slots, parents, 256), BF16),
            pltpu.VMEM((parents, 32), I32),
            pltpu.VMEM((leaves, 32), I32),
            pltpu.VMEM(shift_angle.shape, F32),
            pltpu.VMEM(shift_angle.shape, F32),
            pltpu.VMEM(aggregate.shape, BF16),
            pltpu.VMEM(interp.shape, BF16),
        ),
        (
            place,
            *in_hbm(
                far_list.T,
                far_kind.T,
                shift_angle,
                translation.reshape(-1, translation.shape[2]),
                near_list.T,
                aggregate,
                interp,
            ),
        ),
        [whole(pltpu.SMEM)] + [whole(pltpu.HBM)] * 7,
        [
            pltpu.VMEM((slots, parents), I32),
            pltpu.VMEM((slots, parents), I32),
            pltpu.VMEM(shift_angle.shape, F32),
            pltpu.VMEM((2 * translation.shape[0], translation.shape[2]), F32),
            pltpu.VMEM((near_slots, leaves), I32),
            pltpu.VMEM((384, 256), BF16),
            pltpu.SemaphoreType.DMA((7,)),
        ],
        8,
        2 * slots * parents * 384 * 256,
        11 << 20,
    )

    up, relay = call(
        up_kernel,
        (
            jax.ShapeDtypeStruct((dirs, 4 * leaves // 8, 128), BF16),
            jax.ShapeDtypeStruct(currents.shape, BF16),
        ),
        (currents, far_half, held_aggregate, cosine, sine, in_vmem(held)),
        [whole()] * 6,
        [],
        8,
        2 * 128 * 1024 * 4608,
        10 << 20,
    )
    upper = lax.all_to_all(up, "dir", split_axis=0, concat_axis=0, tiled=True)

    cross = [(i, min(max(i + (1 if i % 2 else -1), 0), n - 1)) for i in range(n)]
    from_cross = lax.ppermute(relay, BOTH, cross)
    local = call(
        translate_kernel,
        jax.ShapeDtypeStruct((dirs, 2 * leaves // 8, 128), BF16),
        (upper, index, operators),
        [whole()] * 3,
        [],
        8,
        2 * slots * parents * 256 * 256,
        2 << 20,
    )
    incoming = lax.all_to_all(local, "dir", split_axis=0, concat_axis=0, tiled=True)

    near = call(
        near_kernel,
        jax.ShapeDtypeStruct((leaves, width), F32),
        (currents, from_sibling, from_cross, column, *in_hbm(near_matrix), local),
        [whole()] * 4 + [whole(pltpu.HBM), whole(pl.ANY)],
        [
            pltpu.VMEM(near_matrix.shape, BF16),
            pltpu.VMEM((near_slots * leaves, 3 * leaves), BF16),
            pltpu.SemaphoreType.DMA((near_slots,)),
        ],
        24,
        2 * leaves * 27 * 512 * 640,
        15 << 20,
    )

    return call(
        down_kernel,
        jax.ShapeDtypeStruct((leaves, width), F32),
        (incoming, cosine, sine, near, *in_hbm(receive, interp)),
        [whole()] * 4 + [whole(pltpu.HBM)] * 2,
        [
            pltpu.VMEM(interp.shape, BF16),
            pltpu.VMEM((leaves, interp.shape[1]), BF16),
            pltpu.VMEM(receive.shape, BF16),
            pltpu.SemaphoreType.DMA((interp.shape[1] // 256 + 1,)),
        ],
        16,
        2 * 64 * 4096 * 1536,
        10 << 20,
    )


def solution(mesh):
    placed = (
        P(BOTH, None),
        P(BOTH, None),
        P(),
        P(),
        P(),
        P(),
        P(),
        P(),
        P(None, None, "dir"),
        P(),
    )
    body = functools.partial(on_device, mesh.shape["box"], mesh.shape["dir"])
    return jax.shard_map(
        body, mesh=mesh, in_specs=placed, out_specs=P(BOTH, None), check_vma=False
    )
```

```python
import functools

import jax
import jax.numpy as jnp
from jax import lax
from jax.experimental import pallas as pl
from jax.experimental.pallas import tpu as pltpu
from jax.sharding import PartitionSpec as P

BF16, F32, I32 = jnp.bfloat16, jnp.float32, jnp.int32
BOTH = ("box", "dir")
VMEM = pltpu.VMEM
WIDTH = 256
EARLY = 5
KEPT = 3


def whole(space=VMEM):
    return pl.BlockSpec(memory_space=space)


def call(body, out, args, specs, scratch, mib, flops, moved):
    return pl.pallas_call(
        body,
        out_shape=out,
        in_specs=specs,
        out_specs=jax.tree.map(lambda _: whole(), out),
        scratch_shapes=scratch,
        compiler_params=pltpu.CompilerParams(vmem_limit_bytes=mib << 20),
        cost_estimate=pl.CostEstimate(flops=flops, bytes_accessed=moved, transcendentals=0),
    )(*args)


def in_hbm(*arrays):
    return tuple(pltpu.with_memory_space_constraint(a, pltpu.HBM) for a in arrays)


def in_vmem(array):
    return pltpu.with_memory_space_constraint(array, VMEM)


def dot(a, b, ca=1, cb=0):
    return lax.dot_general(a, b, (((ca,), (cb,)), ((), ())), preferred_element_type=F32)


def early_copies(interp, held, sems, at):
    span, half = EARLY * WIDTH, interp.shape[1] // 2
    return [
        pltpu.make_async_copy(
            interp.at[:, pl.ds(part * half, span)],
            held.at[:, pl.ds(part * span, span)],
            sems.at[at + part],
        )
        for part in range(2)
    ]


def prepare_kernel(
    place_ref,
    far_hbm,
    kind_hbm,
    angle_hbm,
    table_hbm,
    near_list_hbm,
    aggregate,
    interp,
    operators,
    index_ref,
    column_ref,
    cosine_ref,
    sine_ref,
    aggregate_out,
    interp_out,
    far_ref,
    kind_ref,
    angle_ref,
    table_ref,
    near_list_ref,
    table,
    sems,
):
    slots, parents = far_ref.shape
    box, me = place_ref[0], place_ref[1]
    mine = pl.ds(pl.multiple_of(box * parents, parents), parents)
    copies = [
        pltpu.make_async_copy(table_hbm, table_ref, sems.at[0]),
        pltpu.make_async_copy(far_hbm.at[:, mine], far_ref, sems.at[1]),
        pltpu.make_async_copy(kind_hbm.at[:, mine], kind_ref, sems.at[2]),
        pltpu.make_async_copy(near_list_hbm, near_list_ref, sems.at[3]),
        pltpu.make_async_copy(angle_hbm, angle_ref, sems.at[4]),
    ]
    weights = [
        pltpu.make_async_copy(aggregate, aggregate_out, sems.at[5]),
        *early_copies(interp, interp_out, sems, 6),
    ]
    for copy in copies + weights:
        copy.start()
    table[...] = jnp.zeros_like(table)
    for copy in copies:
        copy.wait()
    cosine_ref[...] = jnp.cos(angle_ref[...])
    sine_ref[...] = jnp.sin(angle_ref[...])
    kinds = table_ref.shape[0] // 2
    table[0:kinds, 0:128] = table_ref[pl.ds(0, kinds, stride=2), :].astype(BF16)
    table[0:kinds, 128:256] = table_ref[pl.ds(1, kinds, stride=2), :].astype(BF16)

    leaves = near_list_ref.shape[1]
    rel = near_list_ref[...] - me * leaves
    odd = me & 1
    below = jnp.where(odd == 0, 3 * leaves, leaves * 2)
    above = jnp.where(odd == 0, 0, leaves)
    column = jnp.where(rel < 0, rel + below, jnp.where(rel < leaves, rel, rel + above))
    column_ref[...] = jnp.pad(column, ((0, 32 - column.shape[0]), (0, 0))).T

    q = far_ref[...] - box * parents
    half = parents // 2
    g = jnp.where(q < 0, q + half, q - parents)
    own = ((q >> 3) << 4) + (q & 7)
    row = ((((g >> 3) & 3) ^ 2) << 4) + 8 + (g & 7)
    low, high = row + ((2 + (g >> 5)) << 6), row + ((g >> 5) << 6)
    index = jnp.where(q < 0, low, jnp.where(q < parents, own, high))
    index_ref[...] = jnp.pad(index, ((0, 32 - slots), (0, 0))).T
    kind = jnp.pad(kind_ref[...], ((0, 32 - slots), (0, 0))).T
    lane = lax.broadcasted_iota(I32, (parents, table.shape[0]), 1)
    for j in range(slots):
        hot = jnp.where(lane == kind[:, j : j + 1], 1.0, 0.0).astype(BF16)
        operators[j] = dot(hot, table[...]).astype(BF16)
    for copy in weights:
        copy.wait()


def up_kernel(
    own_ref, far_ref, agg_ref, cos_ref, sin_ref, held, interp, out_ref, relay_ref, late, sems
):
    rest = late.shape[1] // 2
    copies = []
    for j in range(rest // WIDTH):
        for part in range(2):
            copies.append(
                pltpu.make_async_copy(
                    interp.at[
                        :, pl.ds(part * cos_ref.shape[1] + (EARLY + j) * WIDTH, WIDTH)
                    ],
                    late.at[:, pl.ds(part * rest + j * WIDTH, WIDTH)],
                    sems.at[2 * j + part],
                )
            )
    for copy in copies:
        copy.start()
    relay_ref[...] = own_ref[...]
    width = WIDTH
    directions = cos_ref.shape[1]
    leaves = own_ref.shape[0]
    rows = 2 * leaves
    parents = rows // 8
    r = lax.broadcasted_iota(I32, (rows, leaves), 0)
    c = lax.broadcasted_iota(I32, (rows, leaves), 1)
    leaf = 8 * (r % parents) + r // parents
    from_own = jnp.where(c == leaf, 1.0, 0.0).astype(BF16)
    from_far = jnp.where(c + leaves == leaf, 1.0, 0.0).astype(BF16)
    cur = (dot(from_own, own_ref[...]) + dot(from_far, far_ref[...])).astype(BF16)
    pattern = dot(cur, agg_ref[...]).astype(BF16)
    for j in range(directions // width):
        source, at, step = held, j * width, EARLY * WIDTH
        if j >= EARLY:
            source, at, step = late, (j - EARLY) * width, rest
            copies[2 * (j - EARLY)].wait()
            copies[2 * (j - EARLY) + 1].wait()
        re = dot(pattern, source[:, at : at + width])
        im = dot(pattern, source[:, step + at : step + at + width])
        acc_re = jnp.zeros((parents, width), F32)
        acc_im = jnp.zeros((parents, width), F32)
        for k in range(8):
            cosine = cos_ref[pl.ds(k, 1), pl.ds(j * width, width)]
            sine = sin_ref[pl.ds(k, 1), pl.ds(j * width, width)]
            a, b = re[k * parents : (k + 1) * parents], im[k * parents : (k + 1) * parents]
            acc_re += a * cosine - b * sine
            acc_im += a * sine + b * cosine
        for h in range(width // 128):
            s = slice(h * 128, (h + 1) * 128)
            out_ref[j * (width // 128) + h, 0:parents, :] = acc_re[:, s].astype(BF16)
            out_ref[j * (width // 128) + h, parents : 2 * parents, :] = acc_im[:, s].astype(BF16)


def translate_kernel(
    upper_ref, index_ref, operator_ref, interp, out_ref, kept, sem
):
    copy = pltpu.make_async_copy(interp.at[:, pl.ds(0, KEPT * WIDTH)], kept, sem)
    copy.start()
    sources = upper_ref.shape[0] * 16
    slots, rows = operator_ref.shape[:2]
    field = jnp.concatenate(
        [
            upper_ref[:, 0:16, :].reshape(sources, 128),
            upper_ref[:, 16:32, :].reshape(sources, 128),
        ],
        axis=1,
    )
    lane = lax.broadcasted_iota(I32, (rows, sources), 1)
    acc_re = jnp.zeros((rows, 128), F32)
    acc_im = jnp.zeros((rows, 128), F32)
    for j in range(slots):
        hot = jnp.where(lane == index_ref[:, j : j + 1], 1.0, 0.0).astype(BF16)
        x = dot(hot, field)
        op = operator_ref[j].astype(F32)
        xr, xi = x[:, :128], x[:, 128:]
        tr, ti = op[:, :128], op[:, 128:]
        acc_re += tr * xr - ti * xi
        acc_im += tr * xi + ti * xr
    blocks = out_ref.shape[0]
    out_ref[:, 0:8, :] = acc_re.reshape(blocks, 8, 128).astype(BF16)
    out_ref[:, 8:16, :] = acc_im.reshape(blocks, 8, 128).astype(BF16)
    copy.wait()


def down_kernel(
    inc_ref,
    cos_ref,
    sin_ref,
    near_ref,
    kept,
    receive,
    interp,
    out_ref,
    buf,
    received,
    receive_ref,
    sems,
):
    width = WIDTH
    chunks = buf.shape[1] // width
    copies = []
    for j in range(chunks):
        copies.append(
            pltpu.make_async_copy(
                interp.at[:, pl.ds((KEPT + j) * width, width)],
                buf.at[:, pl.ds(j * width, width)],
                sems.at[j],
            )
        )
    copies.append(pltpu.make_async_copy(receive, receive_ref, sems.at[chunks]))
    for copy in copies:
        copy.start()
    leaves = received.shape[0]
    half = received.shape[1] // 2
    for s in range(inc_ref.shape[0]):
        lanes = slice(s * 128, (s + 1) * 128)
        block = inc_ref[s].astype(F32)
        re, im = block[0:8][:, None, :], block[8:16][:, None, :]
        cosine, sine = cos_ref[:, lanes][None], sin_ref[:, lanes][None]
        received[:, s * 128 : (s + 1) * 128] = (
            (re * cosine + im * sine).reshape(leaves, 128).astype(BF16)
        )
        received[:, half + s * 128 : half + (s + 1) * 128] = (
            (im * cosine - re * sine).reshape(leaves, 128).astype(BF16)
        )
    back = dot(received[:, : KEPT * width], kept[...], 1, 1)
    for j in range(chunks):
        copies[j].wait()
        at = (KEPT + j) * width
        back += dot(received[:, at : at + width], buf[:, j * width : (j + 1) * width], 1, 1)
    copies[chunks].wait()
    out_ref[...] = near_ref[...] + dot(back.astype(BF16), receive_ref[...])


def near_kernel(own_ref, sibling_ref, cross_ref, col_ref, near_hbm, _, out_ref, buf, hot, sems):
    slots = near_hbm.shape[0]
    copies = []
    for n in range(slots):
        copies.append(pltpu.make_async_copy(near_hbm.at[n], buf.at[n], sems.at[n]))
        copies[n].start()
    rows = out_ref.shape[0]
    lane = lax.broadcasted_iota(I32, (rows, 3 * rows), 1)
    for n in range(slots):
        hot[n * rows : (n + 1) * rows] = jnp.where(
            lane == col_ref[:, n : n + 1], 1.0, 0.0
        ).astype(BF16)
    sources = jnp.concatenate([own_ref[...], sibling_ref[...], cross_ref[...]], axis=0)
    picked = dot(hot[...], sources).astype(BF16)
    total = jnp.zeros(out_ref.shape, F32)
    for n in range(slots):
        copies[n].wait()
        total += dot(picked[n * rows : (n + 1) * rows], buf[n])
    out_ref[...] = total


def halo_target(i, boxes, dirs):
    b, d = divmod(i, dirs)
    z, r = divmod(d, dirs // 4)
    other = b + 1 if z >= 2 else b - 1
    if other < 0 or other >= boxes:
        return b * dirs + (3 - z) * (dirs // 4) + r
    return other * dirs + z * (dirs // 4) + (r ^ 2)


def on_device(
    boxes,
    dirs,
    currents,
    near_list,
    far_list,
    far_kind,
    aggregate,
    interp,
    receive,
    shift_angle,
    translation,
    near_matrix,
):
    leaves, width = currents.shape
    n = boxes * dirs
    me = lax.axis_index(BOTH)
    box = lax.axis_index("box")
    parents = leaves // 8 * dirs
    slots, near_slots = far_list.shape[1], near_list.shape[1]

    far_half = lax.ppermute(currents, BOTH, [(i, halo_target(i, boxes, dirs)) for i in range(n)])
    from_sibling = lax.ppermute(currents, BOTH, [(i, i ^ 1) for i in range(n)])

    place = jnp.stack([box, me]).astype(I32)
    operators, index, column, cosine, sine, held_aggregate, held = call(
        prepare_kernel,
        (
            pltpu.VMEM((slots, parents, 256), BF16),
            pltpu.VMEM((parents, 32), I32),
            pltpu.VMEM((leaves, 32), I32),
            pltpu.VMEM(shift_angle.shape, F32),
            pltpu.VMEM(shift_angle.shape, F32),
            pltpu.VMEM(aggregate.shape, BF16),
            pltpu.VMEM((interp.shape[0], 2 * EARLY * WIDTH), BF16),
        ),
        (
            place,
            *in_hbm(
                far_list.T,
                far_kind.T,
                shift_angle,
                translation.reshape(-1, translation.shape[2]),
                near_list.T,
                aggregate,
                interp,
            ),
        ),
        [whole(pltpu.SMEM)] + [whole(pltpu.HBM)] * 7,
        [
            pltpu.VMEM((slots, parents), I32),
            pltpu.VMEM((slots, parents), I32),
            pltpu.VMEM(shift_angle.shape, F32),
            pltpu.VMEM((2 * translation.shape[0], translation.shape[2]), F32),
            pltpu.VMEM((near_slots, leaves), I32),
            pltpu.VMEM((384, 256), BF16),
            pltpu.SemaphoreType.DMA((8,)),
        ],
        8,
        2 * slots * parents * 384 * 256,
        11 << 20,
    )

    up, relay = call(
        up_kernel,
        (
            pltpu.VMEM((dirs, 4 * leaves // 8, 128), BF16),
            jax.ShapeDtypeStruct(currents.shape, BF16),
        ),
        (currents, far_half, held_aggregate, cosine, sine, in_vmem(held), *in_hbm(interp)),
        [whole()] * 6 + [whole(pltpu.HBM)],
        [
            pltpu.VMEM((interp.shape[0], interp.shape[1] - 2 * EARLY * WIDTH), BF16),
            pltpu.SemaphoreType.DMA((16 - 2 * EARLY,)),
        ],
        12,
        2 * 128 * 1024 * 4608,
        10 << 20,
    )
    upper = lax.all_to_all(up, "dir", split_axis=0, concat_axis=0, tiled=True)

    cross = [(i, min(max(i + (1 if i % 2 else -1), 0), n - 1)) for i in range(n)]
    from_cross = lax.ppermute(relay, BOTH, cross)
    local, kept = call(
        translate_kernel,
        (
            pltpu.VMEM((dirs, 2 * leaves // 8, 128), BF16),
            pltpu.VMEM((interp.shape[0], KEPT * WIDTH), BF16),
        ),
        (upper, index, operators, *in_hbm(interp)),
        [whole()] * 3 + [whole(pltpu.HBM)],
        [pltpu.SemaphoreType.DMA],
        8,
        2 * slots * parents * 256 * 256,
        2 << 20,
    )
    incoming = lax.all_to_all(local, "dir", split_axis=0, concat_axis=0, tiled=True)

    near = call(
        near_kernel,
        jax.ShapeDtypeStruct((leaves, width), F32),
        (currents, from_sibling, from_cross, column, *in_hbm(near_matrix), local),
        [whole()] * 4 + [whole(pltpu.HBM), whole(pl.ANY)],
        [
            pltpu.VMEM(near_matrix.shape, BF16),
            pltpu.VMEM((near_slots * leaves, 3 * leaves), BF16),
            pltpu.SemaphoreType.DMA((near_slots,)),
        ],
        24,
        2 * leaves * 27 * 512 * 640,
        15 << 20,
    )

    return call(
        down_kernel,
        jax.ShapeDtypeStruct((leaves, width), F32),
        (incoming, cosine, sine, near, in_vmem(kept), *in_hbm(receive, interp)),
        [whole()] * 5 + [whole(pltpu.HBM)] * 2,
        [
            pltpu.VMEM((interp.shape[0], interp.shape[1] - KEPT * WIDTH), BF16),
            pltpu.VMEM((leaves, interp.shape[1]), BF16),
            pltpu.VMEM(receive.shape, BF16),
            pltpu.SemaphoreType.DMA((interp.shape[1] // WIDTH - KEPT + 1,)),
        ],
        16,
        2 * 64 * 4096 * 1536,
        10 << 20,
    )


def solution(mesh):
    placed = (
        P(BOTH, None),
        P(BOTH, None),
        P(),
        P(),
        P(),
        P(),
        P(),
        P(),
        P(None, None, "dir"),
        P(),
    )
    body = functools.partial(on_device, mesh.shape["box"], mesh.shape["dir"])
    return jax.shard_map(
        body, mesh=mesh, in_specs=placed, out_specs=P(BOTH, None), check_vma=False
    )
```

```python
import functools

import jax
import jax.numpy as jnp
from jax import lax
from jax.experimental import pallas as pl
from jax.experimental.pallas import tpu as pltpu
from jax.sharding import PartitionSpec as P

BF16, F32, I32 = jnp.bfloat16, jnp.float32, jnp.int32
BOTH = ("box", "dir")
VMEM = pltpu.VMEM
KEPT = 3


def whole(space=VMEM):
    return pl.BlockSpec(memory_space=space)


def call(body, out, args, specs, scratch, mib, flops, moved):
    return pl.pallas_call(
        body,
        out_shape=out,
        in_specs=specs,
        out_specs=jax.tree.map(lambda _: whole(), out),
        scratch_shapes=scratch,
        compiler_params=pltpu.CompilerParams(vmem_limit_bytes=mib << 20),
        cost_estimate=pl.CostEstimate(flops=flops, bytes_accessed=moved, transcendentals=0),
    )(*args)


def in_hbm(*arrays):
    return tuple(pltpu.with_memory_space_constraint(a, pltpu.HBM) for a in arrays)


def in_vmem(array):
    return pltpu.with_memory_space_constraint(array, VMEM)


def dot(a, b, ca=1, cb=0):
    return lax.dot_general(a, b, (((ca,), (cb,)), ((), ())), preferred_element_type=F32)


def prepare_kernel(
    place_ref,
    far_hbm,
    kind_hbm,
    angle_hbm,
    table_hbm,
    near_list_hbm,
    aggregate,
    interp,
    operators,
    index_ref,
    column_ref,
    cosine_ref,
    sine_ref,
    aggregate_out,
    interp_out,
    far_ref,
    kind_ref,
    angle_ref,
    table_ref,
    near_list_ref,
    table,
    sems,
):
    slots, parents = far_ref.shape
    box, me = place_ref[0], place_ref[1]
    mine = pl.ds(pl.multiple_of(box * parents, parents), parents)
    copies = [
        pltpu.make_async_copy(table_hbm, table_ref, sems.at[0]),
        pltpu.make_async_copy(far_hbm.at[:, mine], far_ref, sems.at[1]),
        pltpu.make_async_copy(kind_hbm.at[:, mine], kind_ref, sems.at[2]),
        pltpu.make_async_copy(near_list_hbm, near_list_ref, sems.at[3]),
        pltpu.make_async_copy(angle_hbm, angle_ref, sems.at[4]),
    ]
    weights = [
        pltpu.make_async_copy(aggregate, aggregate_out, sems.at[5]),
        pltpu.make_async_copy(interp, interp_out, sems.at[6]),
    ]
    for copy in copies + weights:
        copy.start()
    table[...] = jnp.zeros_like(table)
    for copy in copies:
        copy.wait()
    cosine_ref[...] = jnp.cos(angle_ref[...])
    sine_ref[...] = jnp.sin(angle_ref[...])
    kinds = table_ref.shape[0] // 2
    table[0:kinds, 0:128] = table_ref[pl.ds(0, kinds, stride=2), :].astype(BF16)
    table[0:kinds, 128:256] = table_ref[pl.ds(1, kinds, stride=2), :].astype(BF16)

    leaves = near_list_ref.shape[1]
    rel = near_list_ref[...] - me * leaves
    odd = me & 1
    below = jnp.where(odd == 0, 3 * leaves, leaves * 2)
    above = jnp.where(odd == 0, 0, leaves)
    column = jnp.where(rel < 0, rel + below, jnp.where(rel < leaves, rel, rel + above))
    column_ref[...] = jnp.pad(column, ((0, 32 - column.shape[0]), (0, 0))).T

    q = far_ref[...] - box * parents
    half = parents // 2
    g = jnp.where(q < 0, q + half, q - parents)
    own = ((q >> 3) << 4) + (q & 7)
    row = ((((g >> 3) & 3) ^ 2) << 4) + 8 + (g & 7)
    low, high = row + ((2 + (g >> 5)) << 6), row + ((g >> 5) << 6)
    index = jnp.where(q < 0, low, jnp.where(q < parents, own, high))
    index_ref[...] = jnp.pad(index, ((0, 32 - slots), (0, 0))).T
    kind = jnp.pad(kind_ref[...], ((0, 32 - slots), (0, 0))).T
    lane = lax.broadcasted_iota(I32, (parents, table.shape[0]), 1)
    for j in range(slots):
        hot = jnp.where(lane == kind[:, j : j + 1], 1.0, 0.0).astype(BF16)
        operators[j] = dot(hot, table[...]).astype(BF16)
    for copy in weights:
        copy.wait()


def up_kernel(own_ref, far_ref, agg_ref, cos_ref, sin_ref, interp, out_ref, relay_ref):
    relay_ref[...] = own_ref[...]
    width = 256
    directions = cos_ref.shape[1]
    leaves = own_ref.shape[0]
    rows = 2 * leaves
    parents = rows // 8
    r = lax.broadcasted_iota(I32, (rows, leaves), 0)
    c = lax.broadcasted_iota(I32, (rows, leaves), 1)
    leaf = 8 * (r % parents) + r // parents
    from_own = jnp.where(c == leaf, 1.0, 0.0).astype(BF16)
    from_far = jnp.where(c + leaves == leaf, 1.0, 0.0).astype(BF16)
    cur = (dot(from_own, own_ref[...]) + dot(from_far, far_ref[...])).astype(BF16)
    pattern = dot(cur, agg_ref[...]).astype(BF16)
    for j in range(directions // width):
        re = dot(pattern, interp[:, j * width : (j + 1) * width])
        im = dot(pattern, interp[:, directions + j * width : directions + (j + 1) * width])
        acc_re = jnp.zeros((parents, width), F32)
        acc_im = jnp.zeros((parents, width), F32)
        for k in range(8):
            cosine = cos_ref[pl.ds(k, 1), pl.ds(j * width, width)]
            sine = sin_ref[pl.ds(k, 1), pl.ds(j * width, width)]
            a, b = re[k * parents : (k + 1) * parents], im[k * parents : (k + 1) * parents]
            acc_re += a * cosine - b * sine
            acc_im += a * sine + b * cosine
        for h in range(width // 128):
            s = slice(h * 128, (h + 1) * 128)
            out_ref[j * (width // 128) + h, 0:parents, :] = acc_re[:, s].astype(BF16)
            out_ref[j * (width // 128) + h, parents : 2 * parents, :] = acc_im[:, s].astype(BF16)


def translate_kernel(upper_ref, index_ref, operator_ref, out_ref):
    sources = upper_ref.shape[0] * 16
    slots, rows = operator_ref.shape[:2]
    field = jnp.concatenate(
        [
            upper_ref[:, 0:16, :].reshape(sources, 128),
            upper_ref[:, 16:32, :].reshape(sources, 128),
        ],
        axis=1,
    )
    lane = lax.broadcasted_iota(I32, (rows, sources), 1)
    acc_re = jnp.zeros((rows, 128), F32)
    acc_im = jnp.zeros((rows, 128), F32)
    for j in range(slots):
        hot = jnp.where(lane == index_ref[:, j : j + 1], 1.0, 0.0).astype(BF16)
        x = dot(hot, field)
        op = operator_ref[j].astype(F32)
        xr, xi = x[:, :128], x[:, 128:]
        tr, ti = op[:, :128], op[:, 128:]
        acc_re += tr * xr - ti * xi
        acc_im += tr * xi + ti * xr
    blocks = out_ref.shape[0]
    out_ref[:, 0:8, :] = acc_re.reshape(blocks, 8, 128).astype(BF16)
    out_ref[:, 8:16, :] = acc_im.reshape(blocks, 8, 128).astype(BF16)


def down_kernel(inc_ref, cos_ref, sin_ref, near_ref, receive_ref, kept, interp, out_ref, buf, received, sems):
    width = 256
    chunks = buf.shape[1] // width
    copies = []
    for j in range(chunks):
        source = interp.at[:, pl.ds((KEPT + j) * width, width)]
        target = buf.at[:, pl.ds(j * width, width)]
        copies.append(pltpu.make_async_copy(source, target, sems.at[j]))
    for copy in copies:
        copy.start()
    leaves = received.shape[0]
    half = received.shape[1] // 2
    for s in range(inc_ref.shape[0]):
        lanes = slice(s * 128, (s + 1) * 128)
        block = inc_ref[s].astype(F32)
        re, im = block[0:8][:, None, :], block[8:16][:, None, :]
        cosine, sine = cos_ref[:, lanes][None], sin_ref[:, lanes][None]
        received[:, s * 128 : (s + 1) * 128] = (
            (re * cosine + im * sine).reshape(leaves, 128).astype(BF16)
        )
        received[:, half + s * 128 : half + (s + 1) * 128] = (
            (im * cosine - re * sine).reshape(leaves, 128).astype(BF16)
        )
    back = dot(received[:, : KEPT * width], kept[...], 1, 1)
    for j in range(chunks):
        at = (KEPT + j) * width
        copies[j].wait()
        back += dot(received[:, at : at + width], buf[:, j * width : (j + 1) * width], 1, 1)
    out_ref[...] = near_ref[...] + dot(back.astype(BF16), receive_ref[...])


def near_kernel(own_ref, sibling_ref, cross_ref, col_ref, near_hbm, _, out_ref, buf, hot, sems):
    slots = near_hbm.shape[0]
    copies = []
    for n in range(slots):
        copies.append(pltpu.make_async_copy(near_hbm.at[n], buf.at[n], sems.at[n]))
        copies[n].start()
    rows = out_ref.shape[0]
    lane = lax.broadcasted_iota(I32, (rows, 3 * rows), 1)
    for n in range(slots):
        hot[n * rows : (n + 1) * rows] = jnp.where(
            lane == col_ref[:, n : n + 1], 1.0, 0.0
        ).astype(BF16)
    sources = jnp.concatenate([own_ref[...], sibling_ref[...], cross_ref[...]], axis=0)
    picked = dot(hot[...], sources).astype(BF16)
    total = jnp.zeros(out_ref.shape, F32)
    for n in range(slots):
        copies[n].wait()
        total += dot(picked[n * rows : (n + 1) * rows], buf[n])
    out_ref[...] = total


def halo_target(i, boxes, dirs):
    b, d = divmod(i, dirs)
    z, r = divmod(d, dirs // 4)
    other = b + 1 if z >= 2 else b - 1
    if other < 0 or other >= boxes:
        return b * dirs + (3 - z) * (dirs // 4) + r
    return other * dirs + z * (dirs // 4) + (r ^ 2)


def on_device(
    boxes,
    dirs,
    currents,
    near_list,
    far_list,
    far_kind,
    aggregate,
    interp,
    receive,
    shift_angle,
    translation,
    near_matrix,
):
    leaves, width = currents.shape
    n = boxes * dirs
    me = lax.axis_index(BOTH)
    box = lax.axis_index("box")
    parents = leaves // 8 * dirs
    slots, near_slots = far_list.shape[1], near_list.shape[1]

    far_half = lax.ppermute(currents, BOTH, [(i, halo_target(i, boxes, dirs)) for i in range(n)])
    from_sibling = lax.ppermute(currents, BOTH, [(i, i ^ 1) for i in range(n)])

    place = jnp.stack([box, me]).astype(I32)
    operators, index, column, cosine, sine, held_aggregate, held = call(
        prepare_kernel,
        (
            pltpu.VMEM((slots, parents, 256), BF16),
            pltpu.VMEM((parents, 32), I32),
            pltpu.VMEM((leaves, 32), I32),
            pltpu.VMEM(shift_angle.shape, F32),
            pltpu.VMEM(shift_angle.shape, F32),
            pltpu.VMEM(aggregate.shape, BF16),
            pltpu.VMEM(interp.shape, BF16),
        ),
        (
            place,
            *in_hbm(
                far_list.T,
                far_kind.T,
                shift_angle,
                translation.reshape(-1, translation.shape[2]),
                near_list.T,
                aggregate,
                interp,
            ),
        ),
        [whole(pltpu.SMEM)] + [whole(pltpu.HBM)] * 7,
        [
            pltpu.VMEM((slots, parents), I32),
            pltpu.VMEM((slots, parents), I32),
            pltpu.VMEM(shift_angle.shape, F32),
            pltpu.VMEM((2 * translation.shape[0], translation.shape[2]), F32),
            pltpu.VMEM((near_slots, leaves), I32),
            pltpu.VMEM((384, 256), BF16),
            pltpu.SemaphoreType.DMA((7,)),
        ],
        8,
        2 * slots * parents * 384 * 256,
        11 << 20,
    )

    up, relay = call(
        up_kernel,
        (
            jax.ShapeDtypeStruct((dirs, 4 * leaves // 8, 128), BF16),
            jax.ShapeDtypeStruct(currents.shape, BF16),
        ),
        (currents, far_half, held_aggregate, cosine, sine, in_vmem(held)),
        [whole()] * 6,
        [],
        8,
        2 * 128 * 1024 * 4608,
        10 << 20,
    )
    upper = lax.all_to_all(up, "dir", split_axis=0, concat_axis=0, tiled=True)

    cross = [(i, min(max(i + (1 if i % 2 else -1), 0), n - 1)) for i in range(n)]
    from_cross = lax.ppermute(relay, BOTH, cross)
    local = call(
        translate_kernel,
        jax.ShapeDtypeStruct((dirs, 2 * leaves // 8, 128), BF16),
        (upper, index, operators),
        [whole()] * 3,
        [],
        8,
        2 * slots * parents * 256 * 256,
        2 << 20,
    )
    incoming = lax.all_to_all(local, "dir", split_axis=0, concat_axis=0, tiled=True)

    near = call(
        near_kernel,
        jax.ShapeDtypeStruct((leaves, width), F32),
        (currents, from_sibling, from_cross, column, *in_hbm(near_matrix), local),
        [whole()] * 4 + [whole(pltpu.HBM), whole(pl.ANY)],
        [
            pltpu.VMEM(near_matrix.shape, BF16),
            pltpu.VMEM((near_slots * leaves, 3 * leaves), BF16),
            pltpu.SemaphoreType.DMA((near_slots,)),
        ],
        24,
        2 * leaves * 27 * 512 * 640,
        15 << 20,
    )

    return call(
        down_kernel,
        jax.ShapeDtypeStruct((leaves, width), F32),
        (incoming, cosine, sine, near, in_vmem(receive), in_vmem(interp[:, : KEPT * 256]), *in_hbm(interp)),
        [whole()] * 6 + [whole(pltpu.HBM)],
        [
            pltpu.VMEM((interp.shape[0], interp.shape[1] - KEPT * 256), BF16),
            pltpu.VMEM((leaves, interp.shape[1]), BF16),
            pltpu.SemaphoreType.DMA((interp.shape[1] // 256,)),
        ],
        16,
        2 * 64 * 4096 * 1536,
        10 << 20,
    )


def solution(mesh):
    placed = (
        P(BOTH, None),
        P(BOTH, None),
        P(),
        P(),
        P(),
        P(),
        P(),
        P(),
        P(None, None, "dir"),
        P(),
    )
    body = functools.partial(on_device, mesh.shape["box"], mesh.shape["dir"])
    return jax.shard_map(
        body, mesh=mesh, in_specs=placed, out_specs=P(BOTH, None), check_vma=False
    )
```

```python
import functools

import jax
import jax.numpy as jnp
from jax import lax
from jax.experimental import pallas as pl
from jax.experimental.pallas import tpu as pltpu
from jax.sharding import PartitionSpec as P

BF16, F32, I32 = jnp.bfloat16, jnp.float32, jnp.int32
BOTH = ("box", "dir")
VMEM = pltpu.VMEM
AHEAD = 5 * 10**9


def whole(space=VMEM):
    return pl.BlockSpec(memory_space=space)


def call(body, out, args, specs, scratch, mib, flops, moved):
    return pl.pallas_call(
        body,
        out_shape=out,
        in_specs=specs,
        out_specs=jax.tree.map(lambda _: whole(), out),
        scratch_shapes=scratch,
        compiler_params=pltpu.CompilerParams(vmem_limit_bytes=mib << 20),
        cost_estimate=pl.CostEstimate(flops=flops, bytes_accessed=moved, transcendentals=0),
    )(*args)


def in_hbm(*arrays):
    return tuple(pltpu.with_memory_space_constraint(a, pltpu.HBM) for a in arrays)


def in_vmem(array):
    return pltpu.with_memory_space_constraint(array, VMEM)


def dot(a, b, ca=1, cb=0):
    return lax.dot_general(a, b, (((ca,), (cb,)), ((), ())), preferred_element_type=F32)


def prepare_kernel(
    place_ref,
    far_hbm,
    kind_hbm,
    angle_hbm,
    table_hbm,
    near_list_hbm,
    operators,
    index_ref,
    column_ref,
    cosine_ref,
    sine_ref,
    far_ref,
    kind_ref,
    angle_ref,
    table_ref,
    near_list_ref,
    table,
    sems,
):
    slots, parents = far_ref.shape
    box, me = place_ref[0], place_ref[1]
    mine = pl.ds(pl.multiple_of(box * parents, parents), parents)
    copies = [
        pltpu.make_async_copy(table_hbm, table_ref, sems.at[0]),
        pltpu.make_async_copy(far_hbm.at[:, mine], far_ref, sems.at[1]),
        pltpu.make_async_copy(kind_hbm.at[:, mine], kind_ref, sems.at[2]),
        pltpu.make_async_copy(near_list_hbm, near_list_ref, sems.at[3]),
        pltpu.make_async_copy(angle_hbm, angle_ref, sems.at[4]),
    ]
    for copy in copies:
        copy.start()
    table[...] = jnp.zeros_like(table)
    for copy in copies:
        copy.wait()
    cosine_ref[...] = jnp.cos(angle_ref[...])
    sine_ref[...] = jnp.sin(angle_ref[...])
    kinds = table_ref.shape[0] // 2
    table[0:kinds, 0:128] = table_ref[pl.ds(0, kinds, stride=2), :].astype(BF16)
    table[0:kinds, 128:256] = table_ref[pl.ds(1, kinds, stride=2), :].astype(BF16)

    leaves = near_list_ref.shape[1]
    rel = near_list_ref[...] - me * leaves
    odd = me & 1
    below = jnp.where(odd == 0, 3 * leaves, leaves * 2)
    above = jnp.where(odd == 0, 0, leaves)
    column = jnp.where(rel < 0, rel + below, jnp.where(rel < leaves, rel, rel + above))
    column_ref[...] = jnp.pad(column, ((0, 32 - column.shape[0]), (0, 0))).T

    q = far_ref[...] - box * parents
    half = parents // 2
    g = jnp.where(q < 0, q + half, q - parents)
    own = ((q >> 3) << 4) + (q & 7)
    row = ((((g >> 3) & 3) ^ 2) << 4) + 8 + (g & 7)
    low, high = row + ((2 + (g >> 5)) << 6), row + ((g >> 5) << 6)
    index = jnp.where(q < 0, low, jnp.where(q < parents, own, high))
    index_ref[...] = jnp.pad(index, ((0, 32 - slots), (0, 0))).T
    kind = jnp.pad(kind_ref[...], ((0, 32 - slots), (0, 0))).T
    lane = lax.broadcasted_iota(I32, (parents, table.shape[0]), 1)
    for j in range(slots):
        hot = jnp.where(lane == kind[:, j : j + 1], 1.0, 0.0).astype(BF16)
        operators[j] = dot(hot, table[...]).astype(BF16)


def up_kernel(own_ref, far_ref, agg_ref, cos_ref, sin_ref, interp, out_ref, relay_ref):
    relay_ref[...] = own_ref[...]
    width = 256
    directions = cos_ref.shape[1]
    leaves = own_ref.shape[0]
    rows = 2 * leaves
    parents = rows // 8
    r = lax.broadcasted_iota(I32, (rows, leaves), 0)
    c = lax.broadcasted_iota(I32, (rows, leaves), 1)
    leaf = 8 * (r % parents) + r // parents
    from_own = jnp.where(c == leaf, 1.0, 0.0).astype(BF16)
    from_far = jnp.where(c + leaves == leaf, 1.0, 0.0).astype(BF16)
    cur = (dot(from_own, own_ref[...]) + dot(from_far, far_ref[...])).astype(BF16)
    pattern = dot(cur, agg_ref[...]).astype(BF16)
    for j in range(directions // width):
        re = dot(pattern, interp[:, j * width : (j + 1) * width])
        im = dot(pattern, interp[:, directions + j * width : directions + (j + 1) * width])
        acc_re = jnp.zeros((parents, width), F32)
        acc_im = jnp.zeros((parents, width), F32)
        for k in range(8):
            cosine = cos_ref[pl.ds(k, 1), pl.ds(j * width, width)]
            sine = sin_ref[pl.ds(k, 1), pl.ds(j * width, width)]
            a, b = re[k * parents : (k + 1) * parents], im[k * parents : (k + 1) * parents]
            acc_re += a * cosine - b * sine
            acc_im += a * sine + b * cosine
        for h in range(width // 128):
            s = slice(h * 128, (h + 1) * 128)
            out_ref[j * (width // 128) + h, 0:parents, :] = acc_re[:, s].astype(BF16)
            out_ref[j * (width // 128) + h, parents : 2 * parents, :] = acc_im[:, s].astype(BF16)


def translate_kernel(upper_ref, index_ref, operator_ref, out_ref):
    sources = upper_ref.shape[0] * 16
    slots, rows = operator_ref.shape[:2]
    field = jnp.concatenate(
        [
            upper_ref[:, 0:16, :].reshape(sources, 128),
            upper_ref[:, 16:32, :].reshape(sources, 128),
        ],
        axis=1,
    )
    lane = lax.broadcasted_iota(I32, (rows, sources), 1)
    acc_re = jnp.zeros((rows, 128), F32)
    acc_im = jnp.zeros((rows, 128), F32)
    for j in range(slots):
        hot = jnp.where(lane == index_ref[:, j : j + 1], 1.0, 0.0).astype(BF16)
        x = dot(hot, field)
        op = operator_ref[j].astype(F32)
        xr, xi = x[:, :128], x[:, 128:]
        tr, ti = op[:, :128], op[:, 128:]
        acc_re += tr * xr - ti * xi
        acc_im += tr * xi + ti * xr
    blocks = out_ref.shape[0]
    out_ref[:, 0:8, :] = acc_re.reshape(blocks, 8, 128).astype(BF16)
    out_ref[:, 8:16, :] = acc_im.reshape(blocks, 8, 128).astype(BF16)


def down_kernel(inc_ref, cos_ref, sin_ref, near_ref, receive_ref, interp, out_ref, buf, received, sems):
    width = 256
    chunks = buf.shape[1] // width
    copies = []
    for j in range(chunks):
        lanes = pl.ds(j * width, width)
        copies.append(pltpu.make_async_copy(interp.at[:, lanes], buf.at[:, lanes], sems.at[j]))
    for copy in copies:
        copy.start()
    leaves = received.shape[0]
    half = received.shape[1] // 2
    for s in range(inc_ref.shape[0]):
        lanes = slice(s * 128, (s + 1) * 128)
        block = inc_ref[s].astype(F32)
        re, im = block[0:8][:, None, :], block[8:16][:, None, :]
        cosine, sine = cos_ref[:, lanes][None], sin_ref[:, lanes][None]
        received[:, s * 128 : (s + 1) * 128] = (
            (re * cosine + im * sine).reshape(leaves, 128).astype(BF16)
        )
        received[:, half + s * 128 : half + (s + 1) * 128] = (
            (im * cosine - re * sine).reshape(leaves, 128).astype(BF16)
        )
    back = jnp.zeros((leaves, buf.shape[0]), F32)
    for j in range(chunks):
        lanes = slice(j * width, (j + 1) * width)
        copies[j].wait()
        back += dot(received[:, lanes], buf[:, lanes], 1, 1)
    out_ref[...] = near_ref[...] + dot(back.astype(BF16), receive_ref[...])


def near_kernel(own_ref, sibling_ref, cross_ref, col_ref, near_hbm, _, out_ref, buf, hot, sems):
    slots = near_hbm.shape[0]
    copies = []
    for n in range(slots):
        copies.append(pltpu.make_async_copy(near_hbm.at[n], buf.at[n], sems.at[n]))
        copies[n].start()
    rows = out_ref.shape[0]
    lane = lax.broadcasted_iota(I32, (rows, 3 * rows), 1)
    for n in range(slots):
        hot[n * rows : (n + 1) * rows] = jnp.where(
            lane == col_ref[:, n : n + 1], 1.0, 0.0
        ).astype(BF16)
    sources = jnp.concatenate([own_ref[...], sibling_ref[...], cross_ref[...]], axis=0)
    picked = dot(hot[...], sources).astype(BF16)
    total = jnp.zeros(out_ref.shape, F32)
    for n in range(slots):
        copies[n].wait()
        total += dot(picked[n * rows : (n + 1) * rows], buf[n])
    out_ref[...] = total


def halo_target(i, boxes, dirs):
    b, d = divmod(i, dirs)
    z, r = divmod(d, dirs // 4)
    other = b + 1 if z >= 2 else b - 1
    if other < 0 or other >= boxes:
        return b * dirs + (3 - z) * (dirs // 4) + r
    return other * dirs + z * (dirs // 4) + (r ^ 2)


def on_device(
    boxes,
    dirs,
    currents,
    near_list,
    far_list,
    far_kind,
    aggregate,
    interp,
    receive,
    shift_angle,
    translation,
    near_matrix,
):
    leaves, width = currents.shape
    n = boxes * dirs
    me = lax.axis_index(BOTH)
    box = lax.axis_index("box")
    parents = leaves // 8 * dirs
    slots, near_slots = far_list.shape[1], near_list.shape[1]

    far_half = lax.ppermute(currents, BOTH, [(i, halo_target(i, boxes, dirs)) for i in range(n)])
    from_sibling = lax.ppermute(currents, BOTH, [(i, i ^ 1) for i in range(n)])

    place = jnp.stack([box, me]).astype(I32)
    operators, index, column, cosine, sine = call(
        prepare_kernel,
        (
            pltpu.VMEM((slots, parents, 256), BF16),
            pltpu.VMEM((parents, 32), I32),
            pltpu.VMEM((leaves, 32), I32),
            pltpu.VMEM(shift_angle.shape, F32),
            pltpu.VMEM(shift_angle.shape, F32),
        ),
        (
            place,
            *in_hbm(
                far_list.T,
                far_kind.T,
                shift_angle,
                translation.reshape(-1, translation.shape[2]),
                near_list.T,
            ),
        ),
        [whole(pltpu.SMEM)] + [whole(pltpu.HBM)] * 5,
        [
            pltpu.VMEM((slots, parents), I32),
            pltpu.VMEM((slots, parents), I32),
            pltpu.VMEM(shift_angle.shape, F32),
            pltpu.VMEM((2 * translation.shape[0], translation.shape[2]), F32),
            pltpu.VMEM((near_slots, leaves), I32),
            pltpu.VMEM((384, 256), BF16),
            pltpu.SemaphoreType.DMA((5,)),
        ],
        8,
        AHEAD,
        11 << 20,
    )

    up, relay = call(
        up_kernel,
        (
            jax.ShapeDtypeStruct((dirs, 4 * leaves // 8, 128), BF16),
            jax.ShapeDtypeStruct(currents.shape, BF16),
        ),
        (currents, far_half, in_vmem(aggregate), cosine, sine, in_vmem(interp)),
        [whole()] * 6,
        [],
        8,
        2 * 128 * 1024 * 4608,
        10 << 20,
    )
    upper = lax.all_to_all(up, "dir", split_axis=0, concat_axis=0, tiled=True)

    cross = [(i, min(max(i + (1 if i % 2 else -1), 0), n - 1)) for i in range(n)]
    from_cross = lax.ppermute(relay, BOTH, cross)
    local = call(
        translate_kernel,
        jax.ShapeDtypeStruct((dirs, 2 * leaves // 8, 128), BF16),
        (upper, index, operators),
        [whole()] * 3,
        [],
        8,
        2 * slots * parents * 256 * 256,
        2 << 20,
    )
    incoming = lax.all_to_all(local, "dir", split_axis=0, concat_axis=0, tiled=True)

    near = call(
        near_kernel,
        jax.ShapeDtypeStruct((leaves, width), F32),
        (currents, from_sibling, from_cross, column, *in_hbm(near_matrix), local),
        [whole()] * 4 + [whole(pltpu.HBM), whole(pl.ANY)],
        [
            pltpu.VMEM(near_matrix.shape, BF16),
            pltpu.VMEM((near_slots * leaves, 3 * leaves), BF16),
            pltpu.SemaphoreType.DMA((near_slots,)),
        ],
        24,
        2 * leaves * 27 * 512 * 640,
        15 << 20,
    )

    return call(
        down_kernel,
        jax.ShapeDtypeStruct((leaves, width), F32),
        (incoming, cosine, sine, near, in_vmem(receive), *in_hbm(interp)),
        [whole()] * 5 + [whole(pltpu.HBM)],
        [
            pltpu.VMEM(interp.shape, BF16),
            pltpu.VMEM((leaves, interp.shape[1]), BF16),
            pltpu.SemaphoreType.DMA((interp.shape[1] // 256,)),
        ],
        16,
        2 * 64 * 4096 * 1536,
        10 << 20,
    )


def solution(mesh):
    placed = (
        P(BOTH, None),
        P(BOTH, None),
        P(),
        P(),
        P(),
        P(),
        P(),
        P(),
        P(None, None, "dir"),
        P(),
    )
    body = functools.partial(on_device, mesh.shape["box"], mesh.shape["dir"])
    return jax.shard_map(
        body, mesh=mesh, in_specs=placed, out_specs=P(BOTH, None), check_vma=False
    )
```

```python
import functools

import jax
import jax.numpy as jnp
from jax import lax
from jax.experimental import pallas as pl
from jax.experimental.pallas import tpu as pltpu
from jax.sharding import PartitionSpec as P

BF16, F32, I32 = jnp.bfloat16, jnp.float32, jnp.int32
BOTH = ("box", "dir")
VMEM = pltpu.VMEM
KEPT = 3
AHEAD = 5 * 10**9


def whole(space=VMEM):
    return pl.BlockSpec(memory_space=space)


def call(body, out, args, specs, scratch, mib, flops, moved):
    return pl.pallas_call(
        body,
        out_shape=out,
        in_specs=specs,
        out_specs=jax.tree.map(lambda _: whole(), out),
        scratch_shapes=scratch,
        compiler_params=pltpu.CompilerParams(vmem_limit_bytes=mib << 20),
        cost_estimate=pl.CostEstimate(flops=flops, bytes_accessed=moved, transcendentals=0),
    )(*args)


def in_hbm(*arrays):
    return tuple(pltpu.with_memory_space_constraint(a, pltpu.HBM) for a in arrays)


def in_vmem(array):
    return pltpu.with_memory_space_constraint(array, VMEM)


def dot(a, b, ca=1, cb=0):
    return lax.dot_general(a, b, (((ca,), (cb,)), ((), ())), preferred_element_type=F32)


def prepare_kernel(
    place_ref,
    far_hbm,
    kind_hbm,
    angle_hbm,
    table_hbm,
    near_list_hbm,
    operators,
    index_ref,
    column_ref,
    cosine_ref,
    sine_ref,
    far_ref,
    kind_ref,
    angle_ref,
    table_ref,
    near_list_ref,
    table,
    sems,
):
    slots, parents = far_ref.shape
    box, me = place_ref[0], place_ref[1]
    mine = pl.ds(pl.multiple_of(box * parents, parents), parents)
    copies = [
        pltpu.make_async_copy(table_hbm, table_ref, sems.at[0]),
        pltpu.make_async_copy(far_hbm.at[:, mine], far_ref, sems.at[1]),
        pltpu.make_async_copy(kind_hbm.at[:, mine], kind_ref, sems.at[2]),
        pltpu.make_async_copy(near_list_hbm, near_list_ref, sems.at[3]),
        pltpu.make_async_copy(angle_hbm, angle_ref, sems.at[4]),
    ]
    for copy in copies:
        copy.start()
    table[...] = jnp.zeros_like(table)
    for copy in copies:
        copy.wait()
    cosine_ref[...] = jnp.cos(angle_ref[...])
    sine_ref[...] = jnp.sin(angle_ref[...])
    kinds = table_ref.shape[0] // 2
    table[0:kinds, 0:128] = table_ref[pl.ds(0, kinds, stride=2), :].astype(BF16)
    table[0:kinds, 128:256] = table_ref[pl.ds(1, kinds, stride=2), :].astype(BF16)

    leaves = near_list_ref.shape[1]
    rel = near_list_ref[...] - me * leaves
    odd = me & 1
    below = jnp.where(odd == 0, 3 * leaves, leaves * 2)
    above = jnp.where(odd == 0, 0, leaves)
    column = jnp.where(rel < 0, rel + below, jnp.where(rel < leaves, rel, rel + above))
    column_ref[...] = jnp.pad(column, ((0, 32 - column.shape[0]), (0, 0))).T

    q = far_ref[...] - box * parents
    half = parents // 2
    g = jnp.where(q < 0, q + half, q - parents)
    own = ((q >> 3) << 4) + (q & 7)
    row = ((((g >> 3) & 3) ^ 2) << 4) + 8 + (g & 7)
    low, high = row + ((2 + (g >> 5)) << 6), row + ((g >> 5) << 6)
    index = jnp.where(q < 0, low, jnp.where(q < parents, own, high))
    index_ref[...] = jnp.pad(index, ((0, 32 - slots), (0, 0))).T
    kind = jnp.pad(kind_ref[...], ((0, 32 - slots), (0, 0))).T
    lane = lax.broadcasted_iota(I32, (parents, table.shape[0]), 1)
    for j in range(slots):
        hot = jnp.where(lane == kind[:, j : j + 1], 1.0, 0.0).astype(BF16)
        operators[j] = dot(hot, table[...]).astype(BF16)


def up_kernel(
    own_ref, far_ref, agg_ref, cos_ref, sin_ref, interp, out_ref, relay_ref, kept, sem
):
    copy = pltpu.make_async_copy(interp.at[:, pl.ds(0, KEPT * 256)], kept, sem)
    copy.start()
    relay_ref[...] = own_ref[...]
    width = 256
    directions = cos_ref.shape[1]
    leaves = own_ref.shape[0]
    rows = 2 * leaves
    parents = rows // 8
    r = lax.broadcasted_iota(I32, (rows, leaves), 0)
    c = lax.broadcasted_iota(I32, (rows, leaves), 1)
    leaf = 8 * (r % parents) + r // parents
    from_own = jnp.where(c == leaf, 1.0, 0.0).astype(BF16)
    from_far = jnp.where(c + leaves == leaf, 1.0, 0.0).astype(BF16)
    cur = (dot(from_own, own_ref[...]) + dot(from_far, far_ref[...])).astype(BF16)
    pattern = dot(cur, agg_ref[...]).astype(BF16)
    for j in range(directions // width):
        re = dot(pattern, interp[:, j * width : (j + 1) * width])
        im = dot(pattern, interp[:, directions + j * width : directions + (j + 1) * width])
        acc_re = jnp.zeros((parents, width), F32)
        acc_im = jnp.zeros((parents, width), F32)
        for k in range(8):
            cosine = cos_ref[pl.ds(k, 1), pl.ds(j * width, width)]
            sine = sin_ref[pl.ds(k, 1), pl.ds(j * width, width)]
            a, b = re[k * parents : (k + 1) * parents], im[k * parents : (k + 1) * parents]
            acc_re += a * cosine - b * sine
            acc_im += a * sine + b * cosine
        for h in range(width // 128):
            s = slice(h * 128, (h + 1) * 128)
            out_ref[j * (width // 128) + h, 0:parents, :] = acc_re[:, s].astype(BF16)
            out_ref[j * (width // 128) + h, parents : 2 * parents, :] = acc_im[:, s].astype(BF16)
    copy.wait()


def translate_kernel(upper_ref, index_ref, operator_ref, out_ref):
    sources = upper_ref.shape[0] * 16
    slots, rows = operator_ref.shape[:2]
    field = jnp.concatenate(
        [
            upper_ref[:, 0:16, :].reshape(sources, 128),
            upper_ref[:, 16:32, :].reshape(sources, 128),
        ],
        axis=1,
    )
    lane = lax.broadcasted_iota(I32, (rows, sources), 1)
    acc_re = jnp.zeros((rows, 128), F32)
    acc_im = jnp.zeros((rows, 128), F32)
    for j in range(slots):
        hot = jnp.where(lane == index_ref[:, j : j + 1], 1.0, 0.0).astype(BF16)
        x = dot(hot, field)
        op = operator_ref[j].astype(F32)
        xr, xi = x[:, :128], x[:, 128:]
        tr, ti = op[:, :128], op[:, 128:]
        acc_re += tr * xr - ti * xi
        acc_im += tr * xi + ti * xr
    blocks = out_ref.shape[0]
    out_ref[:, 0:8, :] = acc_re.reshape(blocks, 8, 128).astype(BF16)
    out_ref[:, 8:16, :] = acc_im.reshape(blocks, 8, 128).astype(BF16)


def down_kernel(inc_ref, cos_ref, sin_ref, near_ref, receive_ref, kept, interp, out_ref, buf, received, sems):
    width = 256
    chunks = buf.shape[1] // width
    copies = []
    for j in range(chunks):
        source = interp.at[:, pl.ds((KEPT + j) * width, width)]
        target = buf.at[:, pl.ds(j * width, width)]
        copies.append(pltpu.make_async_copy(source, target, sems.at[j]))
    for copy in copies:
        copy.start()
    leaves = received.shape[0]
    half = received.shape[1] // 2
    for s in range(inc_ref.shape[0]):
        lanes = slice(s * 128, (s + 1) * 128)
        block = inc_ref[s].astype(F32)
        re, im = block[0:8][:, None, :], block[8:16][:, None, :]
        cosine, sine = cos_ref[:, lanes][None], sin_ref[:, lanes][None]
        received[:, s * 128 : (s + 1) * 128] = (
            (re * cosine + im * sine).reshape(leaves, 128).astype(BF16)
        )
        received[:, half + s * 128 : half + (s + 1) * 128] = (
            (im * cosine - re * sine).reshape(leaves, 128).astype(BF16)
        )
    back = dot(received[:, : KEPT * width], kept[...], 1, 1)
    for j in range(chunks):
        at = (KEPT + j) * width
        copies[j].wait()
        back += dot(received[:, at : at + width], buf[:, j * width : (j + 1) * width], 1, 1)
    out_ref[...] = near_ref[...] + dot(back.astype(BF16), receive_ref[...])


def near_kernel(own_ref, sibling_ref, cross_ref, col_ref, near_hbm, _, out_ref, buf, hot, sems):
    slots = near_hbm.shape[0]
    copies = []
    for n in range(slots):
        copies.append(pltpu.make_async_copy(near_hbm.at[n], buf.at[n], sems.at[n]))
        copies[n].start()
    rows = out_ref.shape[0]
    lane = lax.broadcasted_iota(I32, (rows, 3 * rows), 1)
    for n in range(slots):
        hot[n * rows : (n + 1) * rows] = jnp.where(
            lane == col_ref[:, n : n + 1], 1.0, 0.0
        ).astype(BF16)
    sources = jnp.concatenate([own_ref[...], sibling_ref[...], cross_ref[...]], axis=0)
    picked = dot(hot[...], sources).astype(BF16)
    total = jnp.zeros(out_ref.shape, F32)
    for n in range(slots):
        copies[n].wait()
        total += dot(picked[n * rows : (n + 1) * rows], buf[n])
    out_ref[...] = total


def halo_target(i, boxes, dirs):
    b, d = divmod(i, dirs)
    z, r = divmod(d, dirs // 4)
    other = b + 1 if z >= 2 else b - 1
    if other < 0 or other >= boxes:
        return b * dirs + (3 - z) * (dirs // 4) + r
    return other * dirs + z * (dirs // 4) + (r ^ 2)


def on_device(
    boxes,
    dirs,
    currents,
    near_list,
    far_list,
    far_kind,
    aggregate,
    interp,
    receive,
    shift_angle,
    translation,
    near_matrix,
):
    leaves, width = currents.shape
    n = boxes * dirs
    me = lax.axis_index(BOTH)
    box = lax.axis_index("box")
    parents = leaves // 8 * dirs
    slots, near_slots = far_list.shape[1], near_list.shape[1]

    far_half = lax.ppermute(currents, BOTH, [(i, halo_target(i, boxes, dirs)) for i in range(n)])
    from_sibling = lax.ppermute(currents, BOTH, [(i, i ^ 1) for i in range(n)])

    place = jnp.stack([box, me]).astype(I32)
    operators, index, column, cosine, sine = call(
        prepare_kernel,
        (
            pltpu.VMEM((slots, parents, 256), BF16),
            pltpu.VMEM((parents, 32), I32),
            pltpu.VMEM((leaves, 32), I32),
            pltpu.VMEM(shift_angle.shape, F32),
            pltpu.VMEM(shift_angle.shape, F32),
        ),
        (
            place,
            *in_hbm(
                far_list.T,
                far_kind.T,
                shift_angle,
                translation.reshape(-1, translation.shape[2]),
                near_list.T,
            ),
        ),
        [whole(pltpu.SMEM)] + [whole(pltpu.HBM)] * 5,
        [
            pltpu.VMEM((slots, parents), I32),
            pltpu.VMEM((slots, parents), I32),
            pltpu.VMEM(shift_angle.shape, F32),
            pltpu.VMEM((2 * translation.shape[0], translation.shape[2]), F32),
            pltpu.VMEM((near_slots, leaves), I32),
            pltpu.VMEM((384, 256), BF16),
            pltpu.SemaphoreType.DMA((5,)),
        ],
        8,
        AHEAD,
        11 << 20,
    )

    up, relay, kept = call(
        up_kernel,
        (
            jax.ShapeDtypeStruct((dirs, 4 * leaves // 8, 128), BF16),
            jax.ShapeDtypeStruct(currents.shape, BF16),
            pltpu.VMEM((interp.shape[0], KEPT * 256), BF16),
        ),
        (currents, far_half, in_vmem(aggregate), cosine, sine, in_vmem(interp)),
        [whole()] * 6,
        [pltpu.SemaphoreType.DMA],
        8,
        2 * 128 * 1024 * 4608,
        10 << 20,
    )
    upper = lax.all_to_all(up, "dir", split_axis=0, concat_axis=0, tiled=True)

    cross = [(i, min(max(i + (1 if i % 2 else -1), 0), n - 1)) for i in range(n)]
    from_cross = lax.ppermute(relay, BOTH, cross)
    local = call(
        translate_kernel,
        jax.ShapeDtypeStruct((dirs, 2 * leaves // 8, 128), BF16),
        (upper, index, operators),
        [whole()] * 3,
        [],
        8,
        2 * slots * parents * 256 * 256,
        2 << 20,
    )
    incoming = lax.all_to_all(local, "dir", split_axis=0, concat_axis=0, tiled=True)

    near = call(
        near_kernel,
        jax.ShapeDtypeStruct((leaves, width), F32),
        (currents, from_sibling, from_cross, column, *in_hbm(near_matrix), local),
        [whole()] * 4 + [whole(pltpu.HBM), whole(pl.ANY)],
        [
            pltpu.VMEM(near_matrix.shape, BF16),
            pltpu.VMEM((near_slots * leaves, 3 * leaves), BF16),
            pltpu.SemaphoreType.DMA((near_slots,)),
        ],
        24,
        2 * leaves * 27 * 512 * 640,
        15 << 20,
    )

    return call(
        down_kernel,
        jax.ShapeDtypeStruct((leaves, width), F32),
        (incoming, cosine, sine, near, in_vmem(receive), in_vmem(kept), *in_hbm(interp)),
        [whole()] * 6 + [whole(pltpu.HBM)],
        [
            pltpu.VMEM((interp.shape[0], interp.shape[1] - KEPT * 256), BF16),
            pltpu.VMEM((leaves, interp.shape[1]), BF16),
            pltpu.SemaphoreType.DMA((interp.shape[1] // 256,)),
        ],
        16,
        2 * 64 * 4096 * 1536,
        10 << 20,
    )


def solution(mesh):
    placed = (
        P(BOTH, None),
        P(BOTH, None),
        P(),
        P(),
        P(),
        P(),
        P(),
        P(),
        P(None, None, "dir"),
        P(),
    )
    body = functools.partial(on_device, mesh.shape["box"], mesh.shape["dir"])
    return jax.shard_map(
        body, mesh=mesh, in_specs=placed, out_specs=P(BOTH, None), check_vma=False
    )
```

```python
import functools

import jax
import jax.numpy as jnp
from jax import lax
from jax.experimental import pallas as pl
from jax.experimental.pallas import tpu as pltpu
from jax.sharding import PartitionSpec as P

BF16, F32, I32 = jnp.bfloat16, jnp.float32, jnp.int32
BOTH = ("box", "dir")
VMEM = pltpu.VMEM
KEPT = 3
AHEAD = 5 * 10**9


def whole(space=VMEM):
    return pl.BlockSpec(memory_space=space)


def call(body, out, args, specs, scratch, mib, flops, moved):
    return pl.pallas_call(
        body,
        out_shape=out,
        in_specs=specs,
        out_specs=jax.tree.map(lambda _: whole(), out),
        scratch_shapes=scratch,
        compiler_params=pltpu.CompilerParams(vmem_limit_bytes=mib << 20),
        cost_estimate=pl.CostEstimate(flops=flops, bytes_accessed=moved, transcendentals=0),
    )(*args)


def in_hbm(*arrays):
    return tuple(pltpu.with_memory_space_constraint(a, pltpu.HBM) for a in arrays)


def in_vmem(array):
    return pltpu.with_memory_space_constraint(array, VMEM)


def dot(a, b, ca=1, cb=0):
    return lax.dot_general(a, b, (((ca,), (cb,)), ((), ())), preferred_element_type=F32)


def prepare_kernel(
    place_ref,
    far_hbm,
    kind_hbm,
    angle_hbm,
    table_hbm,
    near_list_hbm,
    operators,
    index_ref,
    column_ref,
    cosine_ref,
    sine_ref,
    far_ref,
    kind_ref,
    angle_ref,
    table_ref,
    near_list_ref,
    table,
    sems,
):
    slots, parents = far_ref.shape
    box, me = place_ref[0], place_ref[1]
    mine = pl.ds(pl.multiple_of(box * parents, parents), parents)
    copies = [
        pltpu.make_async_copy(
            table_hbm, table_ref.at[pl.ds(0, table_hbm.shape[0])], sems.at[0]
        ),
        pltpu.make_async_copy(far_hbm.at[:, mine], far_ref, sems.at[1]),
        pltpu.make_async_copy(kind_hbm.at[:, mine], kind_ref, sems.at[2]),
        pltpu.make_async_copy(near_list_hbm, near_list_ref, sems.at[3]),
        pltpu.make_async_copy(angle_hbm, angle_ref, sems.at[4]),
    ]
    for copy in copies:
        copy.start()
    used = table_hbm.shape[0]
    table_ref[used:, :] = jnp.zeros((table_ref.shape[0] - used, table_ref.shape[1]), F32)
    for copy in copies:
        copy.wait()
    cosine_ref[...] = jnp.cos(angle_ref[...])
    sine_ref[...] = jnp.sin(angle_ref[...])
    kinds = table_ref.shape[0] // 2
    table[0:kinds, 0:128] = table_ref[pl.ds(0, kinds, stride=2), :].astype(BF16)
    table[0:kinds, 128:256] = table_ref[pl.ds(1, kinds, stride=2), :].astype(BF16)
    table[kinds:, :] = jnp.zeros((table.shape[0] - kinds, table.shape[1]), BF16)

    leaves = near_list_ref.shape[1]
    rel = near_list_ref[...] - me * leaves
    odd = me & 1
    below = jnp.where(odd == 0, 3 * leaves, leaves * 2)
    above = jnp.where(odd == 0, 0, leaves)
    column = jnp.where(rel < 0, rel + below, jnp.where(rel < leaves, rel, rel + above))
    column_ref[...] = jnp.pad(column, ((0, 32 - column.shape[0]), (0, 0))).T

    q = far_ref[...] - box * parents
    half = parents // 2
    g = jnp.where(q < 0, q + half, q - parents)
    own = ((q >> 3) << 4) + (q & 7)
    row = ((((g >> 3) & 3) ^ 2) << 4) + 8 + (g & 7)
    low, high = row + ((2 + (g >> 5)) << 6), row + ((g >> 5) << 6)
    index = jnp.where(q < 0, low, jnp.where(q < parents, own, high))
    index_ref[...] = jnp.pad(index, ((0, 32 - slots), (0, 0))).T
    kind = jnp.pad(kind_ref[...], ((0, 32 - slots), (0, 0))).T
    lane = lax.broadcasted_iota(I32, (parents, table.shape[0]), 1)
    for j in range(slots):
        hot = jnp.where(lane == kind[:, j : j + 1], 1.0, 0.0).astype(BF16)
        operators[j] = dot(hot, table[...]).astype(BF16)


def up_kernel(
    own_ref, far_ref, agg_ref, cos_ref, sin_ref, interp, out_ref, relay_ref, kept, sem
):
    copy = pltpu.make_async_copy(interp.at[:, pl.ds(0, KEPT * 256)], kept, sem)
    copy.start()
    relay_ref[...] = own_ref[...]
    width = 256
    directions = cos_ref.shape[1]
    leaves = own_ref.shape[0]
    rows = 2 * leaves
    parents = rows // 8
    r = lax.broadcasted_iota(I32, (rows, leaves), 0)
    c = lax.broadcasted_iota(I32, (rows, leaves), 1)
    leaf = 8 * (r % parents) + r // parents
    from_own = jnp.where(c == leaf, 1.0, 0.0).astype(BF16)
    from_far = jnp.where(c + leaves == leaf, 1.0, 0.0).astype(BF16)
    cur = (dot(from_own, own_ref[...]) + dot(from_far, far_ref[...])).astype(BF16)
    pattern = dot(cur, agg_ref[...]).astype(BF16)
    for j in range(directions // width):
        re = dot(pattern, interp[:, j * width : (j + 1) * width])
        im = dot(pattern, interp[:, directions + j * width : directions + (j + 1) * width])
        acc_re = jnp.zeros((parents, width), F32)
        acc_im = jnp.zeros((parents, width), F32)
        for k in range(8):
            cosine = cos_ref[pl.ds(k, 1), pl.ds(j * width, width)]
            sine = sin_ref[pl.ds(k, 1), pl.ds(j * width, width)]
            a, b = re[k * parents : (k + 1) * parents], im[k * parents : (k + 1) * parents]
            acc_re += a * cosine - b * sine
            acc_im += a * sine + b * cosine
        for h in range(width // 128):
            s = slice(h * 128, (h + 1) * 128)
            out_ref[j * (width // 128) + h, 0:parents, :] = acc_re[:, s].astype(BF16)
            out_ref[j * (width // 128) + h, parents : 2 * parents, :] = acc_im[:, s].astype(BF16)
    copy.wait()


def translate_kernel(upper_ref, index_ref, operator_ref, out_ref):
    sources = upper_ref.shape[0] * 16
    slots, rows = operator_ref.shape[:2]
    field = jnp.concatenate(
        [
            upper_ref[:, 0:16, :].reshape(sources, 128),
            upper_ref[:, 16:32, :].reshape(sources, 128),
        ],
        axis=1,
    )
    lane = lax.broadcasted_iota(I32, (rows, sources), 1)
    acc_re = jnp.zeros((rows, 128), F32)
    acc_im = jnp.zeros((rows, 128), F32)
    for j in range(slots):
        hot = jnp.where(lane == index_ref[:, j : j + 1], 1.0, 0.0).astype(BF16)
        x = dot(hot, field)
        op = operator_ref[j].astype(F32)
        xr, xi = x[:, :128], x[:, 128:]
        tr, ti = op[:, :128], op[:, 128:]
        acc_re += tr * xr - ti * xi
        acc_im += tr * xi + ti * xr
    blocks = out_ref.shape[0]
    out_ref[:, 0:8, :] = acc_re.reshape(blocks, 8, 128).astype(BF16)
    out_ref[:, 8:16, :] = acc_im.reshape(blocks, 8, 128).astype(BF16)


def down_kernel(inc_ref, cos_ref, sin_ref, near_ref, receive_ref, kept, interp, out_ref, buf, received, sems):
    width = 256
    chunks = buf.shape[1] // width
    copies = []
    for j in range(chunks):
        source = interp.at[:, pl.ds((KEPT + j) * width, width)]
        target = buf.at[:, pl.ds(j * width, width)]
        copies.append(pltpu.make_async_copy(source, target, sems.at[j]))
    for copy in copies:
        copy.start()
    leaves = received.shape[0]
    half = received.shape[1] // 2
    for s in range(inc_ref.shape[0]):
        lanes = slice(s * 128, (s + 1) * 128)
        block = inc_ref[s].astype(F32)
        re, im = block[0:8][:, None, :], block[8:16][:, None, :]
        cosine, sine = cos_ref[:, lanes][None], sin_ref[:, lanes][None]
        received[:, s * 128 : (s + 1) * 128] = (
            (re * cosine + im * sine).reshape(leaves, 128).astype(BF16)
        )
        received[:, half + s * 128 : half + (s + 1) * 128] = (
            (im * cosine - re * sine).reshape(leaves, 128).astype(BF16)
        )
    back = dot(received[:, : KEPT * width], kept[...], 1, 1)
    for j in range(chunks):
        at = (KEPT + j) * width
        copies[j].wait()
        back += dot(received[:, at : at + width], buf[:, j * width : (j + 1) * width], 1, 1)
    out_ref[...] = near_ref[...] + dot(back.astype(BF16), receive_ref[...])


def near_kernel(own_ref, sibling_ref, cross_ref, col_ref, near_hbm, _, out_ref, buf, hot, sems):
    slots = near_hbm.shape[0]
    copies = []
    for n in range(slots):
        copies.append(pltpu.make_async_copy(near_hbm.at[n], buf.at[n], sems.at[n]))
        copies[n].start()
    rows = out_ref.shape[0]
    lane = lax.broadcasted_iota(I32, (rows, 4 * rows), 1)
    for n in range(slots):
        hot[n * rows : (n + 1) * rows] = jnp.where(
            lane == col_ref[:, n : n + 1], 1.0, 0.0
        ).astype(BF16)
    blocks = (own_ref, sibling_ref, cross_ref, own_ref)
    sources = jnp.concatenate([block[...] for block in blocks], axis=0)
    picked = dot(hot[...], sources).astype(BF16)
    total = jnp.zeros(out_ref.shape, F32)
    for n in range(slots):
        copies[n].wait()
        total += dot(picked[n * rows : (n + 1) * rows], buf[n])
    out_ref[...] = total


def halo_target(i, boxes, dirs):
    b, d = divmod(i, dirs)
    z, r = divmod(d, dirs // 4)
    other = b + 1 if z >= 2 else b - 1
    if other < 0 or other >= boxes:
        return b * dirs + (3 - z) * (dirs // 4) + r
    return other * dirs + z * (dirs // 4) + (r ^ 2)


def on_device(
    boxes,
    dirs,
    currents,
    near_list,
    far_list,
    far_kind,
    aggregate,
    interp,
    receive,
    shift_angle,
    translation,
    near_matrix,
):
    leaves, width = currents.shape
    n = boxes * dirs
    me = lax.axis_index(BOTH)
    box = lax.axis_index("box")
    parents = leaves // 8 * dirs
    slots, near_slots = far_list.shape[1], near_list.shape[1]

    far_half = lax.ppermute(currents, BOTH, [(i, halo_target(i, boxes, dirs)) for i in range(n)])
    from_sibling = lax.ppermute(currents, BOTH, [(i, i ^ 1) for i in range(n)])

    place = jnp.stack([box, me]).astype(I32)
    operators, index, column, cosine, sine = call(
        prepare_kernel,
        (
            pltpu.VMEM((slots, parents, 256), BF16),
            pltpu.VMEM((parents, 32), I32),
            pltpu.VMEM((leaves, 32), I32),
            pltpu.VMEM(shift_angle.shape, F32),
            pltpu.VMEM(shift_angle.shape, F32),
        ),
        (
            place,
            *in_hbm(
                far_list.T,
                far_kind.T,
                shift_angle,
                translation.reshape(-1, translation.shape[2]),
                near_list.T,
            ),
        ),
        [whole(pltpu.SMEM)] + [whole(pltpu.HBM)] * 5,
        [
            pltpu.VMEM((slots, parents), I32),
            pltpu.VMEM((slots, parents), I32),
            pltpu.VMEM(shift_angle.shape, F32),
            pltpu.VMEM((640, translation.shape[2]), F32),
            pltpu.VMEM((near_slots, leaves), I32),
            pltpu.VMEM((384, 256), BF16),
            pltpu.SemaphoreType.DMA((5,)),
        ],
        8,
        AHEAD,
        11 << 20,
    )

    up, relay, kept = call(
        up_kernel,
        (
            jax.ShapeDtypeStruct((dirs, 4 * leaves // 8, 128), BF16),
            jax.ShapeDtypeStruct(currents.shape, BF16),
            pltpu.VMEM((interp.shape[0], KEPT * 256), BF16),
        ),
        (currents, far_half, in_vmem(aggregate), cosine, sine, in_vmem(interp)),
        [whole()] * 6,
        [pltpu.SemaphoreType.DMA],
        8,
        2 * 128 * 1024 * 4608,
        10 << 20,
    )
    upper = lax.all_to_all(up, "dir", split_axis=0, concat_axis=0, tiled=True)

    cross = [(i, min(max(i + (1 if i % 2 else -1), 0), n - 1)) for i in range(n)]
    from_cross = lax.ppermute(relay, BOTH, cross)
    local = call(
        translate_kernel,
        jax.ShapeDtypeStruct((dirs, 2 * leaves // 8, 128), BF16),
        (upper, index, operators),
        [whole()] * 3,
        [],
        8,
        2 * slots * parents * 256 * 256,
        2 << 20,
    )
    incoming = lax.all_to_all(local, "dir", split_axis=0, concat_axis=0, tiled=True)

    near = call(
        near_kernel,
        jax.ShapeDtypeStruct((leaves, width), F32),
        (currents, from_sibling, from_cross, column, *in_hbm(near_matrix), local),
        [whole()] * 4 + [whole(pltpu.HBM), whole(pl.ANY)],
        [
            pltpu.VMEM(near_matrix.shape, BF16),
            pltpu.VMEM((near_slots * leaves, 4 * leaves), BF16),
            pltpu.SemaphoreType.DMA((near_slots,)),
        ],
        24,
        2 * leaves * 27 * 512 * 640,
        15 << 20,
    )

    return call(
        down_kernel,
        jax.ShapeDtypeStruct((leaves, width), F32),
        (incoming, cosine, sine, near, in_vmem(receive), in_vmem(kept), *in_hbm(interp)),
        [whole()] * 6 + [whole(pltpu.HBM)],
        [
            pltpu.VMEM((interp.shape[0], interp.shape[1] - KEPT * 256), BF16),
            pltpu.VMEM((leaves, interp.shape[1]), BF16),
            pltpu.SemaphoreType.DMA((interp.shape[1] // 256,)),
        ],
        16,
        2 * 64 * 4096 * 1536,
        10 << 20,
    )


def solution(mesh):
    placed = (
        P(BOTH, None),
        P(BOTH, None),
        P(),
        P(),
        P(),
        P(),
        P(),
        P(),
        P(None, None, "dir"),
        P(),
    )
    body = functools.partial(on_device, mesh.shape["box"], mesh.shape["dir"])
    return jax.shard_map(
        body, mesh=mesh, in_specs=placed, out_specs=P(BOTH, None), check_vma=False
    )
```

```python
import functools

import jax
import jax.numpy as jnp
from jax import lax
from jax.experimental import pallas as pl
from jax.experimental.pallas import tpu as pltpu
from jax.sharding import PartitionSpec as P

BF16, F32, I32 = jnp.bfloat16, jnp.float32, jnp.int32
BOTH = ("box", "dir")
VMEM = pltpu.VMEM
KEPT = 2
AHEAD = 5 * 10**9


def whole(space=VMEM):
    return pl.BlockSpec(memory_space=space)


def call(body, out, args, specs, scratch, mib, flops, moved):
    return pl.pallas_call(
        body,
        out_shape=out,
        in_specs=specs,
        out_specs=jax.tree.map(lambda _: whole(), out),
        scratch_shapes=scratch,
        compiler_params=pltpu.CompilerParams(vmem_limit_bytes=mib << 20),
        cost_estimate=pl.CostEstimate(flops=flops, bytes_accessed=moved, transcendentals=0),
    )(*args)


def in_hbm(*arrays):
    return tuple(pltpu.with_memory_space_constraint(a, pltpu.HBM) for a in arrays)


def in_vmem(array):
    return pltpu.with_memory_space_constraint(array, VMEM)


def dot(a, b, ca=1, cb=0):
    return lax.dot_general(a, b, (((ca,), (cb,)), ((), ())), preferred_element_type=F32)


def prepare_kernel(
    place_ref,
    far_hbm,
    kind_hbm,
    angle_hbm,
    table_hbm,
    near_list_hbm,
    operators,
    index_ref,
    column_ref,
    cosine_ref,
    sine_ref,
    far_ref,
    kind_ref,
    angle_ref,
    table_ref,
    near_list_ref,
    table,
    sems,
):
    slots, parents = far_ref.shape
    box, me = place_ref[0], place_ref[1]
    mine = pl.ds(pl.multiple_of(box * parents, parents), parents)
    copies = [
        pltpu.make_async_copy(
            table_hbm, table_ref.at[pl.ds(0, table_hbm.shape[0])], sems.at[0]
        ),
        pltpu.make_async_copy(far_hbm.at[:, mine], far_ref, sems.at[1]),
        pltpu.make_async_copy(kind_hbm.at[:, mine], kind_ref, sems.at[2]),
        pltpu.make_async_copy(near_list_hbm, near_list_ref, sems.at[3]),
        pltpu.make_async_copy(angle_hbm, angle_ref, sems.at[4]),
    ]
    for copy in copies:
        copy.start()
    used = table_hbm.shape[0]
    table_ref[used:, :] = jnp.zeros((table_ref.shape[0] - used, table_ref.shape[1]), F32)
    for copy in copies:
        copy.wait()
    cosine_ref[...] = jnp.cos(angle_ref[...])
    sine_ref[...] = jnp.sin(angle_ref[...])
    kinds = table_ref.shape[0] // 2
    table[0:kinds, 0:128] = table_ref[pl.ds(0, kinds, stride=2), :].astype(BF16)
    table[0:kinds, 128:256] = table_ref[pl.ds(1, kinds, stride=2), :].astype(BF16)
    table[kinds:, :] = jnp.zeros((table.shape[0] - kinds, table.shape[1]), BF16)

    leaves = near_list_ref.shape[1]
    rel = near_list_ref[...] - me * leaves
    odd = me & 1
    below = jnp.where(odd == 0, 3 * leaves, leaves * 2)
    above = jnp.where(odd == 0, 0, leaves)
    column = jnp.where(rel < 0, rel + below, jnp.where(rel < leaves, rel, rel + above))
    column_ref[...] = jnp.pad(column, ((0, 32 - column.shape[0]), (0, 0))).T

    q = far_ref[...] - box * parents
    half = parents // 2
    g = jnp.where(q < 0, q + half, q - parents)
    own = ((q >> 3) << 4) + (q & 7)
    row = ((((g >> 3) & 3) ^ 2) << 4) + 8 + (g & 7)
    low, high = row + ((2 + (g >> 5)) << 6), row + ((g >> 5) << 6)
    index = jnp.where(q < 0, low, jnp.where(q < parents, own, high))
    index_ref[...] = jnp.pad(index, ((0, 32 - slots), (0, 0))).T
    kind = jnp.pad(kind_ref[...], ((0, 32 - slots), (0, 0))).T
    lane = lax.broadcasted_iota(I32, (parents, table.shape[0]), 1)
    for j in range(slots):
        hot = jnp.where(lane == kind[:, j : j + 1], 1.0, 0.0).astype(BF16)
        operators[j] = dot(hot, table[...]).astype(BF16)


def up_kernel(
    own_ref, far_ref, agg_ref, cos_ref, sin_ref, interp, out_ref, relay_ref, kept, sem
):
    copy = pltpu.make_async_copy(interp.at[:, pl.ds(0, KEPT * 256)], kept, sem)
    copy.start()
    relay_ref[...] = own_ref[...]
    width = 256
    directions = cos_ref.shape[1]
    leaves = own_ref.shape[0]
    rows = 2 * leaves
    parents = rows // 8
    r = lax.broadcasted_iota(I32, (rows, leaves), 0)
    c = lax.broadcasted_iota(I32, (rows, leaves), 1)
    leaf = 8 * (r % parents) + r // parents
    from_own = jnp.where(c == leaf, 1.0, 0.0).astype(BF16)
    from_far = jnp.where(c + leaves == leaf, 1.0, 0.0).astype(BF16)
    cur = (dot(from_own, own_ref[...]) + dot(from_far, far_ref[...])).astype(BF16)
    pattern = dot(cur, agg_ref[...]).astype(BF16)
    for j in range(directions // width):
        re = dot(pattern, interp[:, j * width : (j + 1) * width])
        im = dot(pattern, interp[:, directions + j * width : directions + (j + 1) * width])
        acc_re = jnp.zeros((parents, width), F32)
        acc_im = jnp.zeros((parents, width), F32)
        for k in range(8):
            cosine = cos_ref[pl.ds(k, 1), pl.ds(j * width, width)]
            sine = sin_ref[pl.ds(k, 1), pl.ds(j * width, width)]
            a, b = re[k * parents : (k + 1) * parents], im[k * parents : (k + 1) * parents]
            acc_re += a * cosine - b * sine
            acc_im += a * sine + b * cosine
        for h in range(width // 128):
            s = slice(h * 128, (h + 1) * 128)
            out_ref[j * (width // 128) + h, 0:parents, :] = acc_re[:, s].astype(BF16)
            out_ref[j * (width // 128) + h, parents : 2 * parents, :] = acc_im[:, s].astype(BF16)
    copy.wait()


def translate_kernel(upper_ref, index_ref, operator_ref, out_ref):
    sources = upper_ref.shape[0] * 16
    slots, rows = operator_ref.shape[:2]
    field = jnp.concatenate(
        [
            upper_ref[:, 0:16, :].reshape(sources, 128),
            upper_ref[:, 16:32, :].reshape(sources, 128),
        ],
        axis=1,
    )
    lane = lax.broadcasted_iota(I32, (rows, sources), 1).astype(BF16)
    index = index_ref[...].astype(BF16)
    one, zero = jnp.ones((), BF16), jnp.zeros((), BF16)
    acc_re = jnp.zeros((rows, 128), F32)
    acc_im = jnp.zeros((rows, 128), F32)
    for first in range(0, slots, 4):
        hot = [jnp.where(lane == index[:, j : j + 1], one, zero) for j in range(first, first + 4)]
        picked = dot(jnp.concatenate(hot, axis=0), field)
        for k in range(4):
            x = picked[k * rows : (k + 1) * rows]
            op = operator_ref[first + k].astype(F32)
            xr, xi = x[:, :128], x[:, 128:]
            tr, ti = op[:, :128], op[:, 128:]
            acc_re += tr * xr - ti * xi
            acc_im += tr * xi + ti * xr
    blocks = out_ref.shape[0]
    out_ref[:, 0:8, :] = acc_re.reshape(blocks, 8, 128).astype(BF16)
    out_ref[:, 8:16, :] = acc_im.reshape(blocks, 8, 128).astype(BF16)


def down_kernel(inc_ref, cos_ref, sin_ref, near_ref, receive_ref, kept, more, interp, out_ref, buf, received, sems):
    width = 256
    chunks = buf.shape[1] // width
    copies = []
    for j in range(chunks):
        source = interp.at[:, pl.ds((KEPT + 1 + j) * width, width)]
        target = buf.at[:, pl.ds(j * width, width)]
        copies.append(pltpu.make_async_copy(source, target, sems.at[j]))
    for copy in copies:
        copy.start()
    leaves = received.shape[0]
    half = received.shape[1] // 2
    for s in range(inc_ref.shape[0]):
        lanes = slice(s * 128, (s + 1) * 128)
        block = inc_ref[s].astype(F32)
        re, im = block[0:8][:, None, :], block[8:16][:, None, :]
        cosine, sine = cos_ref[:, lanes][None], sin_ref[:, lanes][None]
        received[:, s * 128 : (s + 1) * 128] = (
            (re * cosine + im * sine).reshape(leaves, 128).astype(BF16)
        )
        received[:, half + s * 128 : half + (s + 1) * 128] = (
            (im * cosine - re * sine).reshape(leaves, 128).astype(BF16)
        )
    back = dot(received[:, : KEPT * width], kept[...], 1, 1)
    back += dot(received[:, KEPT * width : (KEPT + 1) * width], more[...], 1, 1)
    for j in range(chunks):
        at = (KEPT + 1 + j) * width
        copies[j].wait()
        back += dot(received[:, at : at + width], buf[:, j * width : (j + 1) * width], 1, 1)
    out_ref[...] = near_ref[...] + dot(back.astype(BF16), receive_ref[...])


def near_kernel(
    own_ref, sibling_ref, cross_ref, col_ref, near_hbm, interp, _, out_ref, more, buf, hot, sems
):
    slots = near_hbm.shape[0]
    copies = []
    for n in range(slots):
        copies.append(pltpu.make_async_copy(near_hbm.at[n], buf.at[n], sems.at[n]))
        copies[n].start()
    extra = pltpu.make_async_copy(
        interp.at[:, pl.ds(KEPT * 256, more.shape[1])], more, sems.at[slots]
    )
    extra.start()
    rows = out_ref.shape[0]
    lane = lax.broadcasted_iota(I32, (rows, 4 * rows), 1)
    for n in range(slots):
        hot[n * rows : (n + 1) * rows] = jnp.where(
            lane == col_ref[:, n : n + 1], 1.0, 0.0
        ).astype(BF16)
    blocks = (own_ref, sibling_ref, cross_ref, own_ref)
    sources = jnp.concatenate([block[...] for block in blocks], axis=0)
    picked = dot(hot[...], sources).astype(BF16)
    total = jnp.zeros(out_ref.shape, F32)
    for n in range(slots):
        copies[n].wait()
        total += dot(picked[n * rows : (n + 1) * rows], buf[n])
    out_ref[...] = total
    extra.wait()


def halo_target(i, boxes, dirs):
    b, d = divmod(i, dirs)
    z, r = divmod(d, dirs // 4)
    other = b + 1 if z >= 2 else b - 1
    if other < 0 or other >= boxes:
        return b * dirs + (3 - z) * (dirs // 4) + r
    return other * dirs + z * (dirs // 4) + (r ^ 2)


def on_device(
    boxes,
    dirs,
    currents,
    near_list,
    far_list,
    far_kind,
    aggregate,
    interp,
    receive,
    shift_angle,
    translation,
    near_matrix,
):
    leaves, width = currents.shape
    n = boxes * dirs
    me = lax.axis_index(BOTH)
    box = lax.axis_index("box")
    parents = leaves // 8 * dirs
    slots, near_slots = far_list.shape[1], near_list.shape[1]

    far_half = lax.ppermute(currents, BOTH, [(i, halo_target(i, boxes, dirs)) for i in range(n)])
    from_sibling = lax.ppermute(currents, BOTH, [(i, i ^ 1) for i in range(n)])

    place = jnp.stack([box, me]).astype(I32)
    operators, index, column, cosine, sine = call(
        prepare_kernel,
        (
            pltpu.VMEM((slots, parents, 256), BF16),
            pltpu.VMEM((parents, 32), I32),
            pltpu.VMEM((leaves, 32), I32),
            pltpu.VMEM(shift_angle.shape, F32),
            pltpu.VMEM(shift_angle.shape, F32),
        ),
        (
            place,
            *in_hbm(
                far_list.T,
                far_kind.T,
                shift_angle,
                translation.reshape(-1, translation.shape[2]),
                near_list.T,
            ),
        ),
        [whole(pltpu.SMEM)] + [whole(pltpu.HBM)] * 5,
        [
            pltpu.VMEM((slots, parents), I32),
            pltpu.VMEM((slots, parents), I32),
            pltpu.VMEM(shift_angle.shape, F32),
            pltpu.VMEM((640, translation.shape[2]), F32),
            pltpu.VMEM((near_slots, leaves), I32),
            pltpu.VMEM((384, 256), BF16),
            pltpu.SemaphoreType.DMA((5,)),
        ],
        8,
        AHEAD,
        11 << 20,
    )

    up, relay, kept = call(
        up_kernel,
        (
            jax.ShapeDtypeStruct((dirs, 4 * leaves // 8, 128), BF16),
            jax.ShapeDtypeStruct(currents.shape, BF16),
            pltpu.VMEM((interp.shape[0], KEPT * 256), BF16),
        ),
        (currents, far_half, in_vmem(aggregate), cosine, sine, in_vmem(interp)),
        [whole()] * 6,
        [pltpu.SemaphoreType.DMA],
        8,
        2 * 128 * 1024 * 4608,
        10 << 20,
    )
    upper = lax.all_to_all(up, "dir", split_axis=0, concat_axis=0, tiled=True)

    cross = [(i, min(max(i + (1 if i % 2 else -1), 0), n - 1)) for i in range(n)]
    from_cross = lax.ppermute(relay, BOTH, cross)
    local = call(
        translate_kernel,
        jax.ShapeDtypeStruct((dirs, 2 * leaves // 8, 128), BF16),
        (upper, index, operators),
        [whole()] * 3,
        [],
        8,
        2 * slots * parents * 256 * 256,
        2 << 20,
    )
    incoming = lax.all_to_all(local, "dir", split_axis=0, concat_axis=0, tiled=True)

    near, more = call(
        near_kernel,
        (
            jax.ShapeDtypeStruct((leaves, width), F32),
            pltpu.VMEM((interp.shape[0], 256), BF16),
        ),
        (currents, from_sibling, from_cross, column, *in_hbm(near_matrix, interp), local),
        [whole()] * 4 + [whole(pltpu.HBM)] * 2 + [whole(pl.ANY)],
        [
            pltpu.VMEM(near_matrix.shape, BF16),
            pltpu.VMEM((near_slots * leaves, 4 * leaves), BF16),
            pltpu.SemaphoreType.DMA((near_slots + 1,)),
        ],
        24,
        2 * leaves * 27 * 512 * 640,
        15 << 20,
    )

    return call(
        down_kernel,
        jax.ShapeDtypeStruct((leaves, width), F32),
        (incoming, cosine, sine, near, in_vmem(receive), in_vmem(kept), in_vmem(more), *in_hbm(interp)),
        [whole()] * 7 + [whole(pltpu.HBM)],
        [
            pltpu.VMEM((interp.shape[0], interp.shape[1] - (KEPT + 1) * 256), BF16),
            pltpu.VMEM((leaves, interp.shape[1]), BF16),
            pltpu.SemaphoreType.DMA((interp.shape[1] // 256,)),
        ],
        16,
        2 * 64 * 4096 * 1536,
        10 << 20,
    )


def solution(mesh):
    placed = (
        P(BOTH, None),
        P(BOTH, None),
        P(),
        P(),
        P(),
        P(),
        P(),
        P(),
        P(None, None, "dir"),
        P(),
    )
    body = functools.partial(on_device, mesh.shape["box"], mesh.shape["dir"])
    return jax.shard_map(
        body, mesh=mesh, in_specs=placed, out_specs=P(BOTH, None), check_vma=False
    )
```

```python
import functools

import jax
import jax.numpy as jnp
from jax import lax
from jax.experimental import pallas as pl
from jax.experimental.pallas import tpu as pltpu
from jax.sharding import PartitionSpec as P

BF16, F32, I32 = jnp.bfloat16, jnp.float32, jnp.int32
BOTH = ("box", "dir")
VMEM = pltpu.VMEM
MORE = 2
KEPT = 1
AHEAD = 5 * 10**9


def whole(space=VMEM):
    return pl.BlockSpec(memory_space=space)


def call(body, out, args, specs, scratch, mib, flops, moved):
    return pl.pallas_call(
        body,
        out_shape=out,
        in_specs=specs,
        out_specs=jax.tree.map(lambda _: whole(), out),
        scratch_shapes=scratch,
        compiler_params=pltpu.CompilerParams(vmem_limit_bytes=mib << 20),
        cost_estimate=pl.CostEstimate(flops=flops, bytes_accessed=moved, transcendentals=0),
    )(*args)


def in_hbm(*arrays):
    return tuple(pltpu.with_memory_space_constraint(a, pltpu.HBM) for a in arrays)


def in_vmem(array):
    return pltpu.with_memory_space_constraint(array, VMEM)


def dot(a, b, ca=1, cb=0):
    return lax.dot_general(a, b, (((ca,), (cb,)), ((), ())), preferred_element_type=F32)


def prepare_kernel(
    place_ref,
    far_hbm,
    kind_hbm,
    angle_hbm,
    table_hbm,
    near_list_hbm,
    operators,
    index_ref,
    column_ref,
    cosine_ref,
    sine_ref,
    far_ref,
    kind_ref,
    angle_ref,
    table_ref,
    near_list_ref,
    table,
    sems,
):
    slots, parents = far_ref.shape
    box, me = place_ref[0], place_ref[1]
    mine = pl.ds(pl.multiple_of(box * parents, parents), parents)
    copies = [
        pltpu.make_async_copy(
            table_hbm, table_ref.at[pl.ds(0, table_hbm.shape[0])], sems.at[0]
        ),
        pltpu.make_async_copy(far_hbm.at[:, mine], far_ref, sems.at[1]),
        pltpu.make_async_copy(kind_hbm.at[:, mine], kind_ref, sems.at[2]),
        pltpu.make_async_copy(near_list_hbm, near_list_ref, sems.at[3]),
        pltpu.make_async_copy(angle_hbm, angle_ref, sems.at[4]),
    ]
    for copy in copies:
        copy.start()
    used = table_hbm.shape[0]
    table_ref[used:, :] = jnp.zeros((table_ref.shape[0] - used, table_ref.shape[1]), F32)
    for copy in copies:
        copy.wait()
    cosine_ref[...] = jnp.cos(angle_ref[...])
    sine_ref[...] = jnp.sin(angle_ref[...])
    kinds = table_ref.shape[0] // 2
    table[0:kinds, 0:128] = table_ref[pl.ds(0, kinds, stride=2), :].astype(BF16)
    table[0:kinds, 128:256] = table_ref[pl.ds(1, kinds, stride=2), :].astype(BF16)
    table[kinds:, :] = jnp.zeros((table.shape[0] - kinds, table.shape[1]), BF16)

    leaves = near_list_ref.shape[1]
    rel = near_list_ref[...] - me * leaves
    odd = me & 1
    below = jnp.where(odd == 0, 3 * leaves, leaves * 2)
    above = jnp.where(odd == 0, 0, leaves)
    column = jnp.where(rel < 0, rel + below, jnp.where(rel < leaves, rel, rel + above))
    column_ref[...] = jnp.pad(column, ((0, 32 - column.shape[0]), (0, 0))).T

    q = far_ref[...] - box * parents
    half = parents // 2
    g = jnp.where(q < 0, q + half, q - parents)
    own = ((q >> 3) << 4) + (q & 7)
    row = ((((g >> 3) & 3) ^ 2) << 4) + 8 + (g & 7)
    low, high = row + ((2 + (g >> 5)) << 6), row + ((g >> 5) << 6)
    index = jnp.where(q < 0, low, jnp.where(q < parents, own, high))
    index_ref[...] = jnp.pad(index, ((0, 32 - slots), (0, 0))).T
    kind = jnp.pad(kind_ref[...], ((0, 32 - slots), (0, 0))).T
    lane = lax.broadcasted_iota(I32, (parents, table.shape[0]), 1)
    for j in range(slots):
        hot = jnp.where(lane == kind[:, j : j + 1], 1.0, 0.0).astype(BF16)
        operators[j] = dot(hot, table[...]).astype(BF16)


def up_kernel(
    own_ref, far_ref, agg_ref, cos_ref, sin_ref, interp, out_ref, relay_ref, kept, sem
):
    copy = pltpu.make_async_copy(interp.at[:, pl.ds(0, KEPT * 256)], kept, sem)
    copy.start()
    relay_ref[...] = own_ref[...]
    width = 256
    directions = cos_ref.shape[1]
    leaves = own_ref.shape[0]
    rows = 2 * leaves
    parents = rows // 8
    r = lax.broadcasted_iota(I32, (rows, leaves), 0)
    c = lax.broadcasted_iota(I32, (rows, leaves), 1)
    leaf = 8 * (r % parents) + r // parents
    from_own = jnp.where(c == leaf, 1.0, 0.0).astype(BF16)
    from_far = jnp.where(c + leaves == leaf, 1.0, 0.0).astype(BF16)
    cur = (dot(from_own, own_ref[...]) + dot(from_far, far_ref[...])).astype(BF16)
    pattern = dot(cur, agg_ref[...]).astype(BF16)
    for j in range(directions // width):
        re = dot(pattern, interp[:, j * width : (j + 1) * width])
        im = dot(pattern, interp[:, directions + j * width : directions + (j + 1) * width])
        acc_re = jnp.zeros((parents, width), F32)
        acc_im = jnp.zeros((parents, width), F32)
        for k in range(8):
            cosine = cos_ref[pl.ds(k, 1), pl.ds(j * width, width)]
            sine = sin_ref[pl.ds(k, 1), pl.ds(j * width, width)]
            a, b = re[k * parents : (k + 1) * parents], im[k * parents : (k + 1) * parents]
            acc_re += a * cosine - b * sine
            acc_im += a * sine + b * cosine
        for h in range(width // 128):
            s = slice(h * 128, (h + 1) * 128)
            out_ref[j * (width // 128) + h, 0:parents, :] = acc_re[:, s].astype(BF16)
            out_ref[j * (width // 128) + h, parents : 2 * parents, :] = acc_im[:, s].astype(BF16)
    copy.wait()


def translate_kernel(upper_ref, index_ref, operator_ref, out_ref):
    sources = upper_ref.shape[0] * 16
    slots, rows = operator_ref.shape[:2]
    field = jnp.concatenate(
        [
            upper_ref[:, 0:16, :].reshape(sources, 128),
            upper_ref[:, 16:32, :].reshape(sources, 128),
        ],
        axis=1,
    )
    lane = lax.broadcasted_iota(I32, (rows, sources), 1).astype(BF16)
    index = index_ref[...].astype(BF16)
    one, zero = jnp.ones((), BF16), jnp.zeros((), BF16)
    acc_re = jnp.zeros((rows, 128), F32)
    acc_im = jnp.zeros((rows, 128), F32)
    for first in range(0, slots, 4):
        hot = [jnp.where(lane == index[:, j : j + 1], one, zero) for j in range(first, first + 4)]
        picked = dot(jnp.concatenate(hot, axis=0), field)
        for k in range(4):
            x = picked[k * rows : (k + 1) * rows]
            op = operator_ref[first + k].astype(F32)
            xr, xi = x[:, :128], x[:, 128:]
            tr, ti = op[:, :128], op[:, 128:]
            acc_re += tr * xr - ti * xi
            acc_im += tr * xi + ti * xr
    blocks = out_ref.shape[0]
    out_ref[:, 0:8, :] = acc_re.reshape(blocks, 8, 128).astype(BF16)
    out_ref[:, 8:16, :] = acc_im.reshape(blocks, 8, 128).astype(BF16)


def down_kernel(inc_ref, cos_ref, sin_ref, near_ref, receive_ref, kept, more, interp, out_ref, buf, received, sems):
    width = 256
    chunks = buf.shape[1] // width
    copies = []
    for j in range(chunks):
        source = interp.at[:, pl.ds((KEPT + MORE + j) * width, width)]
        target = buf.at[:, pl.ds(j * width, width)]
        copies.append(pltpu.make_async_copy(source, target, sems.at[j]))
    for copy in copies:
        copy.start()
    leaves = received.shape[0]
    half = received.shape[1] // 2
    for s in range(inc_ref.shape[0]):
        lanes = slice(s * 128, (s + 1) * 128)
        block = inc_ref[s].astype(F32)
        re, im = block[0:8][:, None, :], block[8:16][:, None, :]
        cosine, sine = cos_ref[:, lanes][None], sin_ref[:, lanes][None]
        received[:, s * 128 : (s + 1) * 128] = (
            (re * cosine + im * sine).reshape(leaves, 128).astype(BF16)
        )
        received[:, half + s * 128 : half + (s + 1) * 128] = (
            (im * cosine - re * sine).reshape(leaves, 128).astype(BF16)
        )
    back = dot(received[:, : KEPT * width], kept[...], 1, 1)
    back += dot(received[:, KEPT * width : (KEPT + MORE) * width], more[...], 1, 1)
    for j in range(chunks):
        at = (KEPT + MORE + j) * width
        copies[j].wait()
        back += dot(received[:, at : at + width], buf[:, j * width : (j + 1) * width], 1, 1)
    out_ref[...] = near_ref[...] + dot(back.astype(BF16), receive_ref[...])


def near_kernel(
    own_ref, sibling_ref, cross_ref, col_ref, near_hbm, interp, _, out_ref, more, buf, hot, sems
):
    slots = near_hbm.shape[0]
    copies = []
    for n in range(slots):
        copies.append(pltpu.make_async_copy(near_hbm.at[n], buf.at[n], sems.at[n]))
        copies[n].start()
    extra = pltpu.make_async_copy(
        interp.at[:, pl.ds(KEPT * 256, more.shape[1])], more, sems.at[slots]
    )
    extra.start()
    rows = out_ref.shape[0]
    lane = lax.broadcasted_iota(I32, (rows, 4 * rows), 1)
    for n in range(slots):
        hot[n * rows : (n + 1) * rows] = jnp.where(
            lane == col_ref[:, n : n + 1], 1.0, 0.0
        ).astype(BF16)
    blocks = (own_ref, sibling_ref, cross_ref, own_ref)
    sources = jnp.concatenate([block[...] for block in blocks], axis=0)
    picked = dot(hot[...], sources).astype(BF16)
    total = jnp.zeros(out_ref.shape, F32)
    for n in range(slots):
        copies[n].wait()
        total += dot(picked[n * rows : (n + 1) * rows], buf[n])
    out_ref[...] = total
    extra.wait()


def halo_target(i, boxes, dirs):
    b, d = divmod(i, dirs)
    z, r = divmod(d, dirs // 4)
    other = b + 1 if z >= 2 else b - 1
    if other < 0 or other >= boxes:
        return b * dirs + (3 - z) * (dirs // 4) + r
    return other * dirs + z * (dirs // 4) + (r ^ 2)


def on_device(
    boxes,
    dirs,
    currents,
    near_list,
    far_list,
    far_kind,
    aggregate,
    interp,
    receive,
    shift_angle,
    translation,
    near_matrix,
):
    leaves, width = currents.shape
    n = boxes * dirs
    me = lax.axis_index(BOTH)
    box = lax.axis_index("box")
    parents = leaves // 8 * dirs
    slots, near_slots = far_list.shape[1], near_list.shape[1]

    far_half = lax.ppermute(currents, BOTH, [(i, halo_target(i, boxes, dirs)) for i in range(n)])
    from_sibling = lax.ppermute(currents, BOTH, [(i, i ^ 1) for i in range(n)])

    place = jnp.stack([box, me]).astype(I32)
    operators, index, column, cosine, sine = call(
        prepare_kernel,
        (
            pltpu.VMEM((slots, parents, 256), BF16),
            pltpu.VMEM((parents, 32), I32),
            pltpu.VMEM((leaves, 32), I32),
            pltpu.VMEM(shift_angle.shape, F32),
            pltpu.VMEM(shift_angle.shape, F32),
        ),
        (
            place,
            *in_hbm(
                far_list.T,
                far_kind.T,
                shift_angle,
                translation.reshape(-1, translation.shape[2]),
                near_list.T,
            ),
        ),
        [whole(pltpu.SMEM)] + [whole(pltpu.HBM)] * 5,
        [
            pltpu.VMEM((slots, parents), I32),
            pltpu.VMEM((slots, parents), I32),
            pltpu.VMEM(shift_angle.shape, F32),
            pltpu.VMEM((640, translation.shape[2]), F32),
            pltpu.VMEM((near_slots, leaves), I32),
            pltpu.VMEM((384, 256), BF16),
            pltpu.SemaphoreType.DMA((5,)),
        ],
        8,
        AHEAD,
        11 << 20,
    )

    up, relay, kept = call(
        up_kernel,
        (
            jax.ShapeDtypeStruct((dirs, 4 * leaves // 8, 128), BF16),
            jax.ShapeDtypeStruct(currents.shape, BF16),
            pltpu.VMEM((interp.shape[0], KEPT * 256), BF16),
        ),
        (currents, far_half, in_vmem(aggregate), cosine, sine, in_vmem(interp)),
        [whole()] * 6,
        [pltpu.SemaphoreType.DMA],
        8,
        2 * 128 * 1024 * 4608,
        10 << 20,
    )
    upper = lax.all_to_all(up, "dir", split_axis=0, concat_axis=0, tiled=True)

    cross = [(i, min(max(i + (1 if i % 2 else -1), 0), n - 1)) for i in range(n)]
    from_cross = lax.ppermute(relay, BOTH, cross)
    local = call(
        translate_kernel,
        jax.ShapeDtypeStruct((dirs, 2 * leaves // 8, 128), BF16),
        (upper, index, operators),
        [whole()] * 3,
        [],
        8,
        2 * slots * parents * 256 * 256,
        2 << 20,
    )
    incoming = lax.all_to_all(local, "dir", split_axis=0, concat_axis=0, tiled=True)

    near, more = call(
        near_kernel,
        (
            jax.ShapeDtypeStruct((leaves, width), F32),
            pltpu.VMEM((interp.shape[0], MORE * 256), BF16),
        ),
        (currents, from_sibling, from_cross, column, *in_hbm(near_matrix, interp), local),
        [whole()] * 4 + [whole(pltpu.HBM)] * 2 + [whole(pl.ANY)],
        [
            pltpu.VMEM(near_matrix.shape, BF16),
            pltpu.VMEM((near_slots * leaves, 4 * leaves), BF16),
            pltpu.SemaphoreType.DMA((near_slots + 1,)),
        ],
        24,
        2 * leaves * 27 * 512 * 640,
        15 << 20,
    )

    return call(
        down_kernel,
        jax.ShapeDtypeStruct((leaves, width), F32),
        (incoming, cosine, sine, near, in_vmem(receive), in_vmem(kept), in_vmem(more), *in_hbm(interp)),
        [whole()] * 7 + [whole(pltpu.HBM)],
        [
            pltpu.VMEM((interp.shape[0], interp.shape[1] - (KEPT + MORE) * 256), BF16),
            pltpu.VMEM((leaves, interp.shape[1]), BF16),
            pltpu.SemaphoreType.DMA((interp.shape[1] // 256,)),
        ],
        16,
        2 * 64 * 4096 * 1536,
        10 << 20,
    )


def solution(mesh):
    placed = (
        P(BOTH, None),
        P(BOTH, None),
        P(),
        P(),
        P(),
        P(),
        P(),
        P(),
        P(None, None, "dir"),
        P(),
    )
    body = functools.partial(on_device, mesh.shape["box"], mesh.shape["dir"])
    return jax.shard_map(
        body, mesh=mesh, in_specs=placed, out_specs=P(BOTH, None), check_vma=False
    )
```

```python
import functools

import jax
import jax.numpy as jnp
from jax import lax
from jax.experimental import pallas as pl
from jax.experimental.pallas import tpu as pltpu
from jax.sharding import PartitionSpec as P

BF16, F32, I32 = jnp.bfloat16, jnp.float32, jnp.int32
BOTH = ("box", "dir")
VMEM = pltpu.VMEM
MORE = 2
KEPT = 1
AHEAD = 5 * 10**9


def whole(space=VMEM):
    return pl.BlockSpec(memory_space=space)


def call(body, out, args, specs, scratch, mib, flops, moved):
    return pl.pallas_call(
        body,
        out_shape=out,
        in_specs=specs,
        out_specs=jax.tree.map(lambda _: whole(), out),
        scratch_shapes=scratch,
        compiler_params=pltpu.CompilerParams(vmem_limit_bytes=mib << 20),
        cost_estimate=pl.CostEstimate(flops=flops, bytes_accessed=moved, transcendentals=0),
    )(*args)


def in_hbm(*arrays):
    return tuple(pltpu.with_memory_space_constraint(a, pltpu.HBM) for a in arrays)


def in_vmem(array):
    return pltpu.with_memory_space_constraint(array, VMEM)


def dot(a, b, ca=1, cb=0):
    return lax.dot_general(a, b, (((ca,), (cb,)), ((), ())), preferred_element_type=F32)


def prepare_kernel(
    place_ref,
    far_hbm,
    kind_hbm,
    angle_hbm,
    table_hbm,
    near_list_hbm,
    operators,
    index_ref,
    column_ref,
    cosine_ref,
    sine_ref,
    far_ref,
    kind_ref,
    angle_ref,
    table_ref,
    near_list_ref,
    table,
    sems,
):
    slots, parents = far_ref.shape
    box, me = place_ref[0], place_ref[1]
    mine = pl.ds(pl.multiple_of(box * parents, parents), parents)
    copies = [
        pltpu.make_async_copy(
            table_hbm, table_ref.at[pl.ds(0, table_hbm.shape[0])], sems.at[0]
        ),
        pltpu.make_async_copy(far_hbm.at[:, mine], far_ref, sems.at[1]),
        pltpu.make_async_copy(kind_hbm.at[:, mine], kind_ref, sems.at[2]),
        pltpu.make_async_copy(near_list_hbm, near_list_ref, sems.at[3]),
        pltpu.make_async_copy(angle_hbm, angle_ref, sems.at[4]),
    ]
    for copy in copies:
        copy.start()
    used = table_hbm.shape[0]
    table_ref[used:, :] = jnp.zeros((table_ref.shape[0] - used, table_ref.shape[1]), F32)
    for copy in copies:
        copy.wait()
    cosine_ref[...] = jnp.cos(angle_ref[...])
    sine_ref[...] = jnp.sin(angle_ref[...])
    kinds = table_ref.shape[0] // 2
    table[0:kinds, 0:128] = table_ref[pl.ds(0, kinds, stride=2), :].astype(BF16)
    table[0:kinds, 128:256] = table_ref[pl.ds(1, kinds, stride=2), :].astype(BF16)
    table[kinds:, :] = jnp.zeros((table.shape[0] - kinds, table.shape[1]), BF16)

    leaves = near_list_ref.shape[1]
    rel = near_list_ref[...] - me * leaves
    odd = me & 1
    below = jnp.where(odd == 0, 3 * leaves, leaves * 2)
    above = jnp.where(odd == 0, 0, leaves)
    column = jnp.where(rel < 0, rel + below, jnp.where(rel < leaves, rel, rel + above))
    column_ref[...] = jnp.pad(column, ((0, 32 - column.shape[0]), (0, 0))).T

    q = far_ref[...] - box * parents
    half = parents // 2
    g = jnp.where(q < 0, q + half, q - parents)
    own = ((q >> 3) << 4) + (q & 7)
    row = ((((g >> 3) & 3) ^ 2) << 4) + 8 + (g & 7)
    low, high = row + ((2 + (g >> 5)) << 6), row + ((g >> 5) << 6)
    index = jnp.where(q < 0, low, jnp.where(q < parents, own, high))
    index_ref[...] = jnp.pad(index, ((0, 32 - slots), (0, 0))).T
    kind = jnp.pad(kind_ref[...], ((0, 32 - slots), (0, 0))).T
    lane = lax.broadcasted_iota(I32, (parents, table.shape[0]), 1)
    for j in range(slots):
        hot = jnp.where(lane == kind[:, j : j + 1], 1.0, 0.0).astype(BF16)
        operators[j] = dot(hot, table[...]).astype(BF16)


def up_kernel(
    own_ref, far_ref, agg_ref, cos_ref, sin_ref, interp, out_ref, relay_ref, kept, sem
):
    copy = pltpu.make_async_copy(interp.at[:, pl.ds(0, KEPT * 256)], kept, sem)
    copy.start()
    relay_ref[...] = own_ref[...]
    width = 512
    directions = cos_ref.shape[1]
    leaves = own_ref.shape[0]
    rows = 2 * leaves
    parents = rows // 8
    r = lax.broadcasted_iota(I32, (rows, leaves), 0)
    c = lax.broadcasted_iota(I32, (rows, leaves), 1)
    leaf = 8 * (r % parents) + r // parents
    from_own = jnp.where(c == leaf, 1.0, 0.0).astype(BF16)
    from_far = jnp.where(c + leaves == leaf, 1.0, 0.0).astype(BF16)
    cur = (dot(from_own, own_ref[...]) + dot(from_far, far_ref[...])).astype(BF16)
    pattern = dot(cur, agg_ref[...]).astype(BF16)
    for j in range(directions // width):
        re = dot(pattern, interp[:, j * width : (j + 1) * width])
        im = dot(pattern, interp[:, directions + j * width : directions + (j + 1) * width])
        for h in range(width // 128):
            lanes = slice(h * 128, (h + 1) * 128)
            acc_re = jnp.zeros((parents, 128), F32)
            acc_im = jnp.zeros((parents, 128), F32)
            for k in range(8):
                cosine = cos_ref[pl.ds(k, 1), pl.ds(j * width + h * 128, 128)]
                sine = sin_ref[pl.ds(k, 1), pl.ds(j * width + h * 128, 128)]
                a = re[k * parents : (k + 1) * parents, lanes]
                b = im[k * parents : (k + 1) * parents, lanes]
                acc_re += a * cosine - b * sine
                acc_im += a * sine + b * cosine
            block = j * (width // 128) + h
            out_ref[block, 0:parents, :] = acc_re.astype(BF16)
            out_ref[block, parents : 2 * parents, :] = acc_im.astype(BF16)
    copy.wait()


def translate_kernel(upper_ref, index_ref, operator_ref, out_ref):
    sources = upper_ref.shape[0] * 16
    slots, rows = operator_ref.shape[:2]
    field = jnp.concatenate(
        [
            upper_ref[:, 0:16, :].reshape(sources, 128),
            upper_ref[:, 16:32, :].reshape(sources, 128),
        ],
        axis=1,
    )
    lane = lax.broadcasted_iota(I32, (rows, sources), 1).astype(BF16)
    index = index_ref[...].astype(BF16)
    one, zero = jnp.ones((), BF16), jnp.zeros((), BF16)
    acc_re = jnp.zeros((rows, 128), F32)
    acc_im = jnp.zeros((rows, 128), F32)
    for first in range(0, slots, 4):
        hot = [jnp.where(lane == index[:, j : j + 1], one, zero) for j in range(first, first + 4)]
        picked = dot(jnp.concatenate(hot, axis=0), field)
        for k in range(4):
            x = picked[k * rows : (k + 1) * rows]
            op = operator_ref[first + k].astype(F32)
            xr, xi = x[:, :128], x[:, 128:]
            tr, ti = op[:, :128], op[:, 128:]
            acc_re += tr * xr - ti * xi
            acc_im += tr * xi + ti * xr
    blocks = out_ref.shape[0]
    out_ref[:, 0:8, :] = acc_re.reshape(blocks, 8, 128).astype(BF16)
    out_ref[:, 8:16, :] = acc_im.reshape(blocks, 8, 128).astype(BF16)


def down_kernel(inc_ref, cos_ref, sin_ref, near_ref, receive_ref, kept, more, interp, out_ref, buf, received, sems):
    width = 256
    chunks = buf.shape[1] // width
    copies = []
    for j in range(chunks):
        source = interp.at[:, pl.ds((KEPT + MORE + j) * width, width)]
        target = buf.at[:, pl.ds(j * width, width)]
        copies.append(pltpu.make_async_copy(source, target, sems.at[j]))
    for copy in copies:
        copy.start()
    leaves = received.shape[0]
    half = received.shape[1] // 2
    for s in range(inc_ref.shape[0]):
        lanes = slice(s * 128, (s + 1) * 128)
        block = inc_ref[s].astype(F32)
        re, im = block[0:8][:, None, :], block[8:16][:, None, :]
        cosine, sine = cos_ref[:, lanes][None], sin_ref[:, lanes][None]
        received[:, s * 128 : (s + 1) * 128] = (
            (re * cosine + im * sine).reshape(leaves, 128).astype(BF16)
        )
        received[:, half + s * 128 : half + (s + 1) * 128] = (
            (im * cosine - re * sine).reshape(leaves, 128).astype(BF16)
        )
    back = dot(received[:, : KEPT * width], kept[...], 1, 1)
    back += dot(received[:, KEPT * width : (KEPT + MORE) * width], more[...], 1, 1)
    for j in range(chunks):
        at = (KEPT + MORE + j) * width
        copies[j].wait()
        back += dot(received[:, at : at + width], buf[:, j * width : (j + 1) * width], 1, 1)
    out_ref[...] = near_ref[...] + dot(back.astype(BF16), receive_ref[...])


def near_kernel(
    own_ref, sibling_ref, cross_ref, col_ref, near_hbm, interp, _, out_ref, more, buf, hot, sems
):
    slots = near_hbm.shape[0]
    copies = []
    for n in range(slots):
        copies.append(pltpu.make_async_copy(near_hbm.at[n], buf.at[n], sems.at[n]))
        copies[n].start()
    extra = pltpu.make_async_copy(
        interp.at[:, pl.ds(KEPT * 256, more.shape[1])], more, sems.at[slots]
    )
    extra.start()
    rows = out_ref.shape[0]
    lane = lax.broadcasted_iota(I32, (rows, 4 * rows), 1)
    for n in range(slots):
        hot[n * rows : (n + 1) * rows] = jnp.where(
            lane == col_ref[:, n : n + 1], 1.0, 0.0
        ).astype(BF16)
    blocks = (own_ref, sibling_ref, cross_ref, own_ref)
    sources = jnp.concatenate([block[...] for block in blocks], axis=0)
    picked = dot(hot[...], sources).astype(BF16)
    total = jnp.zeros(out_ref.shape, F32)
    for n in range(slots):
        copies[n].wait()
        total += dot(picked[n * rows : (n + 1) * rows], buf[n])
    out_ref[...] = total
    extra.wait()


def halo_target(i, boxes, dirs):
    b, d = divmod(i, dirs)
    z, r = divmod(d, dirs // 4)
    other = b + 1 if z >= 2 else b - 1
    if other < 0 or other >= boxes:
        return b * dirs + (3 - z) * (dirs // 4) + r
    return other * dirs + z * (dirs // 4) + (r ^ 2)


def on_device(
    boxes,
    dirs,
    currents,
    near_list,
    far_list,
    far_kind,
    aggregate,
    interp,
    receive,
    shift_angle,
    translation,
    near_matrix,
):
    leaves, width = currents.shape
    n = boxes * dirs
    me = lax.axis_index(BOTH)
    box = lax.axis_index("box")
    parents = leaves // 8 * dirs
    slots, near_slots = far_list.shape[1], near_list.shape[1]

    far_half = lax.ppermute(currents, BOTH, [(i, halo_target(i, boxes, dirs)) for i in range(n)])
    from_sibling = lax.ppermute(currents, BOTH, [(i, i ^ 1) for i in range(n)])

    place = jnp.stack([box, me]).astype(I32)
    operators, index, column, cosine, sine = call(
        prepare_kernel,
        (
            pltpu.VMEM((slots, parents, 256), BF16),
            pltpu.VMEM((parents, 32), I32),
            pltpu.VMEM((leaves, 32), I32),
            pltpu.VMEM(shift_angle.shape, F32),
            pltpu.VMEM(shift_angle.shape, F32),
        ),
        (
            place,
            *in_hbm(
                far_list.T,
                far_kind.T,
                shift_angle,
                translation.reshape(-1, translation.shape[2]),
                near_list.T,
            ),
        ),
        [whole(pltpu.SMEM)] + [whole(pltpu.HBM)] * 5,
        [
            pltpu.VMEM((slots, parents), I32),
            pltpu.VMEM((slots, parents), I32),
            pltpu.VMEM(shift_angle.shape, F32),
            pltpu.VMEM((640, translation.shape[2]), F32),
            pltpu.VMEM((near_slots, leaves), I32),
            pltpu.VMEM((384, 256), BF16),
            pltpu.SemaphoreType.DMA((5,)),
        ],
        8,
        AHEAD,
        11 << 20,
    )

    up, relay, kept = call(
        up_kernel,
        (
            jax.ShapeDtypeStruct((dirs, 4 * leaves // 8, 128), BF16),
            jax.ShapeDtypeStruct(currents.shape, BF16),
            pltpu.VMEM((interp.shape[0], KEPT * 256), BF16),
        ),
        (currents, far_half, in_vmem(aggregate), cosine, sine, in_vmem(interp)),
        [whole()] * 6,
        [pltpu.SemaphoreType.DMA],
        8,
        2 * 128 * 1024 * 4608,
        10 << 20,
    )
    upper = lax.all_to_all(up, "dir", split_axis=0, concat_axis=0, tiled=True)

    cross = [(i, min(max(i + (1 if i % 2 else -1), 0), n - 1)) for i in range(n)]
    from_cross = lax.ppermute(relay, BOTH, cross)
    local = call(
        translate_kernel,
        jax.ShapeDtypeStruct((dirs, 2 * leaves // 8, 128), BF16),
        (upper, index, operators),
        [whole()] * 3,
        [],
        8,
        2 * slots * parents * 256 * 256,
        2 << 20,
    )
    incoming = lax.all_to_all(local, "dir", split_axis=0, concat_axis=0, tiled=True)

    near, more = call(
        near_kernel,
        (
            jax.ShapeDtypeStruct((leaves, width), F32),
            pltpu.VMEM((interp.shape[0], MORE * 256), BF16),
        ),
        (currents, from_sibling, from_cross, column, *in_hbm(near_matrix, interp), local),
        [whole()] * 4 + [whole(pltpu.HBM)] * 2 + [whole(pl.ANY)],
        [
            pltpu.VMEM(near_matrix.shape, BF16),
            pltpu.VMEM((near_slots * leaves, 4 * leaves), BF16),
            pltpu.SemaphoreType.DMA((near_slots + 1,)),
        ],
        24,
        2 * leaves * 27 * 512 * 640,
        15 << 20,
    )

    return call(
        down_kernel,
        jax.ShapeDtypeStruct((leaves, width), F32),
        (incoming, cosine, sine, near, in_vmem(receive), in_vmem(kept), in_vmem(more), *in_hbm(interp)),
        [whole()] * 7 + [whole(pltpu.HBM)],
        [
            pltpu.VMEM((interp.shape[0], interp.shape[1] - (KEPT + MORE) * 256), BF16),
            pltpu.VMEM((leaves, interp.shape[1]), BF16),
            pltpu.SemaphoreType.DMA((interp.shape[1] // 256,)),
        ],
        16,
        2 * 64 * 4096 * 1536,
        10 << 20,
    )


def solution(mesh):
    placed = (
        P(BOTH, None),
        P(BOTH, None),
        P(),
        P(),
        P(),
        P(),
        P(),
        P(),
        P(None, None, "dir"),
        P(),
    )
    body = functools.partial(on_device, mesh.shape["box"], mesh.shape["dir"])
    return jax.shard_map(
        body, mesh=mesh, in_specs=placed, out_specs=P(BOTH, None), check_vma=False
    )
```

```python
import functools

import jax
import jax.numpy as jnp
from jax import lax
from jax.experimental import pallas as pl
from jax.experimental.pallas import tpu as pltpu
from jax.sharding import PartitionSpec as P

BF16, F32, I32 = jnp.bfloat16, jnp.float32, jnp.int32
BOTH = ("box", "dir")
VMEM = pltpu.VMEM
MORE = 2
KEPT = 1
AHEAD = 5 * 10**9


def whole(space=VMEM):
    return pl.BlockSpec(memory_space=space)


def call(body, out, args, specs, scratch, mib, flops, moved):
    return pl.pallas_call(
        body,
        out_shape=out,
        in_specs=specs,
        out_specs=jax.tree.map(lambda _: whole(), out),
        scratch_shapes=scratch,
        compiler_params=pltpu.CompilerParams(vmem_limit_bytes=mib << 20),
        cost_estimate=pl.CostEstimate(flops=flops, bytes_accessed=moved, transcendentals=0),
    )(*args)


def in_hbm(*arrays):
    return tuple(pltpu.with_memory_space_constraint(a, pltpu.HBM) for a in arrays)


def in_vmem(array):
    return pltpu.with_memory_space_constraint(array, VMEM)


def dot(a, b, ca=1, cb=0):
    return lax.dot_general(a, b, (((ca,), (cb,)), ((), ())), preferred_element_type=F32)


def prepare_kernel(
    far_hbm,
    kind_hbm,
    angle_hbm,
    table_hbm,
    near_list_hbm,
    operators,
    index_ref,
    column_ref,
    cosine_ref,
    sine_ref,
    far_ref,
    kind_ref,
    angle_ref,
    table_ref,
    near_list_ref,
    table,
    sems,
):
    slots, parents = far_ref.shape
    box, me = lax.axis_index("box"), lax.axis_index(BOTH)
    mine = pl.ds(pl.multiple_of(box * parents, parents), parents)
    copies = [
        pltpu.make_async_copy(
            table_hbm, table_ref.at[pl.ds(0, table_hbm.shape[0])], sems.at[0]
        ),
        pltpu.make_async_copy(far_hbm.at[:, mine], far_ref, sems.at[1]),
        pltpu.make_async_copy(kind_hbm.at[:, mine], kind_ref, sems.at[2]),
        pltpu.make_async_copy(near_list_hbm, near_list_ref, sems.at[3]),
        pltpu.make_async_copy(angle_hbm, angle_ref, sems.at[4]),
    ]
    for copy in copies:
        copy.start()
    used = table_hbm.shape[0]
    table_ref[used:, :] = jnp.zeros((table_ref.shape[0] - used, table_ref.shape[1]), F32)
    for copy in copies:
        copy.wait()
    cosine_ref[...] = jnp.cos(angle_ref[...])
    sine_ref[...] = jnp.sin(angle_ref[...])
    kinds = table_ref.shape[0] // 2
    table[0:kinds, 0:128] = table_ref[pl.ds(0, kinds, stride=2), :].astype(BF16)
    table[0:kinds, 128:256] = table_ref[pl.ds(1, kinds, stride=2), :].astype(BF16)
    table[kinds:, :] = jnp.zeros((table.shape[0] - kinds, table.shape[1]), BF16)

    leaves = near_list_ref.shape[1]
    rel = near_list_ref[...] - me * leaves
    odd = me & 1
    below = jnp.where(odd == 0, 3 * leaves, leaves * 2)
    above = jnp.where(odd == 0, 0, leaves)
    column = jnp.where(rel < 0, rel + below, jnp.where(rel < leaves, rel, rel + above))
    column_ref[...] = jnp.pad(column, ((0, 32 - column.shape[0]), (0, 0))).T

    q = far_ref[...] - box * parents
    half = parents // 2
    g = jnp.where(q < 0, q + half, q - parents)
    own = ((q >> 3) << 4) + (q & 7)
    row = ((((g >> 3) & 3) ^ 2) << 4) + 8 + (g & 7)
    low, high = row + ((2 + (g >> 5)) << 6), row + ((g >> 5) << 6)
    index = jnp.where(q < 0, low, jnp.where(q < parents, own, high))
    index_ref[...] = jnp.pad(index, ((0, 32 - slots), (0, 0))).T
    kind = jnp.pad(kind_ref[...], ((0, 32 - slots), (0, 0))).T
    lane = lax.broadcasted_iota(I32, (parents, table.shape[0]), 1)
    for j in range(slots):
        hot = jnp.where(lane == kind[:, j : j + 1], 1.0, 0.0).astype(BF16)
        operators[j] = dot(hot, table[...]).astype(BF16)


def up_kernel(
    own_ref, far_ref, agg_ref, cos_ref, sin_ref, interp, out_ref, relay_ref, kept, sem
):
    copy = pltpu.make_async_copy(interp.at[:, pl.ds(0, KEPT * 256)], kept, sem)
    copy.start()
    relay_ref[...] = own_ref[...]
    width = 512
    directions = cos_ref.shape[1]
    leaves = own_ref.shape[0]
    rows = 2 * leaves
    parents = rows // 8
    r = lax.broadcasted_iota(I32, (rows, leaves), 0)
    c = lax.broadcasted_iota(I32, (rows, leaves), 1)
    leaf = 8 * (r % parents) + r // parents
    from_own = jnp.where(c == leaf, 1.0, 0.0).astype(BF16)
    from_far = jnp.where(c + leaves == leaf, 1.0, 0.0).astype(BF16)
    cur = (dot(from_own, own_ref[...]) + dot(from_far, far_ref[...])).astype(BF16)
    pattern = dot(cur, agg_ref[...]).astype(BF16)
    for j in range(directions // width):
        re = dot(pattern, interp[:, j * width : (j + 1) * width])
        im = dot(pattern, interp[:, directions + j * width : directions + (j + 1) * width])
        for h in range(width // 128):
            lanes = slice(h * 128, (h + 1) * 128)
            acc_re = jnp.zeros((parents, 128), F32)
            acc_im = jnp.zeros((parents, 128), F32)
            for k in range(8):
                cosine = cos_ref[pl.ds(k, 1), pl.ds(j * width + h * 128, 128)]
                sine = sin_ref[pl.ds(k, 1), pl.ds(j * width + h * 128, 128)]
                a = re[k * parents : (k + 1) * parents, lanes]
                b = im[k * parents : (k + 1) * parents, lanes]
                acc_re += a * cosine - b * sine
                acc_im += a * sine + b * cosine
            block = j * (width // 128) + h
            out_ref[block, 0:parents, :] = acc_re.astype(BF16)
            out_ref[block, parents : 2 * parents, :] = acc_im.astype(BF16)
    copy.wait()


def translate_kernel(upper_ref, index_ref, operator_ref, out_ref):
    sources = upper_ref.shape[0] * 16
    slots, rows = operator_ref.shape[:2]
    field = jnp.concatenate(
        [
            upper_ref[:, 0:16, :].reshape(sources, 128),
            upper_ref[:, 16:32, :].reshape(sources, 128),
        ],
        axis=1,
    )
    lane = lax.broadcasted_iota(I32, (rows, sources), 1).astype(BF16)
    index = index_ref[...].astype(BF16)
    one, zero = jnp.ones((), BF16), jnp.zeros((), BF16)
    acc_re = jnp.zeros((rows, 128), F32)
    acc_im = jnp.zeros((rows, 128), F32)
    for first in range(0, slots, 4):
        hot = [jnp.where(lane == index[:, j : j + 1], one, zero) for j in range(first, first + 4)]
        picked = dot(jnp.concatenate(hot, axis=0), field)
        for k in range(4):
            x = picked[k * rows : (k + 1) * rows]
            op = operator_ref[first + k].astype(F32)
            xr, xi = x[:, :128], x[:, 128:]
            tr, ti = op[:, :128], op[:, 128:]
            acc_re += tr * xr - ti * xi
            acc_im += tr * xi + ti * xr
    blocks = out_ref.shape[0]
    out_ref[:, 0:8, :] = acc_re.reshape(blocks, 8, 128).astype(BF16)
    out_ref[:, 8:16, :] = acc_im.reshape(blocks, 8, 128).astype(BF16)


def down_kernel(inc_ref, cos_ref, sin_ref, near_ref, receive_ref, kept, more, interp, out_ref, buf, received, sems):
    width = 256
    chunks = buf.shape[1] // width
    copies = []
    for j in range(chunks):
        source = interp.at[:, pl.ds((KEPT + MORE + j) * width, width)]
        target = buf.at[:, pl.ds(j * width, width)]
        copies.append(pltpu.make_async_copy(source, target, sems.at[j]))
    for copy in copies:
        copy.start()
    leaves = received.shape[0]
    half = received.shape[1] // 2
    for s in range(inc_ref.shape[0]):
        lanes = slice(s * 128, (s + 1) * 128)
        block = inc_ref[s].astype(F32)
        re, im = block[0:8][:, None, :], block[8:16][:, None, :]
        cosine, sine = cos_ref[:, lanes][None], sin_ref[:, lanes][None]
        received[:, s * 128 : (s + 1) * 128] = (
            (re * cosine + im * sine).reshape(leaves, 128).astype(BF16)
        )
        received[:, half + s * 128 : half + (s + 1) * 128] = (
            (im * cosine - re * sine).reshape(leaves, 128).astype(BF16)
        )
    back = dot(received[:, : KEPT * width], kept[...], 1, 1)
    back += dot(received[:, KEPT * width : (KEPT + MORE) * width], more[...], 1, 1)
    for j in range(chunks):
        at = (KEPT + MORE + j) * width
        copies[j].wait()
        back += dot(received[:, at : at + width], buf[:, j * width : (j + 1) * width], 1, 1)
    out_ref[...] = near_ref[...] + dot(back.astype(BF16), receive_ref[...])


def near_kernel(
    own_ref, sibling_ref, cross_ref, col_ref, near_hbm, interp, _, out_ref, more, buf, hot, sems
):
    slots = near_hbm.shape[0]
    copies = []
    for n in range(slots):
        copies.append(pltpu.make_async_copy(near_hbm.at[n], buf.at[n], sems.at[n]))
        copies[n].start()
    extra = pltpu.make_async_copy(
        interp.at[:, pl.ds(KEPT * 256, more.shape[1])], more, sems.at[slots]
    )
    extra.start()
    rows = out_ref.shape[0]
    lane = lax.broadcasted_iota(I32, (rows, 4 * rows), 1)
    for n in range(slots):
        hot[n * rows : (n + 1) * rows] = jnp.where(
            lane == col_ref[:, n : n + 1], 1.0, 0.0
        ).astype(BF16)
    blocks = (own_ref, sibling_ref, cross_ref, own_ref)
    sources = jnp.concatenate([block[...] for block in blocks], axis=0)
    picked = dot(hot[...], sources).astype(BF16)
    total = jnp.zeros(out_ref.shape, F32)
    for n in range(slots):
        copies[n].wait()
        total += dot(picked[n * rows : (n + 1) * rows], buf[n])
    out_ref[...] = total
    extra.wait()


def halo_target(i, boxes, dirs):
    b, d = divmod(i, dirs)
    z, r = divmod(d, dirs // 4)
    other = b + 1 if z >= 2 else b - 1
    if other < 0 or other >= boxes:
        return b * dirs + (3 - z) * (dirs // 4) + r
    return other * dirs + z * (dirs // 4) + (r ^ 2)


def on_device(
    boxes,
    dirs,
    currents,
    near_list,
    far_list,
    far_kind,
    aggregate,
    interp,
    receive,
    shift_angle,
    translation,
    near_matrix,
):
    leaves, width = currents.shape
    n = boxes * dirs
    parents = leaves // 8 * dirs
    slots, near_slots = far_list.shape[1], near_list.shape[1]

    far_half = lax.ppermute(currents, BOTH, [(i, halo_target(i, boxes, dirs)) for i in range(n)])
    from_sibling = lax.ppermute(currents, BOTH, [(i, i ^ 1) for i in range(n)])

    operators, index, column, cosine, sine = call(
        prepare_kernel,
        (
            pltpu.VMEM((slots, parents, 256), BF16),
            pltpu.VMEM((parents, 32), I32),
            pltpu.VMEM((leaves, 32), I32),
            pltpu.VMEM(shift_angle.shape, F32),
            pltpu.VMEM(shift_angle.shape, F32),
        ),
        in_hbm(
            far_list.T,
            far_kind.T,
            shift_angle,
            translation.reshape(-1, translation.shape[2]),
            near_list.T,
        ),
        [whole(pltpu.HBM)] * 5,
        [
            pltpu.VMEM((slots, parents), I32),
            pltpu.VMEM((slots, parents), I32),
            pltpu.VMEM(shift_angle.shape, F32),
            pltpu.VMEM((640, translation.shape[2]), F32),
            pltpu.VMEM((near_slots, leaves), I32),
            pltpu.VMEM((384, 256), BF16),
            pltpu.SemaphoreType.DMA((5,)),
        ],
        8,
        AHEAD,
        11 << 20,
    )

    up, relay, kept = call(
        up_kernel,
        (
            jax.ShapeDtypeStruct((dirs, 4 * leaves // 8, 128), BF16),
            jax.ShapeDtypeStruct(currents.shape, BF16),
            pltpu.VMEM((interp.shape[0], KEPT * 256), BF16),
        ),
        (currents, far_half, in_vmem(aggregate), cosine, sine, in_vmem(interp)),
        [whole()] * 6,
        [pltpu.SemaphoreType.DMA],
        8,
        2 * 128 * 1024 * 4608,
        10 << 20,
    )
    upper = lax.all_to_all(up, "dir", split_axis=0, concat_axis=0, tiled=True)

    cross = [(i, min(max(i + (1 if i % 2 else -1), 0), n - 1)) for i in range(n)]
    from_cross = lax.ppermute(relay, BOTH, cross)
    local = call(
        translate_kernel,
        jax.ShapeDtypeStruct((dirs, 2 * leaves // 8, 128), BF16),
        (upper, index, operators),
        [whole()] * 3,
        [],
        8,
        2 * slots * parents * 256 * 256,
        2 << 20,
    )
    incoming = lax.all_to_all(local, "dir", split_axis=0, concat_axis=0, tiled=True)

    near, more = call(
        near_kernel,
        (
            jax.ShapeDtypeStruct((leaves, width), F32),
            pltpu.VMEM((interp.shape[0], MORE * 256), BF16),
        ),
        (currents, from_sibling, from_cross, column, *in_hbm(near_matrix, interp), local),
        [whole()] * 4 + [whole(pltpu.HBM)] * 2 + [whole(pl.ANY)],
        [
            pltpu.VMEM(near_matrix.shape, BF16),
            pltpu.VMEM((near_slots * leaves, 4 * leaves), BF16),
            pltpu.SemaphoreType.DMA((near_slots + 1,)),
        ],
        24,
        2 * leaves * 27 * 512 * 640,
        15 << 20,
    )

    return call(
        down_kernel,
        jax.ShapeDtypeStruct((leaves, width), F32),
        (incoming, cosine, sine, near, in_vmem(receive), in_vmem(kept), in_vmem(more), *in_hbm(interp)),
        [whole()] * 7 + [whole(pltpu.HBM)],
        [
            pltpu.VMEM((interp.shape[0], interp.shape[1] - (KEPT + MORE) * 256), BF16),
            pltpu.VMEM((leaves, interp.shape[1]), BF16),
            pltpu.SemaphoreType.DMA((interp.shape[1] // 256,)),
        ],
        16,
        2 * 64 * 4096 * 1536,
        10 << 20,
    )


def solution(mesh):
    placed = (
        P(BOTH, None),
        P(BOTH, None),
        P(),
        P(),
        P(),
        P(),
        P(),
        P(),
        P(None, None, "dir"),
        P(),
    )
    body = functools.partial(on_device, mesh.shape["box"], mesh.shape["dir"])
    return jax.shard_map(
        body, mesh=mesh, in_specs=placed, out_specs=P(BOTH, None), check_vma=False
    )
```

```python
import functools

import jax
import jax.numpy as jnp
from jax import lax
from jax.experimental import pallas as pl
from jax.experimental.pallas import tpu as pltpu
from jax.sharding import PartitionSpec as P

BF16, F32, I32 = jnp.bfloat16, jnp.float32, jnp.int32
BOTH = ("box", "dir")
VMEM = pltpu.VMEM
MORE = 2
KEPT = 1
AHEAD = 5 * 10**9


def whole(space=VMEM):
    return pl.BlockSpec(memory_space=space)


def call(body, out, args, specs, scratch, mib, flops, moved, place=VMEM):
    return pl.pallas_call(
        body,
        out_shape=out,
        in_specs=specs,
        out_specs=jax.tree.map(lambda _: whole(place), out),
        scratch_shapes=scratch,
        compiler_params=pltpu.CompilerParams(vmem_limit_bytes=mib << 20),
        cost_estimate=pl.CostEstimate(flops=flops, bytes_accessed=moved, transcendentals=0),
    )(*args)


def in_hbm(*arrays):
    return tuple(pltpu.with_memory_space_constraint(a, pltpu.HBM) for a in arrays)


def in_vmem(array):
    return pltpu.with_memory_space_constraint(array, VMEM)


def dot(a, b, ca=1, cb=0):
    return lax.dot_general(a, b, (((ca,), (cb,)), ((), ())), preferred_element_type=F32)


def prepare_kernel(
    place_ref,
    far_hbm,
    kind_hbm,
    angle_hbm,
    table_hbm,
    near_list_hbm,
    operators,
    index_ref,
    column_ref,
    cosine_ref,
    sine_ref,
    far_ref,
    kind_ref,
    angle_ref,
    table_ref,
    near_list_ref,
    table,
    sems,
):
    slots, parents = far_ref.shape
    box, me = place_ref[0], place_ref[1]
    mine = pl.ds(pl.multiple_of(box * parents, parents), parents)
    copies = [
        pltpu.make_async_copy(
            table_hbm, table_ref.at[pl.ds(0, table_hbm.shape[0])], sems.at[0]
        ),
        pltpu.make_async_copy(far_hbm.at[:, mine], far_ref, sems.at[1]),
        pltpu.make_async_copy(kind_hbm.at[:, mine], kind_ref, sems.at[2]),
        pltpu.make_async_copy(near_list_hbm, near_list_ref, sems.at[3]),
        pltpu.make_async_copy(angle_hbm, angle_ref, sems.at[4]),
    ]
    for copy in copies:
        copy.start()
    used = table_hbm.shape[0]
    table_ref[used:, :] = jnp.zeros((table_ref.shape[0] - used, table_ref.shape[1]), F32)
    for copy in copies:
        copy.wait()
    cosine_ref[...] = jnp.cos(angle_ref[...])
    sine_ref[...] = jnp.sin(angle_ref[...])
    kinds = table_ref.shape[0] // 2
    table[0:kinds, 0:128] = table_ref[pl.ds(0, kinds, stride=2), :].astype(BF16)
    table[0:kinds, 128:256] = table_ref[pl.ds(1, kinds, stride=2), :].astype(BF16)
    table[kinds:, :] = jnp.zeros((table.shape[0] - kinds, table.shape[1]), BF16)

    leaves = near_list_ref.shape[1]
    rel = near_list_ref[...] - me * leaves
    odd = me & 1
    below = jnp.where(odd == 0, 3 * leaves, leaves * 2)
    above = jnp.where(odd == 0, 0, leaves)
    column = jnp.where(rel < 0, rel + below, jnp.where(rel < leaves, rel, rel + above))
    column_ref[...] = jnp.pad(column, ((0, 32 - column.shape[0]), (0, 0))).T

    q = far_ref[...] - box * parents
    half = parents // 2
    g = jnp.where(q < 0, q + half, q - parents)
    own = ((q >> 3) << 4) + (q & 7)
    row = ((((g >> 3) & 3) ^ 2) << 4) + 8 + (g & 7)
    low, high = row + ((2 + (g >> 5)) << 6), row + ((g >> 5) << 6)
    index = jnp.where(q < 0, low, jnp.where(q < parents, own, high))
    index_ref[...] = jnp.pad(index, ((0, 32 - slots), (0, 0))).T
    kind = jnp.pad(kind_ref[...], ((0, 32 - slots), (0, 0))).T
    lane = lax.broadcasted_iota(I32, (parents, table.shape[0]), 1)
    for j in range(slots):
        hot = jnp.where(lane == kind[:, j : j + 1], 1.0, 0.0).astype(BF16)
        operators[j] = dot(hot, table[...]).astype(BF16)


def up_kernel(
    own_ref, far_ref, agg_ref, cos_ref, sin_ref, interp, out_ref, relay_ref, kept, sem
):
    copy = pltpu.make_async_copy(interp.at[:, pl.ds(0, KEPT * 256)], kept, sem)
    copy.start()
    relay_ref[...] = own_ref[...]
    width = 512
    directions = cos_ref.shape[1]
    leaves = own_ref.shape[0]
    rows = 2 * leaves
    parents = rows // 8
    r = lax.broadcasted_iota(I32, (rows, leaves), 0)
    c = lax.broadcasted_iota(I32, (rows, leaves), 1)
    leaf = 8 * (r % parents) + r // parents
    from_own = jnp.where(c == leaf, 1.0, 0.0).astype(BF16)
    from_far = jnp.where(c + leaves == leaf, 1.0, 0.0).astype(BF16)
    cur = (dot(from_own, own_ref[...]) + dot(from_far, far_ref[...])).astype(BF16)
    pattern = dot(cur, agg_ref[...]).astype(BF16)
    for j in range(directions // width):
        re = dot(pattern, interp[:, j * width : (j + 1) * width])
        im = dot(pattern, interp[:, directions + j * width : directions + (j + 1) * width])
        for h in range(width // 128):
            lanes = slice(h * 128, (h + 1) * 128)
            acc_re = jnp.zeros((parents, 128), F32)
            acc_im = jnp.zeros((parents, 128), F32)
            for k in range(8):
                cosine = cos_ref[pl.ds(k, 1), pl.ds(j * width + h * 128, 128)]
                sine = sin_ref[pl.ds(k, 1), pl.ds(j * width + h * 128, 128)]
                a = re[k * parents : (k + 1) * parents, lanes]
                b = im[k * parents : (k + 1) * parents, lanes]
                acc_re += a * cosine - b * sine
                acc_im += a * sine + b * cosine
            block = j * (width // 128) + h
            out_ref[block, 0:parents, :] = acc_re.astype(BF16)
            out_ref[block, parents : 2 * parents, :] = acc_im.astype(BF16)
    copy.wait()


def translate_kernel(upper_ref, index_ref, operator_ref, out, part_ref, sems):
    sources = upper_ref.shape[0] * 16
    slots, parents = operator_ref.shape[:2]
    field = jnp.concatenate(
        [
            upper_ref[:, 0:16, :].reshape(sources, 128),
            upper_ref[:, 16:32, :].reshape(sources, 128),
        ],
        axis=1,
    )
    rows = parents // 2
    blocks = rows // 8
    lane = lax.broadcasted_iota(I32, (rows, sources), 1).astype(BF16)
    one, zero = jnp.ones((), BF16), jnp.zeros((), BF16)
    copies = []
    for part in range(2):
        low = part * rows
        index = index_ref[low : low + rows].astype(BF16)
        acc_re = jnp.zeros((rows, 128), F32)
        acc_im = jnp.zeros((rows, 128), F32)
        for first in range(0, slots, 4):
            hot = [
                jnp.where(lane == index[:, j : j + 1], one, zero) for j in range(first, first + 4)
            ]
            picked = dot(jnp.concatenate(hot, axis=0), field)
            for k in range(4):
                x = picked[k * rows : (k + 1) * rows]
                op = operator_ref[first + k, low : low + rows].astype(F32)
                xr, xi = x[:, :128], x[:, 128:]
                tr, ti = op[:, :128], op[:, 128:]
                acc_re += tr * xr - ti * xi
                acc_im += tr * xi + ti * xr
        part_ref[part, :, 0:8, :] = acc_re.reshape(blocks, 8, 128).astype(BF16)
        part_ref[part, :, 8:16, :] = acc_im.reshape(blocks, 8, 128).astype(BF16)
        target = out.at[pl.ds(part * blocks, blocks)]
        copies.append(pltpu.make_async_copy(part_ref.at[part], target, sems.at[part]))
        copies[part].start()
    for copy in copies:
        copy.wait()


def down_kernel(inc_ref, cos_ref, sin_ref, near_ref, receive_ref, kept, more, interp, out_ref, buf, received, sems):
    width = 256
    chunks = buf.shape[1] // width
    copies = []
    for j in range(chunks):
        source = interp.at[:, pl.ds((KEPT + MORE + j) * width, width)]
        target = buf.at[:, pl.ds(j * width, width)]
        copies.append(pltpu.make_async_copy(source, target, sems.at[j]))
    for copy in copies:
        copy.start()
    leaves = received.shape[0]
    half = received.shape[1] // 2
    for s in range(inc_ref.shape[0]):
        lanes = slice(s * 128, (s + 1) * 128)
        block = inc_ref[s].astype(F32)
        re, im = block[0:8][:, None, :], block[8:16][:, None, :]
        cosine, sine = cos_ref[:, lanes][None], sin_ref[:, lanes][None]
        received[:, s * 128 : (s + 1) * 128] = (
            (re * cosine + im * sine).reshape(leaves, 128).astype(BF16)
        )
        received[:, half + s * 128 : half + (s + 1) * 128] = (
            (im * cosine - re * sine).reshape(leaves, 128).astype(BF16)
        )
    back = dot(received[:, : KEPT * width], kept[...], 1, 1)
    back += dot(received[:, KEPT * width : (KEPT + MORE) * width], more[...], 1, 1)
    for j in range(chunks):
        at = (KEPT + MORE + j) * width
        copies[j].wait()
        back += dot(received[:, at : at + width], buf[:, j * width : (j + 1) * width], 1, 1)
    out_ref[...] = near_ref[...] + dot(back.astype(BF16), receive_ref[...])


def near_kernel(
    own_ref, sibling_ref, cross_ref, col_ref, near_hbm, interp, _, out_ref, more, buf, hot, sems
):
    slots = near_hbm.shape[0]
    copies = []
    for n in range(slots):
        copies.append(pltpu.make_async_copy(near_hbm.at[n], buf.at[n], sems.at[n]))
        copies[n].start()
    extra = pltpu.make_async_copy(
        interp.at[:, pl.ds(KEPT * 256, more.shape[1])], more, sems.at[slots]
    )
    extra.start()
    rows = out_ref.shape[0]
    lane = lax.broadcasted_iota(I32, (rows, 4 * rows), 1)
    for n in range(slots):
        hot[n * rows : (n + 1) * rows] = jnp.where(
            lane == col_ref[:, n : n + 1], 1.0, 0.0
        ).astype(BF16)
    blocks = (own_ref, sibling_ref, cross_ref, own_ref)
    sources = jnp.concatenate([block[...] for block in blocks], axis=0)
    picked = dot(hot[...], sources).astype(BF16)
    total = jnp.zeros(out_ref.shape, F32)
    for n in range(slots):
        copies[n].wait()
        total += dot(picked[n * rows : (n + 1) * rows], buf[n])
    out_ref[...] = total
    extra.wait()


def halo_target(i, boxes, dirs):
    b, d = divmod(i, dirs)
    z, r = divmod(d, dirs // 4)
    other = b + 1 if z >= 2 else b - 1
    if other < 0 or other >= boxes:
        return b * dirs + (3 - z) * (dirs // 4) + r
    return other * dirs + z * (dirs // 4) + (r ^ 2)


def on_device(
    boxes,
    dirs,
    currents,
    near_list,
    far_list,
    far_kind,
    aggregate,
    interp,
    receive,
    shift_angle,
    translation,
    near_matrix,
):
    leaves, width = currents.shape
    n = boxes * dirs
    me = lax.axis_index(BOTH)
    box = lax.axis_index("box")
    parents = leaves // 8 * dirs
    slots, near_slots = far_list.shape[1], near_list.shape[1]

    far_half = lax.ppermute(currents, BOTH, [(i, halo_target(i, boxes, dirs)) for i in range(n)])
    from_sibling = lax.ppermute(currents, BOTH, [(i, i ^ 1) for i in range(n)])

    place = jnp.stack([box, me]).astype(I32)
    operators, index, column, cosine, sine = call(
        prepare_kernel,
        (
            pltpu.VMEM((slots, parents, 256), BF16),
            pltpu.VMEM((parents, 32), I32),
            pltpu.VMEM((leaves, 32), I32),
            pltpu.VMEM(shift_angle.shape, F32),
            pltpu.VMEM(shift_angle.shape, F32),
        ),
        (
            place,
            *in_hbm(
                far_list.T,
                far_kind.T,
                shift_angle,
                translation.reshape(-1, translation.shape[2]),
                near_list.T,
            ),
        ),
        [whole(pltpu.SMEM)] + [whole(pltpu.HBM)] * 5,
        [
            pltpu.VMEM((slots, parents), I32),
            pltpu.VMEM((slots, parents), I32),
            pltpu.VMEM(shift_angle.shape, F32),
            pltpu.VMEM((640, translation.shape[2]), F32),
            pltpu.VMEM((near_slots, leaves), I32),
            pltpu.VMEM((384, 256), BF16),
            pltpu.SemaphoreType.DMA((5,)),
        ],
        8,
        AHEAD,
        11 << 20,
    )

    up, relay, kept = call(
        up_kernel,
        (
            jax.ShapeDtypeStruct((dirs, 4 * leaves // 8, 128), BF16),
            jax.ShapeDtypeStruct(currents.shape, BF16),
            pltpu.VMEM((interp.shape[0], KEPT * 256), BF16),
        ),
        (currents, far_half, in_vmem(aggregate), cosine, sine, in_vmem(interp)),
        [whole()] * 6,
        [pltpu.SemaphoreType.DMA],
        8,
        2 * 128 * 1024 * 4608,
        10 << 20,
    )
    upper = lax.all_to_all(up, "dir", split_axis=0, concat_axis=0, tiled=True)

    cross = [(i, min(max(i + (1 if i % 2 else -1), 0), n - 1)) for i in range(n)]
    from_cross = lax.ppermute(relay, BOTH, cross)
    local = call(
        translate_kernel,
        pltpu.HBM((dirs, 2 * leaves // 8, 128), BF16),
        (upper, index, operators),
        [whole()] * 3,
        [
            pltpu.VMEM((2, dirs // 2, 2 * leaves // 8, 128), BF16),
            pltpu.SemaphoreType.DMA((2,)),
        ],
        8,
        2 * slots * parents * 256 * 256,
        2 << 20,
        pltpu.HBM,
    )
    incoming = lax.all_to_all(local, "dir", split_axis=0, concat_axis=0, tiled=True)

    near, more = call(
        near_kernel,
        (
            jax.ShapeDtypeStruct((leaves, width), F32),
            pltpu.VMEM((interp.shape[0], MORE * 256), BF16),
        ),
        (currents, from_sibling, from_cross, column, *in_hbm(near_matrix, interp), local),
        [whole()] * 4 + [whole(pltpu.HBM)] * 2 + [whole(pl.ANY)],
        [
            pltpu.VMEM(near_matrix.shape, BF16),
            pltpu.VMEM((near_slots * leaves, 4 * leaves), BF16),
            pltpu.SemaphoreType.DMA((near_slots + 1,)),
        ],
        24,
        2 * leaves * 27 * 512 * 640,
        15 << 20,
    )

    return call(
        down_kernel,
        jax.ShapeDtypeStruct((leaves, width), F32),
        (incoming, cosine, sine, near, in_vmem(receive), in_vmem(kept), in_vmem(more), *in_hbm(interp)),
        [whole()] * 7 + [whole(pltpu.HBM)],
        [
            pltpu.VMEM((interp.shape[0], interp.shape[1] - (KEPT + MORE) * 256), BF16),
            pltpu.VMEM((leaves, interp.shape[1]), BF16),
            pltpu.SemaphoreType.DMA((interp.shape[1] // 256,)),
        ],
        16,
        2 * 64 * 4096 * 1536,
        10 << 20,
    )


def solution(mesh):
    placed = (
        P(BOTH, None),
        P(BOTH, None),
        P(),
        P(),
        P(),
        P(),
        P(),
        P(),
        P(None, None, "dir"),
        P(),
    )
    body = functools.partial(on_device, mesh.shape["box"], mesh.shape["dir"])
    return jax.shard_map(
        body, mesh=mesh, in_specs=placed, out_specs=P(BOTH, None), check_vma=False
    )
```
